32 devices in a mesh: groups: 2 (over x), elec: 16 (over z, y, core).
Axes of the slice: x: 2, y: 2, z: 4, core: 2. Of those that a mesh axis runs over, the one named last changes fastest.
Arguments:
- features: bfloat16 [131072, 256], P(('groups', 'elec')), parts along dimension 0, may hold values from -6 to 6
- assignment: int32 [131072], P(('groups', 'elec')), parts along dimension 0, may hold values from 0 to 65535, as said below
- pairs: int32 [2048, 3], P(('groups', 'elec')), parts along dimension 0, may hold values from 0 to 1023, as said below
- w_query: bfloat16 [256, 256], replicated
- w_key: bfloat16 [256, 256], replicated
- w_value: bfloat16 [256, 256], replicated, may hold values from -0.375 to 0.375
- w_out: bfloat16 [256, 256], replicated, may hold values from -0.375 to 0.375
- w_mix: bfloat16 [256, 256], replicated, may hold values from -0.375 to 0.375
Outputs:
- mixed: bfloat16 [131072, 256], P(('groups', 'elec')), parts along dimension 0
The draws below stay inside these ranges and needn't reach their ends.
There are 2 independent parts, one for each index of `groups`. The reference program is written for one: setup_inputs(seed, part) draws one part's arguments, and reference() takes and returns one part's arrays. A program takes and returns all parts, laid end to end along the dimension named above; an argument that names none is the same for every part. Nothing has to cross between parts.
Inputs may be any that keep to these rules, and one draw needn't show every extreme that they name: assignment is a permutation of the rows; each group of 512 rows of one walker on one device is filled from electrons of that same group. pairs[b, :] name blocks of block b's own walker (its blocks lie on the 8 devices whose index has the same remainder modulo 1024 // 512 as block b's device, 8 on each). Over the 64 reader blocks of one device, at most 25 of the listed key blocks lie on any one device (blocks d * 64 to (d + 1) * 64 - 1 lie on device d), and exactly 25 on some device.
All inputs are finite; a program needn't handle non-finite values.
Results may differ from the reference program's by a relative error of at most 0.0078.
Values may be sent and summed in bfloat16 or wider, within the bound.
A program may use at most 128 MiB of HBM per device.

```python
import jax
import jax.numpy as jnp
from jax import lax

D = 256
HEADS = 16
HEAD_DIM = 16
CLUSTER = 64
PAIRS = 3
SPAN = 8
SUB = 8
BLK_DEV = 64
BLOCKS = 1024
ROWS = 65536
CAP = 25


def draw_assignment(key, part):
    group_count = ROWS // (SUB * CLUSTER)
    rows_each = SUB * CLUSTER
    orders = jax.vmap(lambda k: jax.random.permutation(k, rows_each))(jax.random.split(key, group_count))
    offsets = jnp.arange(group_count, dtype=jnp.int32)[:, None] * rows_each
    return (orders.astype(jnp.int32) + offsets).reshape(-1).astype(jnp.int32)


def draw_pairs(key, part):
    shard_count = BLOCKS // BLK_DEV
    stride = shard_count // SPAN
    wanted = BLK_DEV * PAIRS
    rest_count = wanted - SPAN
    rest_cap = CAP - 1
    rest_slots = SPAN * rest_cap

    def one_device(k, device):
        k_perm, k_full, k_shuffle, k_local, k_owner = jax.random.split(k, 5)
        position = device // stride
        group_first = device % stride
        first_owner = jax.random.permutation(k_owner, SPAN).astype(jnp.int32)
        offset = (position - first_owner) % SPAN
        lowbit = jnp.where(offset == 0, SPAN, offset & -offset)
        first_within = (position // lowbit % 2).astype(jnp.int32)
        order_scores = jax.random.permutation(k_perm, rest_slots).astype(jnp.int32)
        full_owner = jax.random.randint(k_full, (), 0, SPAN)
        slot_ids = jnp.arange(rest_slots, dtype=jnp.int32)
        ranked = order_scores - jnp.where(slot_ids // rest_cap == full_owner, rest_slots, 0)
        order = jnp.argsort(ranked, stable=True)
        chosen = order[:rest_count]
        shuffle = jax.random.permutation(k_shuffle, rest_count)
        rest_owner = (chosen[shuffle] // rest_cap).astype(jnp.int32)
        rest_within = jax.random.randint(k_local, (rest_count,), 0, SUB).astype(jnp.int32)
        owner_pos = jnp.concatenate([first_owner, rest_owner])
        within = jnp.concatenate([first_within, rest_within])
        entry = jnp.arange(wanted, dtype=jnp.int32)
        walker_slot = entry // PAIRS // SUB
        listed = (group_first + owner_pos * stride) * BLK_DEV + walker_slot * SUB + within
        return listed.reshape(BLK_DEV, PAIRS)
    devices = jnp.arange(shard_count, dtype=jnp.int32)
    result = jax.vmap(one_device)(jax.random.split(key, shard_count), devices)
    return result.reshape(BLOCKS, PAIRS).astype(jnp.int32)


def projection_pair(key):
    k_one, k_two = jax.random.split(jax.random.fold_in(key, 7), 2)
    first = jax.random.normal(k_one, (D, D), jnp.float32) / D ** 0.5
    second = jax.random.normal(k_two, (D, D), jnp.float32) / D ** 0.5
    return (first, second)


def draw_w_query(key, part):
    return projection_pair(key)[0].astype(jnp.bfloat16)


def draw_w_key(key, part):
    return projection_pair(key)[1].astype(jnp.bfloat16)


def levels(own_key, dims, shards, least, top_value):
    level = 1.0
    for dim, parts in shards:
        draws = jax.random.uniform(jax.random.fold_in(jax.random.fold_in(own_key, 6), dim), (parts,), jnp.float32, least / len(shards), top_value / len(shards))
        level = level * jnp.repeat(jnp.exp(draws), dims[dim] // parts).reshape((-1,) + (1,) * (len(dims) - 1 - dim))
    return level


def noise(stream_key, shape, spread, bound, pieces=(), held_as=jnp.bfloat16):
    values = spread * jax.random.normal(stream_key, shape, jnp.float32)
    if pieces:
        values = values * levels(stream_key, shape, pieces, -0.22, 0.18)
    return jnp.clip(values, -bound, bound).astype(held_as)


def setup_inputs(seed: int = 0, part: int = 0) -> dict:
    streams_of = jax.random.split(jax.random.key(seed), 9)
    part_splits = jax.random.split(jax.random.fold_in(streams_of[8], part), 9)
    return {
        "features": noise(part_splits[0], (ROWS, D), 1.0, 6.0, ((0, 16),)),
        "assignment": draw_assignment(jax.random.fold_in(jax.random.fold_in(streams_of[8], part), 71), part),
        "pairs": draw_pairs(jax.random.fold_in(jax.random.fold_in(streams_of[8], part), 71), part),
        "w_query": draw_w_query(jax.random.fold_in(streams_of[8], 71), part),
        "w_key": draw_w_key(jax.random.fold_in(streams_of[8], 71), part),
        "w_value": noise(streams_of[5], (D, D), D ** -0.5, 0.375),
        "w_out": noise(streams_of[6], (D, D), D ** -0.5, 0.375),
        "w_mix": noise(streams_of[7], (D, D), D ** -0.5, 0.375),
    }


def layer_norm(rows):
    mean = lax.optimization_barrier(jnp.mean(rows, axis=-1, keepdims=True))
    centred = rows - mean
    variance = lax.optimization_barrier(jnp.mean(centred * centred, axis=-1, keepdims=True))
    return centred * lax.rsqrt(variance + 1e-05)

def reference(features, assignment, pairs, w_query, w_key, w_value, w_out, w_mix):
    placed = jnp.take(features, assignment, axis=0)
    normed = layer_norm(placed.astype(jnp.float32)).astype(jnp.bfloat16)
    query = jnp.dot(normed, w_query, preferred_element_type=jnp.float32).astype(jnp.bfloat16)
    keys = jnp.dot(normed, w_key, preferred_element_type=jnp.float32).astype(jnp.bfloat16)
    values = jnp.dot(normed, w_value, preferred_element_type=jnp.float32).astype(jnp.bfloat16)
    query_blocks = query.reshape(BLOCKS, CLUSTER, D)
    key_blocks = keys.reshape(BLOCKS, CLUSTER, D)
    value_blocks = values.reshape(BLOCKS, CLUSTER, D)
    scale = 1.0 / HEAD_DIM ** 0.5

    def attend(args):
        block_query, block_index, listed = args
        chosen = jnp.concatenate([block_index[None], listed]).astype(jnp.int32)
        set_keys = jnp.take(key_blocks, chosen, axis=0).reshape(-1, HEADS, HEAD_DIM).astype(jnp.float32)
        set_values = jnp.take(value_blocks, chosen, axis=0).reshape(-1, HEADS, HEAD_DIM).astype(jnp.float32)
        heads_query = block_query.reshape(CLUSTER, HEADS, HEAD_DIM).astype(jnp.float32)
        scores = jnp.einsum('qhd,khd->hqk', heads_query, set_keys) * scale
        weights = jax.nn.softmax(scores, axis=-1).astype(jnp.bfloat16)
        result = jnp.einsum('hqk,khd->qhd', weights.astype(jnp.float32), set_values)
        return result.astype(jnp.bfloat16).reshape(CLUSTER, D)
    attended = lax.map(attend, (query_blocks, jnp.arange(BLOCKS, dtype=jnp.int32), pairs), batch_size=64)
    attended = attended.reshape(ROWS, D)
    middle = (placed.astype(jnp.float32) + jnp.dot(attended, w_out, preferred_element_type=jnp.float32)).astype(jnp.bfloat16)
    second = layer_norm(middle.astype(jnp.float32)).astype(jnp.bfloat16)
    mixed = middle.astype(jnp.float32) + jnp.tanh(jnp.dot(second, w_mix, preferred_element_type=jnp.float32))
    return mixed.astype(jnp.bfloat16)
```

```python
import functools
import math

import jax
import jax.numpy as jnp
from jax import lax
from jax.experimental import pallas as pl
from jax.experimental.pallas import tpu as pltpu
from jax.sharding import PartitionSpec as P

HEADS = 16
SPAN = 8
LANES = 128
MESH = pl.DeviceIdType.MESH


def layer_norm(rows):
    mean = jnp.mean(rows, axis=-1, keepdims=True)
    centred = rows - mean
    variance = jnp.mean(centred * centred, axis=-1, keepdims=True)
    return centred * lax.rsqrt(variance + 1e-05)


def own_needs(listed, block_count, stride):
    flat = listed.reshape(-1)
    column = (flat // block_count // stride) * block_count + flat % block_count
    columns = jnp.arange(SPAN * block_count, dtype=jnp.int32)
    hit = column[None, :] == columns[:, None]
    return column, jnp.max(jnp.where(hit, 1, 0), axis=1).astype(jnp.int32)


def before(flags):
    size = flags.shape[-1]
    lower = (jnp.arange(size)[:, None] < jnp.arange(size)[None, :]).astype(jnp.bfloat16)
    counts = jnp.dot(
        flags.reshape(-1, size).astype(jnp.bfloat16), lower, preferred_element_type=jnp.float32
    )
    return counts.reshape(flags.shape).astype(jnp.int32)


def invert(place, flags, values, size):
    hit = (place[..., None, :] == jnp.arange(size, dtype=jnp.int32)[:, None]) & (
        flags[..., None, :] > 0
    )
    return jnp.sum(jnp.where(hit, values[..., None, :], 0), axis=-1).astype(jnp.int32)


def make_plan(needs, column, position, capacity):
    blocks = needs.shape[-1]
    owners = jnp.arange(SPAN, dtype=jnp.int32)
    static = list(range(SPAN))
    ends = [2 * (3 * (1 - o // 4)) + o % 2 for o in static]
    first = jnp.stack([needs[ends[o] ^ 1, o] for o in static])
    second = jnp.stack([needs[ends[o], o] for o in static]) * (1 - first)
    third = 1 - first - second
    c0, c1, c2 = before(first), before(second), before(third)
    n0 = jnp.sum(first, axis=1, keepdims=True)
    n1 = jnp.sum(second, axis=1, keepdims=True)
    order = jnp.where(first > 0, c0, jnp.where(second > 0, n0 + c1, n0 + n1 + c2))
    rank = before(needs)
    within = jnp.arange(blocks, dtype=jnp.int32)

    def at(array, index):
        return lax.dynamic_index_in_dim(array, index, 0, keepdims=False)

    near_readers = [position ^ t for t in range(4)]
    mine = lax.dynamic_index_in_dim(needs, position, 1, keepdims=False)
    mine_rank = lax.dynamic_index_in_dim(rank, position, 1, keepdims=False)
    near = jnp.stack(
        [
            invert(at(mine_rank, q), at(mine, q), within, LANES)
            for q in near_readers
        ]
    )
    all_flags = jnp.ones((blocks,), jnp.int32)
    far_list = invert(at(order, position), all_flags, within, LANES)

    z, y = position // 2, position % 2
    half = z // 2
    inner = (z + half) % 2
    partner_needs = at(needs, position ^ 1)
    partner_rank = at(rank, position ^ 1)
    sources = [2 * (2 - half) + y, 2 * (3 * (1 - half)) + y]
    filters = jnp.stack(
        [
            invert(at(partner_rank, s), at(partner_needs, s), at(order, s), LANES)
            for s in sources
        ]
    )
    tables = jnp.concatenate([near, far_list[None], filters], axis=0)

    my_rank = at(rank, position)
    other = owners ^ position
    oz = owners // 2
    owner_inner = (oz + oz // 2) % 2
    slot_index = 1 - owner_inner
    far_base = (4 * capacity) + slot_index * blocks
    side_base = (4 * capacity) + 2 * blocks + slot_index * capacity
    near_loc = (other * capacity)[:, None] + my_rank
    far_loc = far_base[:, None] + order
    side_loc = side_base[:, None] + jnp.where(inner > 0, my_rank, order)
    same_half = (owners // 4 == position // 4)[:, None]
    same_line = (owners % 2 == y)[:, None]
    location = jnp.where(same_half, near_loc, jnp.where(same_line, far_loc, side_loc)).reshape(-1)
    hit = column[:, None] == jnp.arange(SPAN * blocks, dtype=jnp.int32)[None, :]
    slots = jnp.sum(jnp.where(hit, location[None, :], 0), axis=1).astype(jnp.int32)
    return slots, tables


def place_kernel(
    stride, assignment_ref, need_ref, features_ref, placed_ref, normed_ref, needs_ref,
    landing, s_send, s_recv,
):
    groups, _, size = assignment_ref.shape
    me = lax.axis_index("elec")
    group = lax.axis_index("groups")
    peers = lax.axis_size("elec")
    position = me // stride
    step_index = pl.program_id(0)

    def toward(step):
        return (group, lax.rem(me + step * stride, peers))

    def ask(step):
        return pltpu.make_async_remote_copy(
            src_ref=need_ref, dst_ref=landing.at[step],
            send_sem=s_send.at[step], recv_sem=s_recv.at[step],
            device_id=toward(step), device_id_type=MESH,
        )

    @pl.when(step_index == 0)
    def _():
        barrier = pltpu.get_barrier_semaphore()
        for step in range(1, SPAN):
            pl.semaphore_signal(barrier, inc=1, device_id=toward(step), device_id_type=MESH)
        pl.semaphore_wait(barrier, SPAN - 1)
        for step in range(1, SPAN):
            ask(step).start()
        landing[0] = need_ref[...]

    lane = lax.broadcasted_iota(jnp.int32, (size, LANES), 1).astype(jnp.float32)
    for i in range(groups):
        rows = pl.ds(i * size, size)
        base = me * (features_ref.shape[0] * pl.num_programs(0)) + (
            (step_index * groups + i) * size
        )
        local = (assignment_ref[i] - base).astype(jnp.float32)
        takes = jnp.broadcast_to(local, (LANES, size)).T
        one_hot = jnp.concatenate(
            [jnp.where(takes == lane + k, 1.0, 0.0) for k in range(0, size, LANES)], axis=1
        ).astype(jnp.bfloat16)
        placed = jnp.dot(one_hot, features_ref[rows, :], preferred_element_type=jnp.float32)
        placed_ref[rows, :] = placed.astype(jnp.bfloat16)
        normed_ref[rows, :] = layer_norm(placed).astype(jnp.bfloat16)

    @pl.when(step_index == pl.num_programs(0) - 1)
    def _():
        for step in range(1, SPAN):
            ask(step).wait()
        for q in range(SPAN):
            needs_ref[q] = landing[lax.rem(position - q + SPAN, SPAN)]


def exchange_kernel(
    capacity, stride, tables_ref, blocks_ref, arrived_ref,
    out_near, out_far, out_side, far0, far1,
    n_send, n_recv, l_send, f_send, f_recv, w_send, p_send, p_recv, local_sem,
):
    me = lax.axis_index("elec")
    group = lax.axis_index("groups")
    position = me // stride
    rest = lax.rem(me, stride)
    block_count = blocks_ref.shape[0]
    cap = capacity
    z, y = position // 2, lax.rem(position, 2)
    half = z // 2
    inner = lax.rem(z + half, 2)
    pair_z = z + 1 - 2 * lax.rem(z, 2)
    pair_y = 1 - y

    def device(zz, yy):
        return (group, (2 * zz + yy) * stride + rest)

    near_devices = [device(z, pair_y), device(pair_z, y), device(pair_z, pair_y)]
    far_inner = device(2 - half, y)

    barrier = pltpu.get_barrier_semaphore()
    peers = lax.axis_size("elec")
    for step in range(1, SPAN):
        pl.semaphore_signal(
            barrier, inc=1, device_id=(group, lax.rem(me + step * stride, peers)),
            device_id_type=MESH,
        )
    pl.semaphore_wait(barrier, SPAN - 1)

    far = [far0, far1]
    chunks = [(0, cap), (cap, cap), (2 * cap, block_count - 2 * cap)]

    def gather(row, first, count, source, target, base):
        def one(k, carry):
            target[base + first + k] = source[tables_ref[row, first + k]]
            return carry

        lax.fori_loop(0, count, one, 0)

    def far_copy(s, c):
        start, count = chunks[c]
        return pltpu.make_async_remote_copy(
            src_ref=out_far.at[pl.ds(start, count)], dst_ref=far[s].at[pl.ds(start, count)],
            send_sem=l_send.at[c], recv_sem=f_recv.at[s, c],
            device_id=far_inner, device_id_type=MESH,
        )

    def forward_copy(s, c):
        start, count = chunks[c]
        return pltpu.make_async_remote_copy(
            src_ref=far[s].at[pl.ds(start, count)], dst_ref=far[s].at[pl.ds(start, count)],
            send_sem=f_send.at[s, c], recv_sem=f_recv.at[s, c],
            device_id=near_devices[1], device_id_type=MESH,
        )

    side_base = 4 * cap + 2 * block_count

    def side_copy(s, source):
        return pltpu.make_async_remote_copy(
            src_ref=source, dst_ref=arrived_ref.at[pl.ds(side_base + s * cap, cap)],
            send_sem=p_send.at[s], recv_sem=p_recv.at[s],
            device_id=near_devices[0], device_id_type=MESH,
        )

    def near_copy(t):
        return pltpu.make_async_remote_copy(
            src_ref=out_near.at[pl.ds(t * cap, cap)], dst_ref=arrived_ref.at[pl.ds(t * cap, cap)],
            send_sem=n_send.at[t], recv_sem=n_recv.at[t],
            device_id=near_devices[t - 1], device_id_type=MESH,
        )

    def send_far(c):
        gather(4, chunks[c][0], chunks[c][1], blocks_ref, out_far, 0)

        @pl.when(inner == 1)
        def _():
            far_copy(0, c).start()

        @pl.when(inner == 0)
        def _():
            far_copy(1, c).start()

    def send_near(t):
        gather(t, 0, cap, blocks_ref, out_near, t * cap)
        near_copy(t).start()

    send_far(0)
    send_near(2)
    send_near(3)
    send_far(1)
    send_far(2)
    send_near(1)
    gather(0, 0, cap, blocks_ref, out_near, 0)
    own = pltpu.make_async_copy(
        out_near.at[pl.ds(0, cap)], arrived_ref.at[pl.ds(0, cap)], local_sem.at[0]
    )
    own.start()

    def keep(s, count):
        return pltpu.make_async_copy(
            far[s].at[pl.ds(0, count)],
            arrived_ref.at[pl.ds(4 * cap + s * block_count, count)], local_sem.at[1 + s],
        )

    @pl.when(inner == 1)
    def _():
        for c in range(2):
            for s in range(2):
                far_copy(s, c).wait_recv()
                forward_copy(s, c).start()
        for s in range(2):
            far_copy(s, 2).wait_recv()
            gather(5 + s, 0, cap, far[s], out_side, s * cap)
            side_copy(s, out_side.at[pl.ds(s * cap, cap)]).start()
            keep(s, block_count).start()
        for s in range(2):
            for c in range(2):
                forward_copy(s, c).wait_send()
            keep(s, block_count).wait()
            side_copy(s, out_side.at[pl.ds(s * cap, cap)]).wait_send()

    @pl.when(inner == 0)
    def _():
        for s in range(2):
            far_copy(s, 0).wait_recv()
            side_copy(s, far[s].at[pl.ds(0, cap)]).start()
        for s in range(2):
            far_copy(s, 1).wait_recv()
            keep(s, 2 * cap).start()
        for s in range(2):
            keep(s, 2 * cap).wait()
            side_copy(s, far[s].at[pl.ds(0, cap)]).wait_send()

    own.wait()
    for c in range(3):
        far_copy(0, c).wait_send()
    for t in range(1, 4):
        near_copy(t).wait()
    for s in range(2):
        side_copy(s, out_side.at[pl.ds(s * cap, cap)]).wait_recv()


def attend_kernel(
    slots_ref, placed_ref, normed_ref, arrived_ref, wq_ref, wk_ref, wv_ref, wo_ref, wm_ref,
    out_ref, queries, attended,
):
    cluster, width = arrived_ref.shape[1:]
    rows = placed_ref.shape[0]
    blocks = rows // cluster
    pair_count = slots_ref.shape[0] // (blocks * pl.num_programs(0))
    head_width = width // HEADS
    half = LANES // 2
    per = half // head_width
    first = pl.program_id(0) * blocks
    f32, bf16 = jnp.float32, jnp.bfloat16
    lane = lax.broadcasted_iota(jnp.int32, (cluster, LANES), 1)
    low = lane < half
    low_keys = lax.broadcasted_iota(jnp.int32, ((pair_count + 1) * cluster, LANES), 1) < half
    chosen = [jnp.where(lane // head_width == c, 1.0, 0.0).astype(bf16) for c in range(2 * per)]
    own_head = lane % half // head_width
    scale = math.log2(math.e) / head_width**0.5
    queries[...] = (
        jnp.dot(normed_ref[...], wq_ref[...], preferred_element_type=f32) * scale
    ).astype(bf16)

    def one(j, carry):
        start = pl.multiple_of(j * cluster, cluster)
        base = (first + j) * pair_count
        listed = [arrived_ref[slots_ref[base + p]] for p in range(pair_count)]
        key_rows = jnp.concatenate([normed_ref[pl.ds(start, cluster), :]] + listed, axis=0)
        keys = jnp.dot(key_rows, wk_ref[...], preferred_element_type=f32).astype(bf16)
        values = jnp.dot(key_rows, wv_ref[...], preferred_element_type=f32)
        for band in range(0, width, LANES):
            query = queries[pl.ds(start, cluster), band : band + LANES]
            band_keys = keys[:, band : band + LANES]
            band_values = values[:, band : band + LANES]
            folded = []
            for side in range(2):
                stacked = jnp.concatenate(
                    [query * chosen[side * per + c] for c in range(per)], axis=0
                )
                scores = lax.dot_general(
                    stacked, band_keys, (((1,), (1,)), ((), ())), preferred_element_type=f32
                )
                weights = jnp.exp2(scores - jnp.max(scores, axis=1, keepdims=True)).astype(bf16)
                with_ones = (
                    jnp.where(low_keys, band_values, 1.0)
                    if side == 0
                    else jnp.where(low_keys, 1.0, band_values)
                ).astype(bf16)
                result = jnp.dot(weights, with_ones, preferred_element_type=f32)
                kept = result[(per - 1) * cluster :]
                for c in range(per - 1):
                    kept = jnp.where(own_head == c, result[c * cluster : (c + 1) * cluster], kept)
                folded.append(kept)
            numerator = jnp.where(low, folded[0], folded[1])
            denominator = pltpu.roll(jnp.where(low, folded[1], folded[0]), half, 1)
            attended[pl.ds(start, cluster), band : band + LANES] = (
                numerator / denominator
            ).astype(bf16)
        return carry

    lax.fori_loop(0, blocks, one, 0, unroll=True)
    projected = jnp.dot(attended[...], wo_ref[...], preferred_element_type=f32)
    middle = (placed_ref[...].astype(f32) + projected).astype(bf16).astype(f32)
    second = layer_norm(middle).astype(bf16)
    mixed = middle + jnp.tanh(jnp.dot(second, wm_ref[...], preferred_element_type=f32))
    out_ref[...] = mixed.astype(bf16)


def body(features, assignment, pairs, w_query, w_key, w_value, w_out, w_mix):
    rows_dev, width = features.shape
    block_count, pair_count = pairs.shape
    cluster = rows_dev // block_count
    capacity = (block_count * pair_count + SPAN - 1) // SPAN + 1
    stride = lax.axis_size("elec") // SPAN
    position = lax.axis_index("elec") // stride
    group_rows = SPAN * cluster
    groups = rows_dev // group_rows
    bf16 = jnp.bfloat16

    column, need = own_needs(pairs, block_count, stride)
    need_rows = SPAN * block_count // LANES
    batch = math.gcd(groups, 2)
    tile = pl.BlockSpec((batch * group_rows, width), lambda i: (i, 0))
    placed, normed, needs = pl.pallas_call(
        functools.partial(place_kernel, stride),
        grid=(groups // batch,),
        in_specs=[
            pl.BlockSpec((batch, 1, group_rows), lambda i: (i, 0, 0)),
            pl.BlockSpec((need_rows, LANES), lambda i: (0, 0)),
            tile,
        ],
        out_specs=[tile, tile, pl.BlockSpec((SPAN, need_rows, LANES), lambda i: (0, 0, 0))],
        out_shape=[jax.ShapeDtypeStruct((rows_dev, width), bf16)] * 2
        + [jax.ShapeDtypeStruct((SPAN, need_rows, LANES), jnp.int32)],
        scratch_shapes=[
            pltpu.VMEM((SPAN, need_rows, LANES), jnp.int32),
            pltpu.SemaphoreType.DMA((SPAN,)),
            pltpu.SemaphoreType.DMA((SPAN,)),
        ],
        compiler_params=pltpu.CompilerParams(collective_id=1, has_side_effects=True),
    )(
        assignment.reshape(groups, 1, group_rows), need.reshape(need_rows, LANES), features
    )

    slots, tables = make_plan(
        needs.reshape(SPAN, SPAN, block_count), column, position, capacity
    )
    total = 6 * capacity + 2 * block_count
    block = (cluster, width)
    arrived = pl.pallas_call(
        functools.partial(exchange_kernel, capacity, stride),
        in_specs=[
            pl.BlockSpec(memory_space=pltpu.SMEM),
            pl.BlockSpec(memory_space=pltpu.VMEM),
        ],
        out_specs=pl.BlockSpec(memory_space=pl.ANY),
        out_shape=jax.ShapeDtypeStruct((total,) + block, bf16),
        scratch_shapes=[
            pltpu.VMEM((4 * capacity,) + block, bf16),
            pltpu.VMEM((block_count,) + block, bf16),
            pltpu.VMEM((2 * capacity,) + block, bf16),
            pltpu.VMEM((block_count,) + block, bf16),
            pltpu.VMEM((block_count,) + block, bf16),
            pltpu.SemaphoreType.DMA((4,)),
            pltpu.SemaphoreType.DMA((4,)),
            pltpu.SemaphoreType.DMA((3,)),
            pltpu.SemaphoreType.DMA((2, 3)),
            pltpu.SemaphoreType.DMA((2, 3)),
            pltpu.SemaphoreType.DMA((2,)),
            pltpu.SemaphoreType.DMA((2,)),
            pltpu.SemaphoreType.DMA((2,)),
            pltpu.SemaphoreType.DMA((3,)),
        ],
        compiler_params=pltpu.CompilerParams(
            collective_id=0, has_side_effects=True, vmem_limit_bytes=32 * 2**20
        ),
    )(tables, normed.reshape(block_count, cluster, width))

    tile = pl.BlockSpec((group_rows, width), lambda i, s: (i, 0))
    weight = pl.BlockSpec((width, width), lambda i, s: (0, 0))
    return pl.pallas_call(
        attend_kernel,
        grid_spec=pltpu.PrefetchScalarGridSpec(
            num_scalar_prefetch=1,
            grid=(groups,),
            in_specs=[
                tile,
                tile,
                pl.BlockSpec(arrived.shape, lambda i, s: (0, 0, 0)),
            ]
            + [weight] * 5,
            out_specs=tile,
            scratch_shapes=[pltpu.VMEM((group_rows, width), bf16)] * 2,
        ),
        out_shape=jax.ShapeDtypeStruct((rows_dev, width), bf16),
        compiler_params=pltpu.CompilerParams(vmem_limit_bytes=48 * 2**20),
    )(slots, placed, normed, arrived, w_query, w_key, w_value, w_out, w_mix)


def solution(mesh):
    placed = (
        P(("groups", "elec"), None),
        P(("groups", "elec")),
        P(("groups", "elec"), None),
        P(),
        P(),
        P(),
        P(),
        P(),
    )
    return jax.shard_map(
        body, mesh=mesh, in_specs=placed, out_specs=P(("groups", "elec"), None), check_vma=False
    )
```

```python
import functools
import math

import jax
import jax.numpy as jnp
from jax import lax
from jax.experimental import pallas as pl
from jax.experimental.pallas import tpu as pltpu
from jax.sharding import PartitionSpec as P

HEADS = 16
SPAN = 8
LANES = 128
MESH = pl.DeviceIdType.MESH


def layer_norm(rows):
    mean = jnp.mean(rows, axis=-1, keepdims=True)
    centred = rows - mean
    variance = jnp.mean(centred * centred, axis=-1, keepdims=True)
    return centred * lax.rsqrt(variance + 1e-05)


def own_needs(listed, block_count, stride):
    flat = listed.reshape(-1)
    column = (flat // block_count // stride) * block_count + flat % block_count
    columns = jnp.arange(SPAN * block_count, dtype=jnp.int32)
    hit = column[None, :] == columns[:, None]
    return column, jnp.max(jnp.where(hit, 1, 0), axis=1).astype(jnp.int32)


def before(flags):
    size = flags.shape[-1]
    lower = (jnp.arange(size)[:, None] < jnp.arange(size)[None, :]).astype(jnp.bfloat16)
    counts = jnp.dot(
        flags.reshape(-1, size).astype(jnp.bfloat16), lower, preferred_element_type=jnp.float32
    )
    return counts.reshape(flags.shape).astype(jnp.int32)


def invert(place, flags, values, size):
    hit = (place[..., None, :] == jnp.arange(size, dtype=jnp.int32)[:, None]) & (
        flags[..., None, :] > 0
    )
    return jnp.sum(jnp.where(hit, values[..., None, :], 0), axis=-1).astype(jnp.int32)


def make_plan(needs, column, position, capacity, pair_count):
    blocks = needs.shape[-1]
    owners = jnp.arange(SPAN, dtype=jnp.int32)
    static = list(range(SPAN))
    ends = [2 * (3 * (1 - o // 4)) + o % 2 for o in static]
    first = jnp.stack([needs[ends[o] ^ 1, o] for o in static])
    second = jnp.stack([needs[ends[o], o] for o in static]) * (1 - first)
    third = 1 - first - second
    c0, c1, c2 = before(first), before(second), before(third)
    n0 = jnp.sum(first, axis=1, keepdims=True)
    n1 = jnp.sum(second, axis=1, keepdims=True)
    order = jnp.where(first > 0, c0, jnp.where(second > 0, n0 + c1, n0 + n1 + c2))
    rank = before(needs)
    within = jnp.arange(blocks, dtype=jnp.int32)

    def at(array, index):
        return lax.dynamic_index_in_dim(array, index, 0, keepdims=False)

    mine = lax.dynamic_index_in_dim(needs, position, 1, keepdims=False)
    mine_rank = lax.dynamic_index_in_dim(rank, position, 1, keepdims=False)
    near = jnp.stack(
        [
            invert(at(mine_rank, position ^ t), at(mine, position ^ t), within, LANES)
            for t in range(1, 4)
        ]
    )
    all_flags = jnp.ones((blocks,), jnp.int32)
    far_list = invert(at(order, position), all_flags, within, LANES)

    z, y = position // 2, position % 2
    half = z // 2
    inner = (z + half) % 2
    partner_needs = at(needs, position ^ 1)
    partner_rank = at(rank, position ^ 1)
    sources = [2 * (2 - half) + y, 2 * (3 * (1 - half)) + y]
    filters = jnp.stack(
        [
            invert(at(partner_rank, s), at(partner_needs, s), at(order, s), LANES)
            for s in sources
        ]
    )
    tables = jnp.concatenate([near, far_list[None], filters], axis=0)

    my_rank = at(rank, position)
    oz = owners // 2
    outer_owner = 1 - (oz + oz // 2) % 2
    same_half = owners // 4 == position // 4
    same_line = owners % 2 == y
    source_group = jnp.where(
        same_half, owners ^ position, jnp.where(same_line, 4 + outer_owner, 6 + outer_owner)
    )
    location = jnp.where(
        (owners == position)[:, None],
        within[None, :],
        jnp.where(
            same_half[:, None] | ((inner > 0) & ~same_line)[:, None], my_rank, order
        ),
    )
    hit = column[:, None] == jnp.arange(SPAN * blocks, dtype=jnp.int32)[None, :]
    groups = jnp.broadcast_to(source_group[:, None], location.shape)
    packed = (groups * blocks + location).reshape(-1)
    packed = jnp.sum(jnp.where(hit, packed[None, :], 0), axis=1)
    entries = column.shape[0]
    group, key = packed // blocks, packed % blocks
    steps = jnp.arange(entries, dtype=jnp.int32)
    earlier = (group[:, None] == group[None, :]) & (steps[None, :] < steps[:, None])
    slots = group * capacity + jnp.sum(jnp.where(earlier, 1, 0), axis=1)
    slot_hit = slots[None, :] == jnp.arange(SPAN * capacity, dtype=jnp.int32)[:, None]
    jobs = jnp.sum(
        jnp.where(slot_hit, ((steps // pair_count) * blocks + key)[None, :], 0), axis=1
    )
    return (
        tables,
        (jobs // blocks).astype(jnp.int32),
        (jobs % blocks).astype(jnp.int32),
        (slots + blocks).astype(jnp.int32),
    )


def head_step(width):
    return -(-(width // HEADS + 2) // 8) * 8


def place_kernel(
    stride, assignment_ref, need_ref, features_ref, placed_ref, normed_ref, needs_ref,
    landing, s_send, s_recv,
):
    groups, _, size = assignment_ref.shape
    me = lax.axis_index("elec")
    group = lax.axis_index("groups")
    peers = lax.axis_size("elec")
    position = me // stride
    step_index = pl.program_id(0)

    def toward(step):
        return (group, lax.rem(me + step * stride, peers))

    def ask(step):
        return pltpu.make_async_remote_copy(
            src_ref=need_ref, dst_ref=landing.at[step],
            send_sem=s_send.at[step], recv_sem=s_recv.at[step],
            device_id=toward(step), device_id_type=MESH,
        )

    @pl.when(step_index == 0)
    def _():
        barrier = pltpu.get_barrier_semaphore()
        for step in range(1, SPAN):
            pl.semaphore_signal(barrier, inc=1, device_id=toward(step), device_id_type=MESH)
        pl.semaphore_wait(barrier, SPAN - 1)
        for step in range(1, SPAN):
            ask(step).start()
        landing[0] = need_ref[...]

    lane = lax.broadcasted_iota(jnp.int32, (size, LANES), 1).astype(jnp.float32)
    for i in range(groups):
        rows = pl.ds(i * size, size)
        base = me * (features_ref.shape[0] * pl.num_programs(0)) + (
            (step_index * groups + i) * size
        )
        local = (assignment_ref[i] - base).astype(jnp.float32)
        takes = jnp.broadcast_to(local, (LANES, size)).T
        one_hot = jnp.concatenate(
            [jnp.where(takes == lane + k, 1.0, 0.0) for k in range(0, size, LANES)], axis=1
        ).astype(jnp.bfloat16)
        placed = jnp.dot(one_hot, features_ref[rows, :], preferred_element_type=jnp.float32)
        placed_ref[rows, :] = placed.astype(jnp.bfloat16)
        normed_ref[rows, :] = layer_norm(placed).astype(jnp.bfloat16)

    @pl.when(step_index == pl.num_programs(0) - 1)
    def _():
        for step in range(1, SPAN):
            ask(step).wait()
        for q in range(SPAN):
            needs_ref[q] = landing[lax.rem(position - q + SPAN, SPAN)]


def layer_kernel(
    capacity, stride, pair_count,
    tables_ref, reader_ref, key_ref, slot_ref,
    blocks_ref, placed_ref, wq_ref, wk_ref, wv_ref, wo_ref, wm_ref,
    out_ref,
    near1, near2, near3, far0, far1, side0, side1, out_near, out_far, out_side,
    queries, wv_turned, wo_sorted, parts, attended,
    n_send, n_recv, l_send, f_send, f_recv, p_send, p_recv,
):
    f32, bf16 = jnp.float32, jnp.bfloat16
    me = lax.axis_index("elec")
    group = lax.axis_index("groups")
    peers = lax.axis_size("elec")
    position = me // stride
    rest = lax.rem(me, stride)
    block_count, cluster, width = blocks_ref.shape
    head_width = width // HEADS
    cap = capacity
    z, y = position // 2, lax.rem(position, 2)
    half = z // 2
    inner = lax.rem(z + half, 2)
    pair_z = z + 1 - 2 * lax.rem(z, 2)
    pair_y = 1 - y

    def device(zz, yy):
        return (group, (2 * zz + yy) * stride + rest)

    near_devices = [device(z, pair_y), device(pair_z, y), device(pair_z, pair_y)]
    far_inner = device(2 - half, y)
    near, far, side = [near1, near2, near3], [far0, far1], [side0, side1]
    chunks = [(0, cap), (cap, cap), (2 * cap, block_count - 2 * cap)]

    barrier = pltpu.get_barrier_semaphore()
    for step in range(1, SPAN):
        pl.semaphore_signal(
            barrier, inc=1, device_id=(group, lax.rem(me + step * stride, peers)),
            device_id_type=MESH,
        )
    pl.semaphore_wait(barrier, SPAN - 1)

    def gather(row, first, count, source, target, base):
        def one(k, carry):
            target[base + first + k] = source[tables_ref[row, first + k]]
            return carry

        lax.fori_loop(0, count, one, 0)

    def far_copy(s, c):
        start, count = chunks[c]
        return pltpu.make_async_remote_copy(
            src_ref=out_far.at[pl.ds(start, count)], dst_ref=far[s].at[pl.ds(start, count)],
            send_sem=l_send.at[c], recv_sem=f_recv.at[s, c],
            device_id=far_inner, device_id_type=MESH,
        )

    def forward_copy(s, c):
        start, count = chunks[c]
        return pltpu.make_async_remote_copy(
            src_ref=far[s].at[pl.ds(start, count)], dst_ref=far[s].at[pl.ds(start, count)],
            send_sem=f_send.at[s, c], recv_sem=f_recv.at[s, c],
            device_id=near_devices[1], device_id_type=MESH,
        )

    def side_copy(s, source):
        return pltpu.make_async_remote_copy(
            src_ref=source, dst_ref=side[s], send_sem=p_send.at[s], recv_sem=p_recv.at[s],
            device_id=near_devices[0], device_id_type=MESH,
        )

    def filtered(s):
        return side_copy(s, out_side.at[pl.ds(s * cap, cap)])

    def passed_on(s):
        return side_copy(s, far[s].at[pl.ds(0, cap)])

    def near_copy(t):
        return pltpu.make_async_remote_copy(
            src_ref=out_near.at[pl.ds((t - 1) * cap, cap)], dst_ref=near[t - 1],
            send_sem=n_send.at[t - 1], recv_sem=n_recv.at[t - 1],
            device_id=near_devices[t - 1], device_id_type=MESH,
        )

    def send_near(t):
        gather(t - 1, 0, cap, blocks_ref, out_near, (t - 1) * cap)
        near_copy(t).start()

    def send_far(s, c):
        gather(3, chunks[c][0], chunks[c][1], blocks_ref, out_far, 0)
        far_copy(s, c).start()

    @pl.when(inner == 1)
    def _():
        for c in range(3):
            send_far(0, c)

    for t in (2, 3, 1):
        send_near(t)

    lane = lax.broadcasted_iota(jnp.int32, (cluster, LANES), 1)
    per = LANES // 2 // head_width
    chosen = [
        jnp.where(lane // head_width == c, 1.0, 0.0).astype(bf16) for c in range(2 * per)
    ]
    low = lax.broadcasted_iota(jnp.int32, (head_width, LANES), 1) < cluster
    scale = math.log2(math.e) / head_width**0.5
    turned = (((1,), (1,)), ((), ()))

    def unit(size):
        row = lax.broadcasted_iota(jnp.int32, (size, size), 0)
        column = lax.broadcasted_iota(jnp.int32, (size, size), 1)
        return jnp.where(row == column, 1.0, 0.0).astype(bf16)

    wv_turned[...] = lax.dot_general(
        unit(width), wv_ref[...], turned, preferred_element_type=f32
    ).astype(bf16)
    for h in range(HEADS):
        start = (h % 2) * (width // 2) + (h // 2) * head_width
        wo_sorted[start : start + head_width, :] = wo_ref[
            h * head_width : (h + 1) * head_width, :
        ]

    def project(i, carry):
        rows = blocks_ref[pl.ds(i * SPAN, SPAN)].reshape(SPAN * cluster, width)
        result = jnp.dot(rows, wq_ref[...], preferred_element_type=f32) * scale
        queries[pl.ds(i * SPAN, SPAN)] = result.astype(bf16).reshape(SPAN, cluster, width)
        return carry

    lax.fori_loop(0, block_count // SPAN, project, 0)

    def several(places, query_blocks, key_blocks):
        count = len(places)
        keys = jnp.dot(
            jnp.concatenate(key_blocks, axis=0), wk_ref[...], preferred_element_type=f32
        ).astype(bf16)
        values = [
            lax.dot_general(wv_turned[...], rows, turned, preferred_element_type=f32).astype(bf16)
            for rows in key_blocks
        ]
        scores = []
        for i in range(count):
            for g in range(HEADS // per):
                band = (g // 2) * LANES
                query = query_blocks[i][:, band : band + LANES]
                stacked = jnp.concatenate(
                    [query * chosen[(g % 2) * per + c] for c in range(per)], axis=0
                )
                scores.append(
                    lax.dot_general(
                        keys[i * cluster : (i + 1) * cluster, band : band + LANES],
                        stacked, turned, preferred_element_type=f32,
                    )
                )
        weights = []
        for i in range(count):
            for g in range(HEADS // per):
                score = scores[i * (HEADS // per) + g]
                columns = pl.ds(g * per * cluster, per * cluster)
                top = jnp.max(score, axis=0, keepdims=True)
                weight = jnp.exp2(score - top)
                parts[places[i], head_width : head_width + 1, columns] = top
                parts[places[i], head_width + 1 : head_width + 2, columns] = jnp.sum(
                    weight, axis=0, keepdims=True
                )
                weights.append(weight.astype(bf16))
        for i in range(count):
            for g in range(HEADS // per):
                rows = per * head_width
                result = jnp.dot(
                    values[i][g * rows : (g + 1) * rows], weights[i * (HEADS // per) + g],
                    preferred_element_type=f32,
                )
                for k in range(per // 2):
                    top = 2 * k * head_width
                    lanes = slice(k * LANES, (k + 1) * LANES)
                    first = (g * per // 2 + k) * LANES
                    parts[places[i], 0:head_width, pl.ds(first, LANES)] = jnp.where(
                        low,
                        result[top : top + head_width, lanes],
                        result[top + head_width : top + 2 * head_width, lanes],
                    )

    def own_blocks(first, count, batch):
        def one(i, carry):
            index = [first + i * batch + k for k in range(batch)]
            several(index, [queries[j] for j in index], [blocks_ref[j] for j in index])
            return carry

        lax.fori_loop(0, count // batch, one, 0)

    def listed(which, source):
        batch = 5 if cap % 5 == 0 else 1

        def one(i, carry):
            index = [which * cap + i * batch + k for k in range(batch)]
            several(
                [block_count + j for j in index],
                [queries[reader_ref[j]] for j in index],
                [source[key_ref[j]] for j in index],
            )
            return carry

        lax.fori_loop(0, cap // batch, one, 0)

    def on_inner(work):
        pl.when(inner == 1)(work)

    def on_outer(work):
        pl.when(inner == 0)(work)

    def relay(s, c):
        far_copy(s, c).wait_recv()
        forward_copy(s, c).start()

    def refine(s):
        far_copy(s, 2).wait_recv()
        gather(4 + s, 0, cap, far[s], out_side, s * cap)
        filtered(s).start()

    def pass_on(s):
        far_copy(s, 0).wait_recv()
        passed_on(s).start()

    own_blocks(0, block_count // 2, 4)

    @pl.when(inner == 0)
    def _():
        for c in range(3):
            send_far(1, c)

    on_inner(lambda: relay(0, 0))
    own_blocks(block_count // 2, block_count // 2, 4)
    on_inner(lambda: relay(0, 1))
    listed(0, blocks_ref)
    near_copy(1).wait_recv()
    listed(1, near1)
    near_copy(2).wait_recv()
    listed(2, near2)
    near_copy(3).wait_recv()
    listed(3, near3)
    on_inner(lambda: refine(0))
    on_inner(lambda: relay(1, 0))
    on_outer(lambda: pass_on(0))
    on_outer(lambda: far_copy(0, 1).wait_recv())
    listed(4, far0)
    on_inner(lambda: relay(1, 1))
    on_outer(lambda: pass_on(1))
    filtered(0).wait_recv()
    listed(6, side0)
    on_inner(lambda: refine(1))

    @pl.when(inner == 1)
    def _():
        listed(5, far1)
        filtered(1).wait_recv()
        listed(7, side1)

    @pl.when(inner == 0)
    def _():
        filtered(1).wait_recv()
        listed(7, side1)
        far_copy(1, 1).wait_recv()
        listed(5, far1)

    def combine(i, carry):
        for k in range(SPAN):
            j = i * SPAN + k
            places = [j] + [slot_ref[j * pair_count + p] for p in range(pair_count)]
            tops = [parts[a, head_width : head_width + 1, :] for a in places]
            sums = [parts[a, head_width + 1 : head_width + 2, :] for a in places]
            top = functools.reduce(jnp.maximum, tops)
            factors = [jnp.exp2(t - top) for t in tops]
            total = sum(f * s for f, s in zip(factors, sums))
            inverse = 1.0 / total
            merged = sum(
                parts[a, 0:head_width, :] * (f * inverse) for a, f in zip(places, factors)
            ).astype(bf16)
            stacked = jnp.concatenate(
                [merged[:, c : c + LANES] for c in range(0, HEADS * cluster, LANES)], axis=0
            )
            upright = lax.dot_general(
                unit(LANES), stacked, turned, preferred_element_type=f32
            ).astype(bf16)
            rows = slice(k * cluster, (k + 1) * cluster)
            attended[rows, 0:LANES] = upright[0:cluster]
            attended[rows, LANES : 2 * LANES] = upright[cluster : 2 * cluster]
        here = pl.ds(pl.multiple_of(i * SPAN * cluster, SPAN * cluster), SPAN * cluster)
        projected = jnp.dot(attended[...], wo_sorted[...], preferred_element_type=f32)
        middle = (placed_ref[here, :].astype(f32) + projected).astype(bf16).astype(f32)
        second = layer_norm(middle).astype(bf16)
        mixed = middle + jnp.tanh(jnp.dot(second, wm_ref[...], preferred_element_type=f32))
        out_ref[here, :] = mixed.astype(bf16)
        return carry

    lax.fori_loop(0, block_count // SPAN, combine, 0)

    @pl.when(inner == 1)
    def _():
        for s in range(2):
            for c in range(2):
                forward_copy(s, c).wait_send()
            filtered(s).wait_send()

    @pl.when(inner == 0)
    def _():
        for s in range(2):
            passed_on(s).wait_send()

    for c in range(3):
        far_copy(0, c).wait_send()
    for t in range(1, 4):
        near_copy(t).wait_send()


def body(features, assignment, pairs, w_query, w_key, w_value, w_out, w_mix):
    rows_dev, width = features.shape
    block_count, pair_count = pairs.shape
    cluster = rows_dev // block_count
    capacity = (block_count * pair_count + SPAN - 1) // SPAN + 1
    stride = lax.axis_size("elec") // SPAN
    position = lax.axis_index("elec") // stride
    group_rows = SPAN * cluster
    groups = rows_dev // group_rows
    bf16 = jnp.bfloat16

    column, need = own_needs(pairs, block_count, stride)
    need_rows = SPAN * block_count // LANES
    batch = math.gcd(groups, 2)
    tile = pl.BlockSpec((batch * group_rows, width), lambda i: (i, 0))
    placed, normed, needs = pl.pallas_call(
        functools.partial(place_kernel, stride),
        grid=(groups // batch,),
        in_specs=[
            pl.BlockSpec((batch, 1, group_rows), lambda i: (i, 0, 0)),
            pl.BlockSpec((need_rows, LANES), lambda i: (0, 0)),
            tile,
        ],
        out_specs=[tile, tile, pl.BlockSpec((SPAN, need_rows, LANES), lambda i: (0, 0, 0))],
        out_shape=[jax.ShapeDtypeStruct((rows_dev, width), bf16)] * 2
        + [jax.ShapeDtypeStruct((SPAN, need_rows, LANES), jnp.int32)],
        scratch_shapes=[
            pltpu.VMEM((SPAN, need_rows, LANES), jnp.int32),
            pltpu.SemaphoreType.DMA((SPAN,)),
            pltpu.SemaphoreType.DMA((SPAN,)),
        ],
        compiler_params=pltpu.CompilerParams(collective_id=1, has_side_effects=True),
    )(
        assignment.reshape(groups, 1, group_rows), need.reshape(need_rows, LANES), features
    )

    tables, reader, key, slot = make_plan(
        needs.reshape(SPAN, SPAN, block_count), column, position, capacity, pair_count
    )
    block = (cluster, width)
    part = (head_step(width), HEADS * cluster)
    in_smem = pl.BlockSpec(memory_space=pltpu.SMEM)
    in_vmem = pl.BlockSpec(memory_space=pltpu.VMEM)
    return pl.pallas_call(
        functools.partial(layer_kernel, capacity, stride, pair_count),
        in_specs=[in_smem] * 4 + [in_vmem] * 7,
        out_specs=in_vmem,
        out_shape=jax.ShapeDtypeStruct((rows_dev, width), bf16),
        scratch_shapes=[pltpu.VMEM((capacity,) + block, bf16)] * 3
        + [pltpu.VMEM((block_count,) + block, bf16)] * 2
        + [pltpu.VMEM((capacity,) + block, bf16)] * 2
        + [
            pltpu.VMEM((3 * capacity,) + block, bf16),
            pltpu.VMEM((block_count,) + block, bf16),
            pltpu.VMEM((2 * capacity,) + block, bf16),
            pltpu.VMEM((block_count,) + block, bf16),
            pltpu.VMEM((width, width), bf16),
            pltpu.VMEM((width, width), bf16),
            pltpu.VMEM((block_count + SPAN * capacity,) + part, jnp.float32),
            pltpu.VMEM((SPAN * cluster, width), bf16),
            pltpu.SemaphoreType.DMA((3,)),
            pltpu.SemaphoreType.DMA((3,)),
            pltpu.SemaphoreType.DMA((3,)),
            pltpu.SemaphoreType.DMA((2, 2)),
            pltpu.SemaphoreType.DMA((2, 3)),
            pltpu.SemaphoreType.DMA((2,)),
            pltpu.SemaphoreType.DMA((2,)),
        ],
        compiler_params=pltpu.CompilerParams(
            collective_id=0, has_side_effects=True, vmem_limit_bytes=60 * 2**20
        ),
    )(
        tables, reader, key, slot, normed.reshape(block_count, cluster, width), placed,
        w_query, w_key, w_value, w_out, w_mix,
    )


def solution(mesh):
    placed = (
        P(("groups", "elec"), None),
        P(("groups", "elec")),
        P(("groups", "elec"), None),
        P(),
        P(),
        P(),
        P(),
        P(),
    )
    return jax.shard_map(
        body, mesh=mesh, in_specs=placed, out_specs=P(("groups", "elec"), None), check_vma=False
    )
```

```python
import functools
import math

import jax
import jax.numpy as jnp
from jax import lax
from jax.experimental import pallas as pl
from jax.experimental.pallas import tpu as pltpu
from jax.sharding import PartitionSpec as P

HEADS = 16
SPAN = 8
LANES = 128
MESH = pl.DeviceIdType.MESH


def layer_norm(rows):
    mean = jnp.mean(rows, axis=-1, keepdims=True)
    centred = rows - mean
    variance = jnp.mean(centred * centred, axis=-1, keepdims=True)
    return centred * lax.rsqrt(variance + 1e-05)


def own_needs(listed, block_count, stride):
    flat = listed.reshape(-1)
    column = (flat // block_count // stride) * block_count + flat % block_count
    columns = jnp.arange(SPAN * block_count, dtype=jnp.int32)
    hit = column[None, :] == columns[:, None]
    return column, jnp.max(jnp.where(hit, 1, 0), axis=1).astype(jnp.int32)


def before(flags):
    size = flags.shape[-1]
    lower = (jnp.arange(size)[:, None] < jnp.arange(size)[None, :]).astype(jnp.bfloat16)
    counts = jnp.dot(
        flags.reshape(-1, size).astype(jnp.bfloat16), lower, preferred_element_type=jnp.float32
    )
    return counts.reshape(flags.shape).astype(jnp.int32)


def invert(place, flags, values, size):
    hit = (place[..., None, :] == jnp.arange(size, dtype=jnp.int32)[:, None]) & (
        flags[..., None, :] > 0
    )
    return jnp.sum(jnp.where(hit, values[..., None, :], 0), axis=-1).astype(jnp.int32)


def make_plan(needs, column, position, capacity, pair_count):
    blocks = needs.shape[-1]
    owners = jnp.arange(SPAN, dtype=jnp.int32)
    static = list(range(SPAN))
    ends = [2 * (3 * (1 - o // 4)) + o % 2 for o in static]
    first = jnp.stack([needs[ends[o] ^ 1, o] for o in static])
    second = jnp.stack([needs[ends[o], o] for o in static]) * (1 - first)
    third = 1 - first - second
    c0, c1, c2 = before(first), before(second), before(third)
    n0 = jnp.sum(first, axis=1, keepdims=True)
    n1 = jnp.sum(second, axis=1, keepdims=True)
    order = jnp.where(first > 0, c0, jnp.where(second > 0, n0 + c1, n0 + n1 + c2))
    rank = before(needs)
    within = jnp.arange(blocks, dtype=jnp.int32)

    def at(array, index):
        return lax.dynamic_index_in_dim(array, index, 0, keepdims=False)

    mine = lax.dynamic_index_in_dim(needs, position, 1, keepdims=False)
    mine_rank = lax.dynamic_index_in_dim(rank, position, 1, keepdims=False)
    near = jnp.stack(
        [
            invert(at(mine_rank, position ^ t), at(mine, position ^ t), within, LANES)
            for t in range(1, 4)
        ]
    )
    all_flags = jnp.ones((blocks,), jnp.int32)
    far_list = invert(at(order, position), all_flags, within, LANES)

    z, y = position // 2, position % 2
    half = z // 2
    inner = (z + half) % 2
    partner_needs = at(needs, position ^ 1)
    partner_rank = at(rank, position ^ 1)
    sources = [2 * (2 - half) + y, 2 * (3 * (1 - half)) + y]
    filters = jnp.stack(
        [
            invert(at(partner_rank, s), at(partner_needs, s), at(order, s), LANES)
            for s in sources
        ]
    )
    tables = jnp.concatenate([near, far_list[None], filters], axis=0)

    my_rank = at(rank, position)
    oz = owners // 2
    outer_owner = 1 - (oz + oz // 2) % 2
    same_half = owners // 4 == position // 4
    same_line = owners % 2 == y
    source_group = jnp.where(
        same_half, owners ^ position, jnp.where(same_line, 4 + outer_owner, 6 + outer_owner)
    )
    location = jnp.where(
        (owners == position)[:, None],
        within[None, :],
        jnp.where(
            same_half[:, None] | ((inner > 0) & ~same_line)[:, None], my_rank, order
        ),
    )
    hit = column[:, None] == jnp.arange(SPAN * blocks, dtype=jnp.int32)[None, :]
    groups = jnp.broadcast_to(source_group[:, None], location.shape)
    packed = (groups * blocks + location).reshape(-1)
    packed = jnp.sum(jnp.where(hit, packed[None, :], 0), axis=1)
    entries = column.shape[0]
    group, key = packed // blocks, packed % blocks
    steps = jnp.arange(entries, dtype=jnp.int32)
    earlier = (group[:, None] == group[None, :]) & (steps[None, :] < steps[:, None])
    slots = group * capacity + jnp.sum(jnp.where(earlier, 1, 0), axis=1)
    slot_hit = slots[None, :] == jnp.arange(SPAN * capacity, dtype=jnp.int32)[:, None]
    jobs = jnp.sum(
        jnp.where(slot_hit, ((steps // pair_count) * blocks + key)[None, :], 0), axis=1
    )
    return (
        tables,
        (jobs // blocks).astype(jnp.int32),
        (jobs % blocks).astype(jnp.int32),
        (slots + blocks).astype(jnp.int32),
    )


def head_step(width):
    return -(-(width // HEADS + 2) // 8) * 8


def place_kernel(
    stride, assignment_ref, need_ref, features_ref, placed_ref, normed_ref, needs_ref,
    landing, s_send, s_recv,
):
    groups, _, size = assignment_ref.shape
    me = lax.axis_index("elec")
    group = lax.axis_index("groups")
    peers = lax.axis_size("elec")
    position = me // stride
    step_index = pl.program_id(0)

    def toward(step):
        return (group, lax.rem(me + step * stride, peers))

    def ask(step):
        return pltpu.make_async_remote_copy(
            src_ref=need_ref, dst_ref=landing.at[step],
            send_sem=s_send.at[step], recv_sem=s_recv.at[step],
            device_id=toward(step), device_id_type=MESH,
        )

    @pl.when(step_index == 0)
    def _():
        barrier = pltpu.get_barrier_semaphore()
        for step in range(1, SPAN):
            pl.semaphore_signal(barrier, inc=1, device_id=toward(step), device_id_type=MESH)
        pl.semaphore_wait(barrier, SPAN - 1)
        for step in range(1, SPAN):
            ask(step).start()
        landing[0] = need_ref[...]

    lane = lax.broadcasted_iota(jnp.int32, (size, LANES), 1).astype(jnp.float32)
    for i in range(groups):
        rows = pl.ds(i * size, size)
        base = me * (features_ref.shape[0] * pl.num_programs(0)) + (
            (step_index * groups + i) * size
        )
        local = (assignment_ref[i] - base).astype(jnp.float32)
        takes = jnp.broadcast_to(local, (LANES, size)).T
        one_hot = jnp.concatenate(
            [jnp.where(takes == lane + k, 1.0, 0.0) for k in range(0, size, LANES)], axis=1
        ).astype(jnp.bfloat16)
        placed = jnp.dot(one_hot, features_ref[rows, :], preferred_element_type=jnp.float32)
        placed_ref[rows, :] = placed.astype(jnp.bfloat16)
        normed_ref[rows, :] = layer_norm(placed).astype(jnp.bfloat16)

    @pl.when(step_index == pl.num_programs(0) - 1)
    def _():
        for step in range(1, SPAN):
            ask(step).wait()
        for q in range(SPAN):
            needs_ref[q] = landing[lax.rem(position - q + SPAN, SPAN)]


def layer_kernel(
    capacity, stride, pair_count,
    tables_ref, reader_ref, key_ref, slot_ref,
    blocks_ref, placed_ref, wq_ref, wk_ref, wv_ref, wo_ref, wm_ref,
    out_ref,
    near1, near2, near3, far0, far1, side0, side1, out_near, out_far, out_side,
    queries, wv_turned, wo_sorted, parts, attended,
    n_send, n_recv, l_send, f_send, f_recv, p_send, p_recv,
):
    f32, bf16 = jnp.float32, jnp.bfloat16
    me = lax.axis_index("elec")
    group = lax.axis_index("groups")
    peers = lax.axis_size("elec")
    position = me // stride
    rest = lax.rem(me, stride)
    block_count, cluster, width = blocks_ref.shape
    head_width = width // HEADS
    cap = capacity
    z, y = position // 2, lax.rem(position, 2)
    half = z // 2
    inner = lax.rem(z + half, 2)
    pair_z = z + 1 - 2 * lax.rem(z, 2)
    pair_y = 1 - y

    def device(zz, yy):
        return (group, (2 * zz + yy) * stride + rest)

    near_devices = [device(z, pair_y), device(pair_z, y), device(pair_z, pair_y)]
    far_inner = device(2 - half, y)
    near, far, side = [near1, near2, near3], [far0, far1], [side0, side1]
    first_half = (cap + 1) // 2
    bounds = [0, first_half, cap, cap + first_half, 2 * cap, block_count]
    chunks = [(a, b - a) for a, b in zip(bounds, bounds[1:])]
    last = len(chunks) - 1

    barrier = pltpu.get_barrier_semaphore()
    for step in range(1, SPAN):
        pl.semaphore_signal(
            barrier, inc=1, device_id=(group, lax.rem(me + step * stride, peers)),
            device_id_type=MESH,
        )
    pl.semaphore_wait(barrier, SPAN - 1)

    def gather(row, first, count, source, target, base):
        def one(k, carry):
            target[base + first + k] = source[tables_ref[row, first + k]]
            return carry

        lax.fori_loop(0, count, one, 0)

    def far_copy(s, c):
        start, count = chunks[c]
        return pltpu.make_async_remote_copy(
            src_ref=out_far.at[pl.ds(start, count)], dst_ref=far[s].at[pl.ds(start, count)],
            send_sem=l_send.at[c], recv_sem=f_recv.at[s, c],
            device_id=far_inner, device_id_type=MESH,
        )

    def forward_copy(s, c):
        start, count = chunks[c]
        return pltpu.make_async_remote_copy(
            src_ref=far[s].at[pl.ds(start, count)], dst_ref=far[s].at[pl.ds(start, count)],
            send_sem=f_send.at[s, c], recv_sem=f_recv.at[s, c],
            device_id=near_devices[1], device_id_type=MESH,
        )

    def side_copy(s, k, source, base):
        start, count = chunks[k]
        return pltpu.make_async_remote_copy(
            src_ref=source.at[pl.ds(base + start, count)], dst_ref=side[s].at[pl.ds(start, count)],
            send_sem=p_send.at[s, k], recv_sem=p_recv.at[s, k],
            device_id=near_devices[0], device_id_type=MESH,
        )

    def filtered(s, k):
        return side_copy(s, k, out_side, s * cap)

    def passed_on(s, k):
        return side_copy(s, k, far[s], 0)

    def near_copy(t):
        return pltpu.make_async_remote_copy(
            src_ref=out_near.at[pl.ds((t - 1) * cap, cap)], dst_ref=near[t - 1],
            send_sem=n_send.at[t - 1], recv_sem=n_recv.at[t - 1],
            device_id=near_devices[t - 1], device_id_type=MESH,
        )

    def send_near(t):
        gather(t - 1, 0, cap, blocks_ref, out_near, (t - 1) * cap)
        near_copy(t).start()

    def send_far(s, c):
        gather(3, chunks[c][0], chunks[c][1], blocks_ref, out_far, 0)
        far_copy(s, c).start()

    @pl.when(inner == 1)
    def _():
        for c in range(last + 1):
            send_far(0, c)

    @pl.when(inner == 0)
    def _():
        for c in range(last + 1):
            send_far(1, c)

    for t in (2, 3, 1):
        send_near(t)

    lane = lax.broadcasted_iota(jnp.int32, (cluster, LANES), 1)
    per = LANES // 2 // head_width
    chosen = [
        jnp.where(lane // head_width == c, 1.0, 0.0).astype(bf16) for c in range(2 * per)
    ]
    low = lax.broadcasted_iota(jnp.int32, (head_width, LANES), 1) < cluster
    scale = math.log2(math.e) / head_width**0.5
    turned = (((1,), (1,)), ((), ()))

    def unit(size):
        row = lax.broadcasted_iota(jnp.int32, (size, size), 0)
        column = lax.broadcasted_iota(jnp.int32, (size, size), 1)
        return jnp.where(row == column, 1.0, 0.0).astype(bf16)

    wv_turned[...] = lax.dot_general(
        unit(width), wv_ref[...], turned, preferred_element_type=f32
    ).astype(bf16)
    for h in range(HEADS):
        start = (h % 2) * (width // 2) + (h // 2) * head_width
        wo_sorted[start : start + head_width, :] = wo_ref[
            h * head_width : (h + 1) * head_width, :
        ]

    def project(i, carry):
        rows = blocks_ref[pl.ds(i * SPAN, SPAN)].reshape(SPAN * cluster, width)
        result = jnp.dot(rows, wq_ref[...], preferred_element_type=f32) * scale
        queries[pl.ds(i * SPAN, SPAN)] = result.astype(bf16).reshape(SPAN, cluster, width)
        return carry

    lax.fori_loop(0, block_count // SPAN, project, 0)

    def several(places, query_blocks, key_blocks):
        count = len(places)
        keys = jnp.dot(
            jnp.concatenate(key_blocks, axis=0), wk_ref[...], preferred_element_type=f32
        ).astype(bf16)
        values = [
            lax.dot_general(wv_turned[...], rows, turned, preferred_element_type=f32).astype(bf16)
            for rows in key_blocks
        ]
        scores = []
        for i in range(count):
            for g in range(HEADS // per):
                band = (g // 2) * LANES
                query = query_blocks[i][:, band : band + LANES]
                stacked = jnp.concatenate(
                    [query * chosen[(g % 2) * per + c] for c in range(per)], axis=0
                )
                scores.append(
                    lax.dot_general(
                        keys[i * cluster : (i + 1) * cluster, band : band + LANES],
                        stacked, turned, preferred_element_type=f32,
                    )
                )
        weights = []
        for i in range(count):
            for g in range(HEADS // per):
                score = scores[i * (HEADS // per) + g]
                columns = pl.ds(g * per * cluster, per * cluster)
                top = jnp.max(score, axis=0, keepdims=True)
                weight = jnp.exp2(score - top)
                parts[places[i], head_width : head_width + 1, columns] = top
                parts[places[i], head_width + 1 : head_width + 2, columns] = jnp.sum(
                    weight, axis=0, keepdims=True
                )
                weights.append(weight.astype(bf16))
        for i in range(count):
            for g in range(HEADS // per):
                rows = per * head_width
                result = jnp.dot(
                    values[i][g * rows : (g + 1) * rows], weights[i * (HEADS // per) + g],
                    preferred_element_type=f32,
                )
                for k in range(per // 2):
                    top = 2 * k * head_width
                    lanes = slice(k * LANES, (k + 1) * LANES)
                    first = (g * per // 2 + k) * LANES
                    parts[places[i], 0:head_width, pl.ds(first, LANES)] = jnp.where(
                        low,
                        result[top : top + head_width, lanes],
                        result[top + head_width : top + 2 * head_width, lanes],
                    )

    def own_blocks(first, count, batch):
        def one(i, carry):
            index = [first + i * batch + k for k in range(batch)]
            several(index, [queries[j] for j in index], [blocks_ref[j] for j in index])
            return carry

        lax.fori_loop(0, count // batch, one, 0)

    def listed(which, source):
        batch = 5 if cap % 5 == 0 else 1

        def one(i, carry):
            index = [which * cap + i * batch + k for k in range(batch)]
            several(
                [block_count + j for j in index],
                [queries[reader_ref[j]] for j in index],
                [source[key_ref[j]] for j in index],
            )
            return carry

        lax.fori_loop(0, cap // batch, one, 0)

    def on_inner(work):
        pl.when(inner == 1)(work)

    def on_outer(work):
        pl.when(inner == 0)(work)

    def relay(s, c):
        far_copy(s, c).wait_recv()
        forward_copy(s, c).start()

    def refine(s):
        far_copy(s, last).wait_recv()
        gather(4 + s, 0, cap, far[s], out_side, s * cap)
        for k in range(2):
            filtered(s, k).start()

    def pass_on(s, k):
        far_copy(s, k).wait_recv()
        passed_on(s, k).start()

    def arrived(s, first, stop):
        for c in range(first, stop):
            far_copy(s, c).wait_recv()

    def side_arrived(s):
        for k in range(2):
            filtered(s, k).wait_recv()

    eighth = block_count // 8
    own_blocks(0, 3 * eighth, 4)
    on_inner(lambda: relay(1, 0))
    own_blocks(3 * eighth, 3 * eighth, 4)
    on_inner(lambda: relay(1, 1))
    own_blocks(6 * eighth, 2 * eighth, 4)
    on_inner(lambda: relay(1, 2))
    listed(0, blocks_ref)
    on_inner(lambda: relay(1, 3))
    near_copy(1).wait_recv()
    listed(1, near1)
    on_inner(lambda: refine(1))

    @pl.when(inner == 1)
    def _():
        listed(5, far1)
        relay(0, 0)
        side_arrived(1)
        listed(7, side1)
        relay(0, 1)
        near_copy(2).wait_recv()
        listed(2, near2)
        relay(0, 2)
        near_copy(3).wait_recv()
        relay(0, 3)
        refine(0)
        listed(3, near3)
        listed(4, far0)
        side_arrived(0)
        listed(6, side0)

    @pl.when(inner == 0)
    def _():
        pass_on(1, 0)
        pass_on(1, 1)
        near_copy(2).wait_recv()
        listed(2, near2)
        near_copy(3).wait_recv()
        listed(3, near3)
        arrived(1, 2, 4)
        listed(5, far1)
        side_arrived(1)
        listed(7, side1)
        pass_on(0, 0)
        pass_on(0, 1)
        side_arrived(0)
        listed(6, side0)
        arrived(0, 2, 4)
        listed(4, far0)

    def combine(i, carry):
        for k in range(SPAN):
            j = i * SPAN + k
            places = [j] + [slot_ref[j * pair_count + p] for p in range(pair_count)]
            tops = [parts[a, head_width : head_width + 1, :] for a in places]
            sums = [parts[a, head_width + 1 : head_width + 2, :] for a in places]
            top = functools.reduce(jnp.maximum, tops)
            factors = [jnp.exp2(t - top) for t in tops]
            total = sum(f * s for f, s in zip(factors, sums))
            inverse = 1.0 / total
            merged = sum(
                parts[a, 0:head_width, :] * (f * inverse) for a, f in zip(places, factors)
            ).astype(bf16)
            stacked = jnp.concatenate(
                [merged[:, c : c + LANES] for c in range(0, HEADS * cluster, LANES)], axis=0
            )
            upright = lax.dot_general(
                unit(LANES), stacked, turned, preferred_element_type=f32
            ).astype(bf16)
            rows = slice(k * cluster, (k + 1) * cluster)
            attended[rows, 0:LANES] = upright[0:cluster]
            attended[rows, LANES : 2 * LANES] = upright[cluster : 2 * cluster]
        here = pl.ds(pl.multiple_of(i * SPAN * cluster, SPAN * cluster), SPAN * cluster)
        projected = jnp.dot(attended[...], wo_sorted[...], preferred_element_type=f32)
        middle = (placed_ref[here, :].astype(f32) + projected).astype(bf16).astype(f32)
        second = layer_norm(middle).astype(bf16)
        mixed = middle + jnp.tanh(jnp.dot(second, wm_ref[...], preferred_element_type=f32))
        out_ref[here, :] = mixed.astype(bf16)
        return carry

    lax.fori_loop(0, block_count // SPAN, combine, 0)

    @pl.when(inner == 1)
    def _():
        for s in range(2):
            for c in range(last):
                forward_copy(s, c).wait_send()
            for k in range(2):
                filtered(s, k).wait_send()

    @pl.when(inner == 0)
    def _():
        for s in range(2):
            for k in range(2):
                passed_on(s, k).wait_send()

    for c in range(last + 1):
        far_copy(0, c).wait_send()
    for t in range(1, 4):
        near_copy(t).wait_send()


def body(features, assignment, pairs, w_query, w_key, w_value, w_out, w_mix):
    rows_dev, width = features.shape
    block_count, pair_count = pairs.shape
    cluster = rows_dev // block_count
    capacity = (block_count * pair_count + SPAN - 1) // SPAN + 1
    stride = lax.axis_size("elec") // SPAN
    position = lax.axis_index("elec") // stride
    group_rows = SPAN * cluster
    groups = rows_dev // group_rows
    bf16 = jnp.bfloat16

    column, need = own_needs(pairs, block_count, stride)
    need_rows = SPAN * block_count // LANES
    batch = math.gcd(groups, 2)
    tile = pl.BlockSpec((batch * group_rows, width), lambda i: (i, 0))
    placed, normed, needs = pl.pallas_call(
        functools.partial(place_kernel, stride),
        grid=(groups // batch,),
        in_specs=[
            pl.BlockSpec((batch, 1, group_rows), lambda i: (i, 0, 0)),
            pl.BlockSpec((need_rows, LANES), lambda i: (0, 0)),
            tile,
        ],
        out_specs=[tile, tile, pl.BlockSpec((SPAN, need_rows, LANES), lambda i: (0, 0, 0))],
        out_shape=[jax.ShapeDtypeStruct((rows_dev, width), bf16)] * 2
        + [jax.ShapeDtypeStruct((SPAN, need_rows, LANES), jnp.int32)],
        scratch_shapes=[
            pltpu.VMEM((SPAN, need_rows, LANES), jnp.int32),
            pltpu.SemaphoreType.DMA((SPAN,)),
            pltpu.SemaphoreType.DMA((SPAN,)),
        ],
        compiler_params=pltpu.CompilerParams(collective_id=1, has_side_effects=True),
    )(
        assignment.reshape(groups, 1, group_rows), need.reshape(need_rows, LANES), features
    )

    tables, reader, key, slot = make_plan(
        needs.reshape(SPAN, SPAN, block_count), column, position, capacity, pair_count
    )
    block = (cluster, width)
    part = (head_step(width), HEADS * cluster)
    in_smem = pl.BlockSpec(memory_space=pltpu.SMEM)
    in_vmem = pl.BlockSpec(memory_space=pltpu.VMEM)
    return pl.pallas_call(
        functools.partial(layer_kernel, capacity, stride, pair_count),
        in_specs=[in_smem] * 4 + [in_vmem] * 7,
        out_specs=in_vmem,
        out_shape=jax.ShapeDtypeStruct((rows_dev, width), bf16),
        scratch_shapes=[pltpu.VMEM((capacity,) + block, bf16)] * 3
        + [pltpu.VMEM((block_count,) + block, bf16)] * 2
        + [pltpu.VMEM((capacity,) + block, bf16)] * 2
        + [
            pltpu.VMEM((3 * capacity,) + block, bf16),
            pltpu.VMEM((block_count,) + block, bf16),
            pltpu.VMEM((2 * capacity,) + block, bf16),
            pltpu.VMEM((block_count,) + block, bf16),
            pltpu.VMEM((width, width), bf16),
            pltpu.VMEM((width, width), bf16),
            pltpu.VMEM((block_count + SPAN * capacity,) + part, jnp.float32),
            pltpu.VMEM((SPAN * cluster, width), bf16),
            pltpu.SemaphoreType.DMA((3,)),
            pltpu.SemaphoreType.DMA((3,)),
            pltpu.SemaphoreType.DMA((5,)),
            pltpu.SemaphoreType.DMA((2, 4)),
            pltpu.SemaphoreType.DMA((2, 5)),
            pltpu.SemaphoreType.DMA((2, 2)),
            pltpu.SemaphoreType.DMA((2, 2)),
        ],
        compiler_params=pltpu.CompilerParams(
            collective_id=0, has_side_effects=True, vmem_limit_bytes=60 * 2**20
        ),
    )(
        tables, reader, key, slot, normed.reshape(block_count, cluster, width), placed,
        w_query, w_key, w_value, w_out, w_mix,
    )


def solution(mesh):
    placed = (
        P(("groups", "elec"), None),
        P(("groups", "elec")),
        P(("groups", "elec"), None),
        P(),
        P(),
        P(),
        P(),
        P(),
    )
    return jax.shard_map(
        body, mesh=mesh, in_specs=placed, out_specs=P(("groups", "elec"), None), check_vma=False
    )
```

```python
import functools
import math

import jax
import jax.numpy as jnp
from jax import lax
from jax.experimental import pallas as pl
from jax.experimental.pallas import tpu as pltpu
from jax.sharding import PartitionSpec as P

HEADS = 16
SPAN = 8
LANES = 128
MESH = pl.DeviceIdType.MESH


def layer_norm(rows):
    mean = jnp.mean(rows, axis=-1, keepdims=True)
    centred = rows - mean
    variance = jnp.mean(centred * centred, axis=-1, keepdims=True)
    return centred * lax.rsqrt(variance + 1e-05)


def own_needs(listed, block_count, stride):
    flat = listed.reshape(-1)
    column = (flat // block_count // stride) * block_count + flat % block_count
    columns = jnp.arange(SPAN * block_count, dtype=jnp.int32)
    hit = column[None, :] == columns[:, None]
    return column, jnp.max(jnp.where(hit, 1, 0), axis=1).astype(jnp.int32)


def before(flags):
    size = flags.shape[-1]
    lower = (jnp.arange(size)[:, None] < jnp.arange(size)[None, :]).astype(jnp.bfloat16)
    counts = jnp.dot(
        flags.reshape(-1, size).astype(jnp.bfloat16), lower, preferred_element_type=jnp.float32
    )
    return counts.reshape(flags.shape).astype(jnp.int32)


def invert(place, flags, values, size):
    hit = (place[..., None, :] == jnp.arange(size, dtype=jnp.int32)[:, None]) & (
        flags[..., None, :] > 0
    )
    return jnp.sum(jnp.where(hit, values[..., None, :], 0), axis=-1).astype(jnp.int32)


def make_plan(needs, column, position, capacity, pair_count):
    blocks = needs.shape[-1]
    owners = jnp.arange(SPAN, dtype=jnp.int32)
    static = list(range(SPAN))

    def arrange(*readers):
        flags, left = [], jnp.ones((SPAN, blocks), jnp.int32)
        for chosen in readers:
            flags.append(jnp.stack([needs[chosen(o), o] for o in static]) * left)
            left = left - flags[-1]
        flags = jnp.stack(flags + [left])
        counts = jnp.sum(flags, axis=-1, keepdims=True)
        start = jnp.cumsum(counts, axis=0) - counts
        return jnp.sum(flags * (before(flags) + start), axis=0)

    def end(o):
        return 2 * (3 * (1 - o // 4)) + o % 2

    def middle(o):
        return 2 * (2 - o // 4) + o % 2

    order = arrange(
        lambda o: end(o) ^ 1, end, lambda o: middle(o) ^ 1, middle
    )
    near_order = arrange(lambda o: o ^ 3, lambda o: o ^ 2)
    rank = before(needs)
    within = jnp.arange(blocks, dtype=jnp.int32)

    def at(array, index):
        return lax.dynamic_index_in_dim(array, index, 0, keepdims=False)

    mine = lax.dynamic_index_in_dim(needs, position, 1, keepdims=False)
    mine_rank = lax.dynamic_index_in_dim(rank, position, 1, keepdims=False)
    all_flags = jnp.ones((blocks,), jnp.int32)
    lists = jnp.stack(
        [
            invert(at(mine_rank, position ^ 1), at(mine, position ^ 1), within, LANES),
            invert(at(near_order, position), all_flags, within, LANES),
            invert(at(order, position), all_flags, within, LANES),
        ]
    )

    z, y = position // 2, position % 2
    half = z // 2
    inner = (z + half) % 2
    partner_needs = at(needs, position ^ 1)
    partner_rank = at(rank, position ^ 1)
    sources = [2 * (2 - half) + y, 2 * (3 * (1 - half)) + y]
    filters = jnp.stack(
        [
            invert(at(partner_rank, s), at(partner_needs, s), at(order, s), LANES)
            for s in sources
        ]
    )
    tables = jnp.concatenate([lists, filters], axis=0)

    my_rank = at(rank, position)
    oz = owners // 2
    outer_owner = 1 - (oz + oz // 2) % 2
    same_half = owners // 4 == position // 4
    same_line = owners % 2 == y
    source_group = jnp.where(
        same_half, owners ^ position, jnp.where(same_line, 4 + outer_owner, 6 + outer_owner)
    )
    by_rank = (owners == (position ^ 1)) | (~same_half & ~same_line & (inner > 0))
    location = jnp.where(
        (owners == position)[:, None],
        within[None, :],
        jnp.where(
            by_rank[:, None], my_rank, jnp.where(same_half[:, None], near_order, order)
        ),
    )
    hit = column[:, None] == jnp.arange(SPAN * blocks, dtype=jnp.int32)[None, :]
    groups = jnp.broadcast_to(source_group[:, None], location.shape)
    packed = (groups * blocks + location).reshape(-1)
    packed = jnp.sum(jnp.where(hit, packed[None, :], 0), axis=1)
    entries = column.shape[0]
    group, key = packed // blocks, packed % blocks
    steps = jnp.arange(entries, dtype=jnp.int32)
    earlier = (group[:, None] == group[None, :]) & (steps[None, :] < steps[:, None])
    slots = group * capacity + jnp.sum(jnp.where(earlier, 1, 0), axis=1)
    slot_hit = slots[None, :] == jnp.arange(SPAN * capacity, dtype=jnp.int32)[:, None]
    jobs = jnp.sum(
        jnp.where(slot_hit, ((steps // pair_count) * blocks + key)[None, :], 0), axis=1
    )
    return (
        tables,
        (jobs // blocks).astype(jnp.int32),
        (jobs % blocks).astype(jnp.int32),
        (slots + blocks).astype(jnp.int32),
    )


def head_step(width):
    return -(-(width // HEADS + 2) // 8) * 8


def excess(readers, limits):
    rows = lax.broadcasted_iota(jnp.int32, readers[0].shape, 0)
    lanes = lax.broadcasted_iota(jnp.int32, readers[0].shape, 1)
    left = lanes < LANES // 2
    lower = rows < SPAN // 4
    large = jnp.maximum
    end = jnp.where(lower, large(readers[6], readers[7]), large(readers[0], readers[1]))
    middle = [jnp.where(lower, readers[4 + k], readers[2 + k]) for k in range(2)]
    first = large(end, jnp.where(left, middle[1], middle[0]))
    union = large(end, large(*middle))
    near = large(readers[4], readers[5])
    for row, k in ((0, 2), (1, 0), (2, 6)):
        near = jnp.where(rows == row, large(readers[k], readers[k + 1]), near)
    over = None
    for flags, limit in zip((near, end, first, union), limits):
        for part in (left, ~left):
            count = jnp.sum(jnp.where(part, flags, 0).astype(jnp.float32), axis=1, keepdims=True)
            worst = jnp.max(count, axis=0, keepdims=True) - float(limit)
            over = worst if over is None else jnp.maximum(over, worst)
    return over


def place_kernel(
    stride, limits, assignment_ref, need_ref, features_ref, placed_ref, normed_ref, needs_ref,
    over_ref, landing, flags, s_send, s_recv, g_send, g_recv,
):
    groups, _, size = assignment_ref.shape
    me = lax.axis_index("elec")
    group = lax.axis_index("groups")
    peers = lax.axis_size("elec")
    position = me // stride
    step_index = pl.program_id(0)
    teams = flags.shape[0]
    team = group * stride + lax.rem(me, stride)

    def toward(step):
        return (group, lax.rem(me + step * stride, peers))

    def across(step):
        other = lax.rem(team + step, teams)
        return (other // stride, position * stride + lax.rem(other, stride))

    def ask(step):
        return pltpu.make_async_remote_copy(
            src_ref=need_ref, dst_ref=landing.at[step],
            send_sem=s_send.at[step], recv_sem=s_recv.at[step],
            device_id=toward(step), device_id_type=MESH,
        )

    def tell(step):
        return pltpu.make_async_remote_copy(
            src_ref=flags.at[0], dst_ref=flags.at[step],
            send_sem=g_send.at[step], recv_sem=g_recv.at[step],
            device_id=across(step), device_id_type=MESH,
        )

    @pl.when(step_index == 0)
    def _():
        barrier = pltpu.get_barrier_semaphore()
        for step in range(1, SPAN):
            pl.semaphore_signal(barrier, inc=1, device_id=toward(step), device_id_type=MESH)
        for step in range(1, teams):
            pl.semaphore_signal(barrier, inc=1, device_id=across(step), device_id_type=MESH)
        pl.semaphore_wait(barrier, SPAN - 1 + teams - 1)
        for step in range(1, SPAN):
            ask(step).start()
        landing[0] = need_ref[...]

    @pl.when(step_index == pl.num_programs(0) // 2)
    def _():
        for step in range(1, SPAN):
            ask(step).wait()
        readers = [landing[lax.rem(position - q + SPAN, SPAN)] for q in range(SPAN)]
        for q in range(SPAN):
            needs_ref[q] = readers[q]
        flags[0] = jnp.broadcast_to(excess(readers, limits), flags.shape[1:])
        for step in range(1, teams):
            tell(step).start()

    lane = lax.broadcasted_iota(jnp.int32, (size, LANES), 1).astype(jnp.float32)
    for i in range(groups):
        rows = pl.ds(i * size, size)
        base = me * (features_ref.shape[0] * pl.num_programs(0)) + (
            (step_index * groups + i) * size
        )
        local = (assignment_ref[i] - base).astype(jnp.float32)
        takes = jnp.broadcast_to(local, (LANES, size)).T
        one_hot = jnp.concatenate(
            [jnp.where(takes == lane + k, 1.0, 0.0) for k in range(0, size, LANES)], axis=1
        ).astype(jnp.bfloat16)
        placed = jnp.dot(one_hot, features_ref[rows, :], preferred_element_type=jnp.float32)
        placed_ref[rows, :] = placed.astype(jnp.bfloat16)
        normed_ref[rows, :] = layer_norm(placed).astype(jnp.bfloat16)

    @pl.when(step_index == pl.num_programs(0) - 1)
    def _():
        for step in range(1, teams):
            tell(step).wait()
        worst = flags[0]
        for step in range(1, teams):
            worst = jnp.maximum(worst, flags[step])
        over_ref[...] = worst


def layer_kernel(
    capacity, limits, stride, pair_count,
    tables_ref, reader_ref, key_ref, slot_ref, blocks_ref, wq_ref, wk_ref, wv_ref,
    out_ref,
    near1, near2, near3, far0, far1, rest0, rest1, side0, side1, out_near, out_plane, out_far, out_side,
    queries, wv_turned, parts,
    n_send, n_recv, l_send, f_send, f_recv, p_send, p_recv,
):
    f32, bf16 = jnp.float32, jnp.bfloat16
    me = lax.axis_index("elec")
    group = lax.axis_index("groups")
    peers = lax.axis_size("elec")
    position = me // stride
    rest = lax.rem(me, stride)
    block_count, cluster, width = blocks_ref.shape
    head_width = width // HEADS
    cap = capacity
    z, y = position // 2, lax.rem(position, 2)
    half = z // 2
    inner = lax.rem(z + half, 2)
    pair_z = z + 1 - 2 * lax.rem(z, 2)
    pair_y = 1 - y

    def device(zz, yy):
        return (group, (2 * zz + yy) * stride + rest)

    near_devices = [device(z, pair_y), device(pair_z, y), device(pair_z, pair_y)]
    far_inner = device(2 - half, y)
    far, late, side = [far0, far1], [rest0, rest1], [side0, side1]
    near_limit, end_limit, first_limit, union_limit = limits
    part_one = (cap + 1) // 2
    part_two = cap + (end_limit - cap + 1) // 2
    bounds = [0, part_one, cap, part_two, end_limit]
    relayed = len(bounds) - 1
    for bound in (first_limit, union_limit):
        if bound > bounds[-1]:
            bounds.append(bound)
    chunks = [(a, b - a) for a, b in zip(bounds, bounds[1:])]
    last = len(chunks) - 1
    refinable = bounds.index(first_limit)
    plane_chunks = [(0, cap), (cap, near_limit - cap)]

    barrier = pltpu.get_barrier_semaphore()
    for step in range(1, SPAN):
        pl.semaphore_signal(
            barrier, inc=1, device_id=(group, lax.rem(me + step * stride, peers)),
            device_id_type=MESH,
        )
    pl.semaphore_wait(barrier, SPAN - 1)

    def gather(row, first, count, source, target, base):
        def one(k, carry):
            target[base + first + k] = source[tables_ref[row, first + k]]
            return carry

        lax.fori_loop(0, count, one, 0)

    def far_copy(s, c):
        start, count = chunks[c]
        target = far[s].at[pl.ds(start, count)]
        if c >= refinable:
            target = late[s].at[pl.ds(start - first_limit, count)]
        return pltpu.make_async_remote_copy(
            src_ref=out_far.at[pl.ds(start, count)], dst_ref=target,
            send_sem=l_send.at[c], recv_sem=f_recv.at[s, c],
            device_id=far_inner, device_id_type=MESH,
        )

    def forward_copy(s, c):
        start, count = chunks[c]
        return pltpu.make_async_remote_copy(
            src_ref=far[s].at[pl.ds(start, count)], dst_ref=far[s].at[pl.ds(start, count)],
            send_sem=f_send.at[s, c], recv_sem=f_recv.at[s, c],
            device_id=near_devices[1], device_id_type=MESH,
        )

    def side_copy(s, k, source, base):
        start, count = chunks[k]
        return pltpu.make_async_remote_copy(
            src_ref=source.at[pl.ds(base + start, count)], dst_ref=side[s].at[pl.ds(start, count)],
            send_sem=p_send.at[s, k], recv_sem=p_recv.at[s, k],
            device_id=near_devices[0], device_id_type=MESH,
        )

    def filtered(s, k):
        return side_copy(s, k, out_side, s * cap)

    def passed_on(s, k):
        return side_copy(s, k, far[s], 0)

    def near_copy():
        return pltpu.make_async_remote_copy(
            src_ref=out_near, dst_ref=near1, send_sem=n_send.at[0], recv_sem=n_recv.at[0],
            device_id=near_devices[0], device_id_type=MESH,
        )

    def plane_copy(c):
        start, count = plane_chunks[c]
        return pltpu.make_async_remote_copy(
            src_ref=out_plane.at[pl.ds(start, count)], dst_ref=near2.at[pl.ds(start, count)],
            send_sem=n_send.at[1 + c], recv_sem=n_recv.at[1 + c],
            device_id=near_devices[1], device_id_type=MESH,
        )

    def plane_pass():
        return pltpu.make_async_remote_copy(
            src_ref=near2.at[pl.ds(0, cap)], dst_ref=near3,
            send_sem=n_send.at[3], recv_sem=n_recv.at[3],
            device_id=near_devices[0], device_id_type=MESH,
        )

    def send_far(s, c):
        gather(2, chunks[c][0], chunks[c][1], blocks_ref, out_far, 0)
        far_copy(s, c).start()

    @pl.when(inner == 1)
    def _():
        for c in range(last + 1):
            send_far(0, c)

    @pl.when(inner == 0)
    def _():
        for c in range(refinable):
            send_far(1, c)

    gather(0, 0, cap, blocks_ref, out_near, 0)
    near_copy().start()
    for c in range(2):
        gather(1, plane_chunks[c][0], plane_chunks[c][1], blocks_ref, out_plane, 0)
        plane_copy(c).start()

    @pl.when(inner == 0)
    def _():
        for c in range(refinable, last + 1):
            send_far(1, c)

    lane = lax.broadcasted_iota(jnp.int32, (cluster, LANES), 1)
    per = LANES // 2 // head_width
    chosen = [
        jnp.where(lane // head_width == c, 1.0, 0.0).astype(bf16) for c in range(2 * per)
    ]
    low = lax.broadcasted_iota(jnp.int32, (head_width, LANES), 1) < cluster
    scale = math.log2(math.e) / head_width**0.5
    turned = (((1,), (1,)), ((), ()))

    def unit(size):
        row = lax.broadcasted_iota(jnp.int32, (size, size), 0)
        column = lax.broadcasted_iota(jnp.int32, (size, size), 1)
        return jnp.where(row == column, 1.0, 0.0).astype(bf16)

    wv_turned[...] = lax.dot_general(
        unit(width), wv_ref[...], turned, preferred_element_type=f32
    ).astype(bf16)

    def project(i, carry):
        rows = blocks_ref[pl.ds(i * SPAN, SPAN)].reshape(SPAN * cluster, width)
        result = jnp.dot(rows, wq_ref[...], preferred_element_type=f32) * scale
        queries[pl.ds(i * SPAN, SPAN)] = result.astype(bf16).reshape(SPAN, cluster, width)
        return carry

    lax.fori_loop(0, block_count // SPAN, project, 0)

    def several(places, query_blocks, key_blocks):
        count = len(places)
        keys = jnp.dot(
            jnp.concatenate(key_blocks, axis=0), wk_ref[...], preferred_element_type=f32
        ).astype(bf16)
        values = [
            lax.dot_general(wv_turned[...], rows, turned, preferred_element_type=f32).astype(bf16)
            for rows in key_blocks
        ]
        scores = []
        for i in range(count):
            for g in range(HEADS // per):
                band = (g // 2) * LANES
                query = query_blocks[i][:, band : band + LANES]
                stacked = jnp.concatenate(
                    [query * chosen[(g % 2) * per + c] for c in range(per)], axis=0
                )
                scores.append(
                    lax.dot_general(
                        keys[i * cluster : (i + 1) * cluster, band : band + LANES],
                        stacked, turned, preferred_element_type=f32,
                    )
                )
        weights = []
        for i in range(count):
            for g in range(HEADS // per):
                score = scores[i * (HEADS // per) + g]
                columns = pl.ds(g * per * cluster, per * cluster)
                top = jnp.max(score, axis=0, keepdims=True)
                weight = jnp.exp2(score - top)
                parts[places[i], head_width : head_width + 1, columns] = top
                parts[places[i], head_width + 1 : head_width + 2, columns] = jnp.sum(
                    weight, axis=0, keepdims=True
                )
                weights.append(weight.astype(bf16))
        for i in range(count):
            for g in range(HEADS // per):
                rows = per * head_width
                result = jnp.dot(
                    values[i][g * rows : (g + 1) * rows], weights[i * (HEADS // per) + g],
                    preferred_element_type=f32,
                )
                for k in range(per // 2):
                    top = 2 * k * head_width
                    lanes = slice(k * LANES, (k + 1) * LANES)
                    first = (g * per // 2 + k) * LANES
                    parts[places[i], 0:head_width, pl.ds(first, LANES)] = jnp.where(
                        low,
                        result[top : top + head_width, lanes],
                        result[top + head_width : top + 2 * head_width, lanes],
                    )

    def own_blocks(first, count, batch):
        def one(i, carry):
            index = [first + i * batch + k for k in range(batch)]
            several(index, [queries[j] for j in index], [blocks_ref[j] for j in index])
            return carry

        lax.fori_loop(0, count // batch, one, 0)

    def listed(which, source):
        batch = 5 if cap % 5 == 0 else 1

        def one(i, carry):
            index = [which * cap + i * batch + k for k in range(batch)]
            several(
                [block_count + j for j in index],
                [queries[reader_ref[j]] for j in index],
                [source[key_ref[j]] for j in index],
            )
            return carry

        lax.fori_loop(0, cap // batch, one, 0)

    def on_inner(work):
        pl.when(inner == 1)(work)

    def on_outer(work):
        pl.when(inner == 0)(work)

    def relay(s, c):
        far_copy(s, c).wait_recv()
        forward_copy(s, c).start()

    def refine(s):
        arrived(s, relayed, refinable)
        gather(3 + s, 0, cap, far[s], out_side, s * cap)
        for k in range(2):
            filtered(s, k).start()

    def pass_on(s, k):
        far_copy(s, k).wait_recv()
        passed_on(s, k).start()

    def arrived(s, first, stop):
        for c in range(first, stop):
            far_copy(s, c).wait_recv()

    def late_arrived(s):
        arrived(s, refinable, last + 1)
        for k in range(union_limit - first_limit):
            far[s][first_limit + k] = late[s][k]

    def side_arrived(s):
        for k in range(2):
            filtered(s, k).wait_recv()

    eighth = block_count // 8
    own_blocks(0, 3 * eighth, 4)
    on_inner(lambda: relay(1, 0))
    own_blocks(3 * eighth, 3 * eighth, 4)
    on_inner(lambda: relay(1, 1))
    own_blocks(6 * eighth, 2 * eighth, 4)
    on_inner(lambda: relay(1, 2))
    listed(0, blocks_ref)
    on_inner(lambda: relay(1, 3))
    near_copy().wait_recv()
    listed(1, near1)

    @pl.when(inner == 1)
    def _():
        refine(1)
        relay(0, 0)
        plane_copy(0).wait_recv()
        plane_pass().start()
        relay(0, 1)
        side_arrived(1)
        listed(7, side1)
        relay(0, 2)
        plane_copy(1).wait_recv()
        relay(0, 3)
        listed(2, near2)
        refine(0)
        late_arrived(1)
        listed(5, far1)
        plane_pass().wait_recv()
        listed(3, near3)
        late_arrived(0)
        listed(4, far0)
        side_arrived(0)
        listed(6, side0)

    @pl.when(inner == 0)
    def _():
        plane_copy(0).wait_recv()
        plane_pass().start()
        pass_on(1, 0)
        pass_on(1, 1)
        plane_copy(1).wait_recv()
        listed(2, near2)
        plane_pass().wait_recv()
        listed(3, near3)
        arrived(1, 2, relayed)
        listed(5, far1)
        side_arrived(1)
        listed(7, side1)
        pass_on(0, 0)
        pass_on(0, 1)
        side_arrived(0)
        listed(6, side0)
        arrived(0, 2, relayed)
        listed(4, far0)

    def combine(i, carry):
        for k in range(SPAN):
            j = i * SPAN + k
            places = [j] + [slot_ref[j * pair_count + p] for p in range(pair_count)]
            tops = [parts[a, head_width : head_width + 1, :] for a in places]
            sums = [parts[a, head_width + 1 : head_width + 2, :] for a in places]
            top = functools.reduce(jnp.maximum, tops)
            factors = [jnp.exp2(t - top) for t in tops]
            total = sum(f * s for f, s in zip(factors, sums))
            inverse = 1.0 / total
            merged = sum(
                parts[a, 0:head_width, :] * (f * inverse) for a, f in zip(places, factors)
            ).astype(bf16)
            stacked = jnp.concatenate(
                [merged[:, c : c + LANES] for c in range(0, HEADS * cluster, LANES)], axis=0
            )
            upright = lax.dot_general(
                unit(LANES), stacked, turned, preferred_element_type=f32
            ).astype(bf16)
            rows = pl.ds(pl.multiple_of(j * cluster, cluster), cluster)
            out_ref[rows, 0:LANES] = upright[0:cluster]
            out_ref[rows, LANES : 2 * LANES] = upright[cluster : 2 * cluster]
        return carry

    lax.fori_loop(0, block_count // SPAN, combine, 0)

    @pl.when(inner == 1)
    def _():
        for s in range(2):
            for c in range(relayed):
                forward_copy(s, c).wait_send()
            for k in range(2):
                filtered(s, k).wait_send()

    @pl.when(inner == 0)
    def _():
        for s in range(2):
            for k in range(2):
                passed_on(s, k).wait_send()

    for c in range(last + 1):
        far_copy(0, c).wait_send()
    near_copy().wait_send()
    for c in range(2):
        plane_copy(c).wait_send()
    plane_pass().wait_send()


def finish_kernel(placed_ref, attended_ref, wo_ref, wm_ref, out_ref, wo_sorted):
    f32, bf16 = jnp.float32, jnp.bfloat16
    width = wo_ref.shape[0]
    head_width = width // HEADS

    @pl.when(pl.program_id(0) == 0)
    def _():
        for h in range(HEADS):
            start = (h % 2) * (width // 2) + (h // 2) * head_width
            wo_sorted[start : start + head_width, :] = wo_ref[
                h * head_width : (h + 1) * head_width, :
            ]

    projected = jnp.dot(attended_ref[...], wo_sorted[...], preferred_element_type=f32)
    middle = (placed_ref[...].astype(f32) + projected).astype(bf16).astype(f32)
    second = layer_norm(middle).astype(bf16)
    mixed = middle + jnp.tanh(jnp.dot(second, wm_ref[...], preferred_element_type=f32))
    out_ref[...] = mixed.astype(bf16)


def body(features, assignment, pairs, w_query, w_key, w_value, w_out, w_mix):
    rows_dev, width = features.shape
    block_count, pair_count = pairs.shape
    cluster = rows_dev // block_count
    capacity = (block_count * pair_count + SPAN - 1) // SPAN + 1
    stride = lax.axis_size("elec") // SPAN
    position = lax.axis_index("elec") // stride
    group_rows = SPAN * cluster
    groups = rows_dev // group_rows
    bf16 = jnp.bfloat16

    column, need = own_needs(pairs, block_count, stride)
    need_rows = SPAN * block_count // LANES
    batch = math.gcd(groups, 2)
    tile = pl.BlockSpec((batch * group_rows, width), lambda i: (i, 0))
    full = (2 * capacity, 2 * capacity, block_count, block_count)
    small = (capacity + 18, capacity + 18, capacity + 27, capacity + 34)
    limits = tuple(min(a, b) for a, b in zip(small, full))
    teams = lax.axis_size("groups") * stride
    placed, normed, needs, over = pl.pallas_call(
        functools.partial(place_kernel, stride, limits),
        grid=(groups // batch,),
        in_specs=[
            pl.BlockSpec((batch, 1, group_rows), lambda i: (i, 0, 0)),
            pl.BlockSpec((need_rows, LANES), lambda i: (0, 0)),
            tile,
        ],
        out_specs=[
            tile,
            tile,
            pl.BlockSpec((SPAN, need_rows, LANES), lambda i: (0, 0, 0)),
            pl.BlockSpec((8, LANES), lambda i: (0, 0)),
        ],
        out_shape=[jax.ShapeDtypeStruct((rows_dev, width), bf16)] * 2
        + [
            jax.ShapeDtypeStruct((SPAN, need_rows, LANES), jnp.int32),
            jax.ShapeDtypeStruct((8, LANES), jnp.float32),
        ],
        scratch_shapes=[
            pltpu.VMEM((SPAN, need_rows, LANES), jnp.int32),
            pltpu.VMEM((teams, 8, LANES), jnp.float32),
            pltpu.SemaphoreType.DMA((SPAN,)),
            pltpu.SemaphoreType.DMA((SPAN,)),
            pltpu.SemaphoreType.DMA((teams,)),
            pltpu.SemaphoreType.DMA((teams,)),
        ],
        compiler_params=pltpu.CompilerParams(collective_id=1, has_side_effects=True),
    )(
        assignment.reshape(groups, 1, group_rows), need.reshape(need_rows, LANES), features
    )

    tables, reader, key, slot = make_plan(
        needs.reshape(SPAN, SPAN, block_count), column, position, capacity, pair_count
    )
    block = (cluster, width)
    part = (head_step(width), HEADS * cluster)
    in_smem = pl.BlockSpec(memory_space=pltpu.SMEM)
    in_vmem = pl.BlockSpec(memory_space=pltpu.VMEM)

    def layer(which, sizes):
        near_limit, end_limit, first_limit, union_limit = sizes
        steps = 4 + len({end_limit, first_limit, union_limit}) - 1
        buffers = [
            capacity, near_limit, capacity, union_limit, union_limit,
            max(union_limit - first_limit, 1), max(union_limit - first_limit, 1),
            capacity, capacity,
            capacity, near_limit, union_limit, 2 * capacity, block_count,
        ]
        return pl.pallas_call(
            functools.partial(layer_kernel, capacity, sizes, stride, pair_count),
            in_specs=[in_smem] * 4 + [in_vmem] * 4,
            out_specs=in_vmem,
            out_shape=jax.ShapeDtypeStruct((rows_dev, width), bf16),
            scratch_shapes=[pltpu.VMEM((count,) + block, bf16) for count in buffers]
            + [
                pltpu.VMEM((width, width), bf16),
                pltpu.VMEM((block_count + SPAN * capacity,) + part, jnp.float32),
                pltpu.SemaphoreType.DMA((4,)),
                pltpu.SemaphoreType.DMA((4,)),
                pltpu.SemaphoreType.DMA((steps,)),
                pltpu.SemaphoreType.DMA((2, 4)),
                pltpu.SemaphoreType.DMA((2, steps)),
                pltpu.SemaphoreType.DMA((2, 2)),
                pltpu.SemaphoreType.DMA((2, 2)),
            ],
            compiler_params=pltpu.CompilerParams(
                collective_id=which, has_side_effects=True, vmem_limit_bytes=60 * 2**20
            ),
        )

    attended = lax.cond(
        over[0, 0] <= 0.0, layer(0, limits), layer(2, full),
        tables, reader, key, slot, normed.reshape(block_count, cluster, width),
        w_query, w_key, w_value,
    )
    tile = pl.BlockSpec((group_rows, width), lambda i: (i, 0))
    weight = pl.BlockSpec((width, width), lambda i: (0, 0))
    return pl.pallas_call(
        finish_kernel,
        grid=(groups,),
        in_specs=[tile, tile, weight, weight],
        out_specs=tile,
        out_shape=jax.ShapeDtypeStruct((rows_dev, width), bf16),
        scratch_shapes=[pltpu.VMEM((width, width), bf16)],
    )(placed, attended, w_out, w_mix)


def solution(mesh):
    placed = (
        P(("groups", "elec"), None),
        P(("groups", "elec")),
        P(("groups", "elec"), None),
        P(),
        P(),
        P(),
        P(),
        P(),
    )
    return jax.shard_map(
        body, mesh=mesh, in_specs=placed, out_specs=P(("groups", "elec"), None), check_vma=False
    )
```

```python
import functools
import math

import jax
import jax.numpy as jnp
from jax import lax
from jax.experimental import pallas as pl
from jax.experimental.pallas import tpu as pltpu
from jax.sharding import PartitionSpec as P

HEADS = 16
SPAN = 8
LANES = 128
MESH = pl.DeviceIdType.MESH


def layer_norm(rows):
    mean = jnp.mean(rows, axis=-1, keepdims=True)
    centred = rows - mean
    variance = jnp.mean(centred * centred, axis=-1, keepdims=True)
    return centred * lax.rsqrt(variance + 1e-05)


def own_needs(listed, block_count, stride):
    flat = listed.reshape(-1)
    column = (flat // block_count // stride) * block_count + flat % block_count
    columns = jnp.arange(SPAN * block_count, dtype=jnp.int32)
    hit = column[None, :] == columns[:, None]
    return column, jnp.max(jnp.where(hit, 1, 0), axis=1).astype(jnp.int32)


def before(flags):
    size = flags.shape[-1]
    lower = (jnp.arange(size)[:, None] < jnp.arange(size)[None, :]).astype(jnp.bfloat16)
    counts = jnp.dot(
        flags.reshape(-1, size).astype(jnp.bfloat16), lower, preferred_element_type=jnp.float32
    )
    return counts.reshape(flags.shape).astype(jnp.int32)


def invert(place, flags, values, size):
    hit = (place[..., None, :] == jnp.arange(size, dtype=jnp.int32)[:, None]) & (
        flags[..., None, :] > 0
    )
    return jnp.sum(jnp.where(hit, values[..., None, :], 0), axis=-1).astype(jnp.int32)


def make_plan(needs, column, position, capacity, pair_count):
    blocks = needs.shape[-1]
    owners = jnp.arange(SPAN, dtype=jnp.int32)
    static = list(range(SPAN))

    def arrange(*readers):
        flags, left = [], jnp.ones((SPAN, blocks), jnp.int32)
        for chosen in readers:
            flags.append(jnp.stack([needs[chosen(o), o] for o in static]) * left)
            left = left - flags[-1]
        flags = jnp.stack(flags + [left])
        counts = jnp.sum(flags, axis=-1, keepdims=True)
        start = jnp.cumsum(counts, axis=0) - counts
        return jnp.sum(flags * (before(flags) + start), axis=0)

    def end(o):
        return 2 * (3 * (1 - o // 4)) + o % 2

    def middle(o):
        return 2 * (2 - o // 4) + o % 2

    order = arrange(
        lambda o: end(o) ^ 1, end, lambda o: middle(o) ^ 1, middle
    )
    near_order = arrange(lambda o: o ^ 3, lambda o: o ^ 2)
    rank = before(needs)
    within = jnp.arange(blocks, dtype=jnp.int32)

    def at(array, index):
        return lax.dynamic_index_in_dim(array, index, 0, keepdims=False)

    mine = lax.dynamic_index_in_dim(needs, position, 1, keepdims=False)
    mine_rank = lax.dynamic_index_in_dim(rank, position, 1, keepdims=False)
    all_flags = jnp.ones((blocks,), jnp.int32)
    lists = jnp.stack(
        [
            invert(at(mine_rank, position ^ 1), at(mine, position ^ 1), within, LANES),
            invert(at(near_order, position), all_flags, within, LANES),
            invert(at(order, position), all_flags, within, LANES),
        ]
    )

    z, y = position // 2, position % 2
    half = z // 2
    inner = (z + half) % 2
    partner_needs = at(needs, position ^ 1)
    partner_rank = at(rank, position ^ 1)
    sources = [2 * (2 - half) + y, 2 * (3 * (1 - half)) + y]
    filters = jnp.stack(
        [
            invert(at(partner_rank, s), at(partner_needs, s), at(order, s), LANES)
            for s in sources
        ]
    )
    tables = jnp.concatenate([lists, filters], axis=0)

    my_rank = at(rank, position)
    oz = owners // 2
    outer_owner = 1 - (oz + oz // 2) % 2
    same_half = owners // 4 == position // 4
    same_line = owners % 2 == y
    source_group = jnp.where(
        same_half, owners ^ position, jnp.where(same_line, 4 + outer_owner, 6 + outer_owner)
    )
    by_rank = (owners == (position ^ 1)) | (~same_half & ~same_line & (inner > 0))
    location = jnp.where(
        (owners == position)[:, None],
        within[None, :],
        jnp.where(
            by_rank[:, None], my_rank, jnp.where(same_half[:, None], near_order, order)
        ),
    )
    hit = column[:, None] == jnp.arange(SPAN * blocks, dtype=jnp.int32)[None, :]
    groups = jnp.broadcast_to(source_group[:, None], location.shape)
    packed = (groups * blocks + location).reshape(-1)
    packed = jnp.sum(jnp.where(hit, packed[None, :], 0), axis=1)
    entries = column.shape[0]
    group, key = packed // blocks, packed % blocks
    steps = jnp.arange(entries, dtype=jnp.int32)
    earlier = (group[:, None] == group[None, :]) & (steps[None, :] < steps[:, None])
    slots = group * capacity + jnp.sum(jnp.where(earlier, 1, 0), axis=1)
    slot_hit = slots[None, :] == jnp.arange(SPAN * capacity, dtype=jnp.int32)[:, None]
    jobs = jnp.sum(
        jnp.where(slot_hit, ((steps // pair_count) * blocks + key)[None, :], 0), axis=1
    )
    return (
        tables,
        (jobs // blocks).astype(jnp.int32),
        (jobs % blocks).astype(jnp.int32),
        (slots + blocks).astype(jnp.int32),
    )


def head_step(width):
    return -(-(width // HEADS + 2) // 8) * 8


def excess(readers, limits):
    rows = lax.broadcasted_iota(jnp.int32, readers[0].shape, 0)
    lanes = lax.broadcasted_iota(jnp.int32, readers[0].shape, 1)
    left = lanes < LANES // 2
    lower = rows < SPAN // 4
    large = jnp.maximum
    end = jnp.where(lower, large(readers[6], readers[7]), large(readers[0], readers[1]))
    middle = [jnp.where(lower, readers[4 + k], readers[2 + k]) for k in range(2)]
    first = large(end, jnp.where(left, middle[1], middle[0]))
    union = large(end, large(*middle))
    near = large(readers[4], readers[5])
    for row, k in ((0, 2), (1, 0), (2, 6)):
        near = jnp.where(rows == row, large(readers[k], readers[k + 1]), near)
    over = None
    for flags, limit in zip((near, end, first, union), limits):
        for part in (left, ~left):
            count = jnp.sum(jnp.where(part, flags, 0).astype(jnp.float32), axis=1, keepdims=True)
            worst = jnp.max(count, axis=0, keepdims=True) - float(limit)
            over = worst if over is None else jnp.maximum(over, worst)
    return over


def place_kernel(
    stride, limits, assignment_ref, need_ref, features_ref, placed_ref, normed_ref, needs_ref,
    over_ref, landing, flags, s_send, s_recv, g_send, g_recv,
):
    groups, _, size = assignment_ref.shape
    me = lax.axis_index("elec")
    group = lax.axis_index("groups")
    peers = lax.axis_size("elec")
    position = me // stride
    step_index = pl.program_id(0)
    teams = flags.shape[0]
    team = group * stride + lax.rem(me, stride)

    def toward(step):
        return (group, lax.rem(me + step * stride, peers))

    def across(step):
        other = lax.rem(team + step, teams)
        return (other // stride, position * stride + lax.rem(other, stride))

    def ask(step):
        return pltpu.make_async_remote_copy(
            src_ref=need_ref, dst_ref=landing.at[step],
            send_sem=s_send.at[step], recv_sem=s_recv.at[step],
            device_id=toward(step), device_id_type=MESH,
        )

    def tell(step):
        return pltpu.make_async_remote_copy(
            src_ref=flags.at[0], dst_ref=flags.at[step],
            send_sem=g_send.at[step], recv_sem=g_recv.at[step],
            device_id=across(step), device_id_type=MESH,
        )

    @pl.when(step_index == 0)
    def _():
        barrier = pltpu.get_barrier_semaphore()
        for step in range(1, SPAN):
            pl.semaphore_signal(barrier, inc=1, device_id=toward(step), device_id_type=MESH)
        for step in range(1, teams):
            pl.semaphore_signal(barrier, inc=1, device_id=across(step), device_id_type=MESH)
        pl.semaphore_wait(barrier, SPAN - 1 + teams - 1)
        for step in range(1, SPAN):
            ask(step).start()
        landing[0] = need_ref[...]

    @pl.when(step_index == pl.num_programs(0) - 1)
    def _():
        for step in range(1, SPAN):
            ask(step).wait()
        readers = [landing[lax.rem(position - q + SPAN, SPAN)] for q in range(SPAN)]
        for q in range(SPAN):
            needs_ref[q] = readers[q]
        flags[0] = jnp.broadcast_to(excess(readers, limits), flags.shape[1:])
        for step in range(1, teams):
            tell(step).start()

    lane = lax.broadcasted_iota(jnp.int32, (size, LANES), 1).astype(jnp.float32)
    for i in range(groups):
        rows = pl.ds(i * size, size)
        base = me * (features_ref.shape[0] * pl.num_programs(0)) + (
            (step_index * groups + i) * size
        )
        local = (assignment_ref[i] - base).astype(jnp.float32)
        takes = jnp.broadcast_to(local, (LANES, size)).T
        one_hot = jnp.concatenate(
            [jnp.where(takes == lane + k, 1.0, 0.0) for k in range(0, size, LANES)], axis=1
        ).astype(jnp.bfloat16)
        placed = jnp.dot(one_hot, features_ref[rows, :], preferred_element_type=jnp.float32)
        placed_ref[rows, :] = placed.astype(jnp.bfloat16)
        normed_ref[rows, :] = layer_norm(placed).astype(jnp.bfloat16)

    @pl.when(step_index == pl.num_programs(0) - 1)
    def _():
        for step in range(1, teams):
            tell(step).wait()
        worst = flags[0]
        for step in range(1, teams):
            worst = jnp.maximum(worst, flags[step])
        over_ref[0, 0] = jnp.max(worst)


def layer_kernel(
    capacity, limits, stride, pair_count,
    tables_ref, reader_ref, key_ref, slot_ref, blocks_ref, wq_ref, wk_ref, wv_ref,
    out_ref,
    near1, near2, near3, far0, far1, rest0, rest1, side0, side1, out_near, out_plane, out_far, out_side,
    queries, wv_turned, parts,
    n_send, n_recv, l_send, f_send, f_recv, p_send, p_recv,
):
    f32, bf16 = jnp.float32, jnp.bfloat16
    me = lax.axis_index("elec")
    group = lax.axis_index("groups")
    peers = lax.axis_size("elec")
    position = me // stride
    rest = lax.rem(me, stride)
    block_count, cluster, width = blocks_ref.shape
    head_width = width // HEADS
    cap = capacity
    z, y = position // 2, lax.rem(position, 2)
    half = z // 2
    inner = lax.rem(z + half, 2)
    pair_z = z + 1 - 2 * lax.rem(z, 2)
    pair_y = 1 - y

    def device(zz, yy):
        return (group, (2 * zz + yy) * stride + rest)

    near_devices = [device(z, pair_y), device(pair_z, y), device(pair_z, pair_y)]
    far_inner = device(2 - half, y)
    far, late, side = [far0, far1], [rest0, rest1], [side0, side1]
    near_limit, end_limit, first_limit, union_limit = limits
    part_one = (cap + 1) // 2
    part_two = cap + (end_limit - cap + 1) // 2
    bounds = [0, part_one, cap, part_two, end_limit]
    relayed = len(bounds) - 1
    for bound in (first_limit, union_limit):
        if bound > bounds[-1]:
            bounds.append(bound)
    chunks = [(a, b - a) for a, b in zip(bounds, bounds[1:])]
    last = len(chunks) - 1
    refinable = bounds.index(first_limit)
    plane_chunks = [(0, cap), (cap, near_limit - cap)]

    barrier = pltpu.get_barrier_semaphore()
    for step in range(1, SPAN):
        pl.semaphore_signal(
            barrier, inc=1, device_id=(group, lax.rem(me + step * stride, peers)),
            device_id_type=MESH,
        )
    pl.semaphore_wait(barrier, SPAN - 1)

    def gather(row, first, count, source, target, base):
        def one(k, carry):
            target[base + first + k] = source[tables_ref[row, first + k]]
            return carry

        lax.fori_loop(0, count, one, 0)

    def far_copy(s, c):
        start, count = chunks[c]
        target = far[s].at[pl.ds(start, count)]
        if c >= refinable:
            target = late[s].at[pl.ds(start - first_limit, count)]
        return pltpu.make_async_remote_copy(
            src_ref=out_far.at[pl.ds(start, count)], dst_ref=target,
            send_sem=l_send.at[c], recv_sem=f_recv.at[s, c],
            device_id=far_inner, device_id_type=MESH,
        )

    def forward_copy(s, c):
        start, count = chunks[c]
        return pltpu.make_async_remote_copy(
            src_ref=far[s].at[pl.ds(start, count)], dst_ref=far[s].at[pl.ds(start, count)],
            send_sem=f_send.at[s, c], recv_sem=f_recv.at[s, c],
            device_id=near_devices[1], device_id_type=MESH,
        )

    def side_copy(s, k, source, base):
        start, count = chunks[k]
        return pltpu.make_async_remote_copy(
            src_ref=source.at[pl.ds(base + start, count)], dst_ref=side[s].at[pl.ds(start, count)],
            send_sem=p_send.at[s, k], recv_sem=p_recv.at[s, k],
            device_id=near_devices[0], device_id_type=MESH,
        )

    def filtered(s, k):
        return side_copy(s, k, out_side, s * cap)

    def passed_on(s, k):
        return side_copy(s, k, far[s], 0)

    def near_copy():
        return pltpu.make_async_remote_copy(
            src_ref=out_near, dst_ref=near1, send_sem=n_send.at[0], recv_sem=n_recv.at[0],
            device_id=near_devices[0], device_id_type=MESH,
        )

    def plane_copy(c):
        start, count = plane_chunks[c]
        return pltpu.make_async_remote_copy(
            src_ref=out_plane.at[pl.ds(start, count)], dst_ref=near2.at[pl.ds(start, count)],
            send_sem=n_send.at[1 + c], recv_sem=n_recv.at[1 + c],
            device_id=near_devices[1], device_id_type=MESH,
        )

    def plane_pass():
        return pltpu.make_async_remote_copy(
            src_ref=near2.at[pl.ds(0, cap)], dst_ref=near3,
            send_sem=n_send.at[3], recv_sem=n_recv.at[3],
            device_id=near_devices[0], device_id_type=MESH,
        )

    def send_far(s, c):
        gather(2, chunks[c][0], chunks[c][1], blocks_ref, out_far, 0)
        far_copy(s, c).start()

    @pl.when(inner == 1)
    def _():
        for c in range(last + 1):
            send_far(0, c)

    @pl.when(inner == 0)
    def _():
        for c in range(refinable):
            send_far(1, c)

    gather(0, 0, cap, blocks_ref, out_near, 0)
    near_copy().start()
    for c in range(2):
        gather(1, plane_chunks[c][0], plane_chunks[c][1], blocks_ref, out_plane, 0)
        plane_copy(c).start()

    @pl.when(inner == 0)
    def _():
        for c in range(refinable, last + 1):
            send_far(1, c)

    lane = lax.broadcasted_iota(jnp.int32, (cluster, LANES), 1)
    per = LANES // 2 // head_width
    chosen = [
        jnp.where(lane // head_width == c, 1.0, 0.0).astype(bf16) for c in range(2 * per)
    ]
    low = lax.broadcasted_iota(jnp.int32, (head_width, LANES), 1) < cluster
    scale = math.log2(math.e) / head_width**0.5
    turned = (((1,), (1,)), ((), ()))

    def unit(size):
        row = lax.broadcasted_iota(jnp.int32, (size, size), 0)
        column = lax.broadcasted_iota(jnp.int32, (size, size), 1)
        return jnp.where(row == column, 1.0, 0.0).astype(bf16)

    wv_turned[...] = lax.dot_general(
        unit(width), wv_ref[...], turned, preferred_element_type=f32
    ).astype(bf16)

    def project(i, carry):
        rows = blocks_ref[pl.ds(i * SPAN, SPAN)].reshape(SPAN * cluster, width)
        result = jnp.dot(rows, wq_ref[...], preferred_element_type=f32) * scale
        queries[pl.ds(i * SPAN, SPAN)] = result.astype(bf16).reshape(SPAN, cluster, width)
        return carry

    lax.fori_loop(0, block_count // SPAN, project, 0)

    def several(places, query_blocks, key_blocks):
        count = len(places)
        keys = jnp.dot(
            jnp.concatenate(key_blocks, axis=0), wk_ref[...], preferred_element_type=f32
        ).astype(bf16)
        values = [
            lax.dot_general(wv_turned[...], rows, turned, preferred_element_type=f32).astype(bf16)
            for rows in key_blocks
        ]
        scores = []
        for i in range(count):
            for g in range(HEADS // per):
                band = (g // 2) * LANES
                query = query_blocks[i][:, band : band + LANES]
                stacked = jnp.concatenate(
                    [query * chosen[(g % 2) * per + c] for c in range(per)], axis=0
                )
                scores.append(
                    lax.dot_general(
                        keys[i * cluster : (i + 1) * cluster, band : band + LANES],
                        stacked, turned, preferred_element_type=f32,
                    )
                )
        weights = []
        for i in range(count):
            for g in range(HEADS // per):
                score = scores[i * (HEADS // per) + g]
                columns = pl.ds(g * per * cluster, per * cluster)
                top = jnp.max(score, axis=0, keepdims=True)
                weight = jnp.exp2(score - top)
                parts[places[i], head_width : head_width + 1, columns] = top
                parts[places[i], head_width + 1 : head_width + 2, columns] = jnp.sum(
                    weight, axis=0, keepdims=True
                )
                weights.append(weight.astype(bf16))
        for i in range(count):
            for g in range(HEADS // per):
                rows = per * head_width
                result = jnp.dot(
                    values[i][g * rows : (g + 1) * rows], weights[i * (HEADS // per) + g],
                    preferred_element_type=f32,
                )
                for k in range(per // 2):
                    top = 2 * k * head_width
                    lanes = slice(k * LANES, (k + 1) * LANES)
                    first = (g * per // 2 + k) * LANES
                    parts[places[i], 0:head_width, pl.ds(first, LANES)] = jnp.where(
                        low,
                        result[top : top + head_width, lanes],
                        result[top + head_width : top + 2 * head_width, lanes],
                    )

    def own_blocks(first, count, batch):
        def one(i, carry):
            index = [first + i * batch + k for k in range(batch)]
            several(index, [queries[j] for j in index], [blocks_ref[j] for j in index])
            return carry

        lax.fori_loop(0, count // batch, one, 0)

    def listed(which, source):
        batch = 5 if cap % 5 == 0 else 1

        def one(i, carry):
            index = [which * cap + i * batch + k for k in range(batch)]
            several(
                [block_count + j for j in index],
                [queries[reader_ref[j]] for j in index],
                [source[key_ref[j]] for j in index],
            )
            return carry

        lax.fori_loop(0, cap // batch, one, 0)

    def on_inner(work):
        pl.when(inner == 1)(work)

    def on_outer(work):
        pl.when(inner == 0)(work)

    def relay(s, c):
        far_copy(s, c).wait_recv()
        forward_copy(s, c).start()

    def refine(s):
        arrived(s, relayed, refinable)
        gather(3 + s, 0, cap, far[s], out_side, s * cap)
        for k in range(2):
            filtered(s, k).start()

    def pass_on(s, k):
        far_copy(s, k).wait_recv()
        passed_on(s, k).start()

    def arrived(s, first, stop):
        for c in range(first, stop):
            far_copy(s, c).wait_recv()

    def late_arrived(s):
        arrived(s, refinable, last + 1)
        for k in range(union_limit - first_limit):
            far[s][first_limit + k] = late[s][k]

    def side_arrived(s):
        for k in range(2):
            filtered(s, k).wait_recv()

    eighth = block_count // 8
    own_blocks(0, 3 * eighth, 4)
    on_inner(lambda: relay(1, 0))
    own_blocks(3 * eighth, 3 * eighth, 4)
    on_inner(lambda: relay(1, 1))
    own_blocks(6 * eighth, 2 * eighth, 4)
    on_inner(lambda: relay(1, 2))
    listed(0, blocks_ref)
    on_inner(lambda: relay(1, 3))
    near_copy().wait_recv()
    listed(1, near1)

    @pl.when(inner == 1)
    def _():
        refine(1)
        relay(0, 0)
        plane_copy(0).wait_recv()
        plane_pass().start()
        relay(0, 1)
        side_arrived(1)
        listed(7, side1)
        relay(0, 2)
        plane_copy(1).wait_recv()
        relay(0, 3)
        listed(2, near2)
        refine(0)
        late_arrived(1)
        listed(5, far1)
        plane_pass().wait_recv()
        listed(3, near3)
        late_arrived(0)
        listed(4, far0)
        side_arrived(0)
        listed(6, side0)

    @pl.when(inner == 0)
    def _():
        plane_copy(0).wait_recv()
        plane_pass().start()
        pass_on(1, 0)
        pass_on(1, 1)
        plane_copy(1).wait_recv()
        listed(2, near2)
        plane_pass().wait_recv()
        listed(3, near3)
        arrived(1, 2, relayed)
        listed(5, far1)
        side_arrived(1)
        listed(7, side1)
        pass_on(0, 0)
        pass_on(0, 1)
        side_arrived(0)
        listed(6, side0)
        arrived(0, 2, relayed)
        listed(4, far0)

    def combine(i, carry):
        for k in range(SPAN):
            j = i * SPAN + k
            places = [j] + [slot_ref[j * pair_count + p] for p in range(pair_count)]
            tops = [parts[a, head_width : head_width + 1, :] for a in places]
            sums = [parts[a, head_width + 1 : head_width + 2, :] for a in places]
            top = functools.reduce(jnp.maximum, tops)
            factors = [jnp.exp2(t - top) for t in tops]
            total = sum(f * s for f, s in zip(factors, sums))
            inverse = 1.0 / total
            merged = sum(
                parts[a, 0:head_width, :] * (f * inverse) for a, f in zip(places, factors)
            ).astype(bf16)
            stacked = jnp.concatenate(
                [merged[:, c : c + LANES] for c in range(0, HEADS * cluster, LANES)], axis=0
            )
            upright = lax.dot_general(
                unit(LANES), stacked, turned, preferred_element_type=f32
            ).astype(bf16)
            rows = pl.ds(pl.multiple_of(j * cluster, cluster), cluster)
            out_ref[rows, 0:LANES] = upright[0:cluster]
            out_ref[rows, LANES : 2 * LANES] = upright[cluster : 2 * cluster]
        return carry

    lax.fori_loop(0, block_count // SPAN, combine, 0)

    @pl.when(inner == 1)
    def _():
        for s in range(2):
            for c in range(relayed):
                forward_copy(s, c).wait_send()
            for k in range(2):
                filtered(s, k).wait_send()

    @pl.when(inner == 0)
    def _():
        for s in range(2):
            for k in range(2):
                passed_on(s, k).wait_send()

    for c in range(last + 1):
        far_copy(0, c).wait_send()
    near_copy().wait_send()
    for c in range(2):
        plane_copy(c).wait_send()
    plane_pass().wait_send()


def finish_kernel(placed_ref, attended_ref, wo_ref, wm_ref, out_ref, wo_sorted):
    f32, bf16 = jnp.float32, jnp.bfloat16
    width = wo_ref.shape[0]
    head_width = width // HEADS

    @pl.when(pl.program_id(0) == 0)
    def _():
        for h in range(HEADS):
            start = (h % 2) * (width // 2) + (h // 2) * head_width
            wo_sorted[start : start + head_width, :] = wo_ref[
                h * head_width : (h + 1) * head_width, :
            ]

    projected = jnp.dot(attended_ref[...], wo_sorted[...], preferred_element_type=f32)
    middle = (placed_ref[...].astype(f32) + projected).astype(bf16).astype(f32)
    second = layer_norm(middle).astype(bf16)
    mixed = middle + jnp.tanh(jnp.dot(second, wm_ref[...], preferred_element_type=f32))
    out_ref[...] = mixed.astype(bf16)


def body(features, assignment, pairs, w_query, w_key, w_value, w_out, w_mix):
    rows_dev, width = features.shape
    block_count, pair_count = pairs.shape
    cluster = rows_dev // block_count
    capacity = (block_count * pair_count + SPAN - 1) // SPAN + 1
    stride = lax.axis_size("elec") // SPAN
    position = lax.axis_index("elec") // stride
    group_rows = SPAN * cluster
    groups = rows_dev // group_rows
    bf16 = jnp.bfloat16

    column, need = own_needs(pairs, block_count, stride)
    need_rows = SPAN * block_count // LANES
    batch = math.gcd(groups, 2)
    tile = pl.BlockSpec((batch * group_rows, width), lambda i: (i, 0))
    full = (2 * capacity, 2 * capacity, block_count, block_count)
    small = (capacity + 18, capacity + 18, capacity + 27, capacity + 34)
    limits = tuple(min(a, b) for a, b in zip(small, full))
    teams = lax.axis_size("groups") * stride
    placed, normed, needs, over = pl.pallas_call(
        functools.partial(place_kernel, stride, limits),
        grid=(groups // batch,),
        in_specs=[
            pl.BlockSpec((batch, 1, group_rows), lambda i: (i, 0, 0)),
            pl.BlockSpec((need_rows, LANES), lambda i: (0, 0)),
            tile,
        ],
        out_specs=[
            tile,
            tile,
            pl.BlockSpec((SPAN, need_rows, LANES), lambda i: (0, 0, 0)),
            pl.BlockSpec(memory_space=pltpu.SMEM),
        ],
        out_shape=[jax.ShapeDtypeStruct((rows_dev, width), bf16)] * 2
        + [
            jax.ShapeDtypeStruct((SPAN, need_rows, LANES), jnp.int32),
            jax.ShapeDtypeStruct((1, 1), jnp.float32),
        ],
        scratch_shapes=[
            pltpu.VMEM((SPAN, need_rows, LANES), jnp.int32),
            pltpu.VMEM((teams, 8, LANES), jnp.float32),
            pltpu.SemaphoreType.DMA((SPAN,)),
            pltpu.SemaphoreType.DMA((SPAN,)),
            pltpu.SemaphoreType.DMA((teams,)),
            pltpu.SemaphoreType.DMA((teams,)),
        ],
        compiler_params=pltpu.CompilerParams(collective_id=1, has_side_effects=True),
    )(
        assignment.reshape(groups, 1, group_rows), need.reshape(need_rows, LANES), features
    )

    tables, reader, key, slot = make_plan(
        needs.reshape(SPAN, SPAN, block_count), column, position, capacity, pair_count
    )
    block = (cluster, width)
    part = (head_step(width), HEADS * cluster)
    in_smem = pl.BlockSpec(memory_space=pltpu.SMEM)
    in_vmem = pl.BlockSpec(memory_space=pltpu.VMEM)

    def layer(which, sizes):
        near_limit, end_limit, first_limit, union_limit = sizes
        steps = 4 + len({end_limit, first_limit, union_limit}) - 1
        buffers = [
            capacity, near_limit, capacity, union_limit, union_limit,
            max(union_limit - first_limit, 1), max(union_limit - first_limit, 1),
            capacity, capacity,
            capacity, near_limit, union_limit, 2 * capacity, block_count,
        ]
        return pl.pallas_call(
            functools.partial(layer_kernel, capacity, sizes, stride, pair_count),
            in_specs=[in_smem] * 4 + [in_vmem] * 4,
            out_specs=in_vmem,
            out_shape=jax.ShapeDtypeStruct((rows_dev, width), bf16),
            scratch_shapes=[pltpu.VMEM((count,) + block, bf16) for count in buffers]
            + [
                pltpu.VMEM((width, width), bf16),
                pltpu.VMEM((block_count + SPAN * capacity,) + part, jnp.float32),
                pltpu.SemaphoreType.DMA((4,)),
                pltpu.SemaphoreType.DMA((4,)),
                pltpu.SemaphoreType.DMA((steps,)),
                pltpu.SemaphoreType.DMA((2, 4)),
                pltpu.SemaphoreType.DMA((2, steps)),
                pltpu.SemaphoreType.DMA((2, 2)),
                pltpu.SemaphoreType.DMA((2, 2)),
            ],
            compiler_params=pltpu.CompilerParams(
                collective_id=which, has_side_effects=True, vmem_limit_bytes=60 * 2**20
            ),
        )

    attended = lax.cond(
        over[0, 0] <= 0.0, layer(0, limits), layer(2, full),
        tables, reader, key, slot, normed.reshape(block_count, cluster, width),
        w_query, w_key, w_value,
    )
    finish_rows = math.gcd(groups, 4) * group_rows
    tile = pl.BlockSpec((finish_rows, width), lambda i: (i, 0))
    weight = pl.BlockSpec((width, width), lambda i: (0, 0))
    return pl.pallas_call(
        finish_kernel,
        grid=(rows_dev // finish_rows,),
        in_specs=[tile, tile, weight, weight],
        out_specs=tile,
        out_shape=jax.ShapeDtypeStruct((rows_dev, width), bf16),
        scratch_shapes=[pltpu.VMEM((width, width), bf16)],
        compiler_params=pltpu.CompilerParams(vmem_limit_bytes=60 * 2**20),
    )(placed, attended, w_out, w_mix)


def solution(mesh):
    placed = (
        P(("groups", "elec"), None),
        P(("groups", "elec")),
        P(("groups", "elec"), None),
        P(),
        P(),
        P(),
        P(),
        P(),
    )
    return jax.shard_map(
        body, mesh=mesh, in_specs=placed, out_specs=P(("groups", "elec"), None), check_vma=False
    )
```

```python
import functools
import math

import jax
import jax.numpy as jnp
from jax import lax
from jax.experimental import pallas as pl
from jax.experimental.pallas import tpu as pltpu
from jax.sharding import PartitionSpec as P

HEADS = 16
SPAN = 8
LANES = 128
MESH = pl.DeviceIdType.MESH


def layer_norm(rows):
    mean = jnp.mean(rows, axis=-1, keepdims=True)
    centred = rows - mean
    variance = jnp.mean(centred * centred, axis=-1, keepdims=True)
    return centred * lax.rsqrt(variance + 1e-05)


def own_needs(listed, block_count, stride):
    flat = listed.reshape(-1)
    column = (flat // block_count // stride) * block_count + flat % block_count
    columns = jnp.arange(SPAN * block_count, dtype=jnp.int32)
    hit = column[None, :] == columns[:, None]
    return column, jnp.max(jnp.where(hit, 1, 0), axis=1).astype(jnp.int32)


def before(flags):
    size = flags.shape[-1]
    lower = (jnp.arange(size)[:, None] < jnp.arange(size)[None, :]).astype(jnp.bfloat16)
    counts = jnp.dot(
        flags.reshape(-1, size).astype(jnp.bfloat16), lower, preferred_element_type=jnp.float32
    )
    return counts.reshape(flags.shape).astype(jnp.int32)


def invert(place, flags, values, size):
    hit = (place[..., None, :] == jnp.arange(size, dtype=jnp.int32)[:, None]) & (
        flags[..., None, :] > 0
    )
    return jnp.sum(jnp.where(hit, values[..., None, :], 0), axis=-1).astype(jnp.int32)


def make_plan(needs, column, position, capacity, pair_count):
    blocks = needs.shape[-1]
    owners = jnp.arange(SPAN, dtype=jnp.int32)
    static = list(range(SPAN))

    def arrange(*readers):
        flags, left = [], jnp.ones((SPAN, blocks), jnp.int32)
        for chosen in readers:
            flags.append(jnp.stack([needs[chosen(o), o] for o in static]) * left)
            left = left - flags[-1]
        flags = jnp.stack(flags + [left])
        counts = jnp.sum(flags, axis=-1, keepdims=True)
        start = jnp.cumsum(counts, axis=0) - counts
        return jnp.sum(flags * (before(flags) + start), axis=0)

    def end(o):
        return 2 * (3 * (1 - o // 4)) + o % 2

    def middle(o):
        return 2 * (2 - o // 4) + o % 2

    order = arrange(
        lambda o: end(o) ^ 1, end, lambda o: middle(o) ^ 1, middle
    )
    near_order = arrange(lambda o: o ^ 3, lambda o: o ^ 2)
    rank = before(needs)
    within = jnp.arange(blocks, dtype=jnp.int32)

    def at(array, index):
        return lax.dynamic_index_in_dim(array, index, 0, keepdims=False)

    mine = lax.dynamic_index_in_dim(needs, position, 1, keepdims=False)
    mine_rank = lax.dynamic_index_in_dim(rank, position, 1, keepdims=False)
    all_flags = jnp.ones((blocks,), jnp.int32)
    lists = jnp.stack(
        [
            invert(at(mine_rank, position ^ 1), at(mine, position ^ 1), within, LANES),
            invert(at(near_order, position), all_flags, within, LANES),
            invert(at(order, position), all_flags, within, LANES),
        ]
    )

    z, y = position // 2, position % 2
    half = z // 2
    inner = (z + half) % 2
    partner_needs = at(needs, position ^ 1)
    partner_rank = at(rank, position ^ 1)
    sources = [2 * (2 - half) + y, 2 * (3 * (1 - half)) + y]
    filters = jnp.stack(
        [
            invert(at(partner_rank, s), at(partner_needs, s), at(order, s), LANES)
            for s in sources
        ]
    )
    tables = jnp.concatenate([lists, filters], axis=0)

    my_rank = at(rank, position)
    oz = owners // 2
    outer_owner = 1 - (oz + oz // 2) % 2
    same_half = owners // 4 == position // 4
    same_line = owners % 2 == y
    source_group = jnp.where(
        same_half, owners ^ position, jnp.where(same_line, 4 + outer_owner, 6 + outer_owner)
    )
    by_rank = (owners == (position ^ 1)) | (~same_half & ~same_line & (inner > 0))
    location = jnp.where(
        (owners == position)[:, None],
        within[None, :],
        jnp.where(
            by_rank[:, None], my_rank, jnp.where(same_half[:, None], near_order, order)
        ),
    )
    hit = column[:, None] == jnp.arange(SPAN * blocks, dtype=jnp.int32)[None, :]
    groups = jnp.broadcast_to(source_group[:, None], location.shape)
    packed = (groups * blocks + location).reshape(-1)
    packed = jnp.sum(jnp.where(hit, packed[None, :], 0), axis=1)
    entries = column.shape[0]
    group, key = packed // blocks, packed % blocks
    steps = jnp.arange(entries, dtype=jnp.int32)
    earlier = (group[:, None] == group[None, :]) & (steps[None, :] < steps[:, None])
    slots = group * capacity + jnp.sum(jnp.where(earlier, 1, 0), axis=1)
    slot_hit = slots[None, :] == jnp.arange(SPAN * capacity, dtype=jnp.int32)[:, None]
    jobs = jnp.sum(
        jnp.where(slot_hit, ((steps // pair_count) * blocks + key)[None, :], 0), axis=1
    )
    return (
        tables,
        (jobs // blocks).astype(jnp.int32),
        (jobs % blocks).astype(jnp.int32),
        (slots + blocks).astype(jnp.int32),
    )


def head_step(width):
    return -(-(width // HEADS + 2) // 8) * 8


def excess(readers, limits):
    rows = lax.broadcasted_iota(jnp.int32, readers[0].shape, 0)
    lanes = lax.broadcasted_iota(jnp.int32, readers[0].shape, 1)
    left = lanes < LANES // 2
    lower = rows < SPAN // 4
    large = jnp.maximum
    end = jnp.where(lower, large(readers[6], readers[7]), large(readers[0], readers[1]))
    middle = [jnp.where(lower, readers[4 + k], readers[2 + k]) for k in range(2)]
    first = large(end, jnp.where(left, middle[1], middle[0]))
    union = large(end, large(*middle))
    near = large(readers[4], readers[5])
    for row, k in ((0, 2), (1, 0), (2, 6)):
        near = jnp.where(rows == row, large(readers[k], readers[k + 1]), near)
    over = None
    for flags, limit in zip((near, end, first, union), limits):
        for part in (left, ~left):
            count = jnp.sum(jnp.where(part, flags, 0).astype(jnp.float32), axis=1, keepdims=True)
            worst = jnp.max(count, axis=0, keepdims=True) - float(limit)
            over = worst if over is None else jnp.maximum(over, worst)
    return over


def place_kernel(
    stride, limits, assignment_ref, need_ref, features_ref, placed_ref, normed_ref, needs_ref,
    over_ref, landing, flags, s_send, s_recv, g_send, g_recv,
):
    groups, _, size = assignment_ref.shape
    me = lax.axis_index("elec")
    group = lax.axis_index("groups")
    peers = lax.axis_size("elec")
    position = me // stride
    step_index = pl.program_id(0)
    teams = flags.shape[0]
    team = group * stride + lax.rem(me, stride)

    def toward(step):
        return (group, lax.rem(me + step * stride, peers))

    def across(step):
        other = lax.rem(team + step, teams)
        return (other // stride, position * stride + lax.rem(other, stride))

    def ask(step):
        return pltpu.make_async_remote_copy(
            src_ref=need_ref, dst_ref=landing.at[step],
            send_sem=s_send.at[step], recv_sem=s_recv.at[step],
            device_id=toward(step), device_id_type=MESH,
        )

    def tell(step):
        return pltpu.make_async_remote_copy(
            src_ref=flags.at[0], dst_ref=flags.at[step],
            send_sem=g_send.at[step], recv_sem=g_recv.at[step],
            device_id=across(step), device_id_type=MESH,
        )

    @pl.when(step_index == 0)
    def _():
        barrier = pltpu.get_barrier_semaphore()
        for step in range(1, SPAN):
            pl.semaphore_signal(barrier, inc=1, device_id=toward(step), device_id_type=MESH)
        for step in range(1, teams):
            pl.semaphore_signal(barrier, inc=1, device_id=across(step), device_id_type=MESH)
        pl.semaphore_wait(barrier, SPAN - 1 + teams - 1)
        for step in range(1, SPAN):
            ask(step).start()
        landing[0] = need_ref[...]

    @pl.when(step_index == pl.num_programs(0) - 1)
    def _():
        for step in range(1, SPAN):
            ask(step).wait()
        readers = [landing[lax.rem(position - q + SPAN, SPAN)] for q in range(SPAN)]
        for q in range(SPAN):
            needs_ref[q] = readers[q]
        flags[0] = jnp.broadcast_to(excess(readers, limits), flags.shape[1:])
        for step in range(1, teams):
            tell(step).start()

    lane = lax.broadcasted_iota(jnp.int32, (size, LANES), 1).astype(jnp.float32)
    for i in range(groups):
        rows = pl.ds(i * size, size)
        base = me * (features_ref.shape[0] * pl.num_programs(0)) + (
            (step_index * groups + i) * size
        )
        local = (assignment_ref[i] - base).astype(jnp.float32)
        takes = jnp.broadcast_to(local, (LANES, size)).T
        one_hot = jnp.concatenate(
            [jnp.where(takes == lane + k, 1.0, 0.0) for k in range(0, size, LANES)], axis=1
        ).astype(jnp.bfloat16)
        placed = jnp.dot(one_hot, features_ref[rows, :], preferred_element_type=jnp.float32)
        placed_ref[rows, :] = placed.astype(jnp.bfloat16)
        normed_ref[rows, :] = layer_norm(placed).astype(jnp.bfloat16)

    @pl.when(step_index == pl.num_programs(0) - 1)
    def _():
        for step in range(1, teams):
            tell(step).wait()
        worst = flags[0]
        for step in range(1, teams):
            worst = jnp.maximum(worst, flags[step])
        over_ref[0, 0] = jnp.max(worst)


def layer_kernel(
    capacity, limits, stride, pair_count,
    tables_ref, reader_ref, key_ref, slot_ref, blocks_ref, wq_ref, wk_ref, wv_ref,
    out_ref,
    near1, near2, near3, far0, far1, rest0, rest1, side0, side1, out_near, out_plane, out_far, out_side,
    queries, wv_turned, parts,
    n_send, n_recv, l_send, f_send, f_recv, p_send, p_recv,
):
    f32, bf16 = jnp.float32, jnp.bfloat16
    me = lax.axis_index("elec")
    group = lax.axis_index("groups")
    peers = lax.axis_size("elec")
    position = me // stride
    rest = lax.rem(me, stride)
    block_count, cluster, width = blocks_ref.shape
    head_width = width // HEADS
    cap = capacity
    z, y = position // 2, lax.rem(position, 2)
    half = z // 2
    inner = lax.rem(z + half, 2)
    pair_z = z + 1 - 2 * lax.rem(z, 2)
    pair_y = 1 - y

    def device(zz, yy):
        return (group, (2 * zz + yy) * stride + rest)

    near_devices = [device(z, pair_y), device(pair_z, y), device(pair_z, pair_y)]
    far_inner = device(2 - half, y)
    far, late, side = [far0, far1], [rest0, rest1], [side0, side1]
    near_limit, end_limit, first_limit, union_limit = limits
    part_one = (cap + 1) // 2
    part_two = cap + (end_limit - cap + 1) // 2
    bounds = [0, part_one, cap, part_two, end_limit]
    relayed = len(bounds) - 1
    for bound in (first_limit, union_limit):
        if bound > bounds[-1]:
            bounds.append(bound)
    chunks = [(a, b - a) for a, b in zip(bounds, bounds[1:])]
    last = len(chunks) - 1
    refinable = bounds.index(first_limit)
    plane_chunks = [(0, cap), (cap, near_limit - cap)]

    barrier = pltpu.get_barrier_semaphore()
    for step in range(1, SPAN):
        pl.semaphore_signal(
            barrier, inc=1, device_id=(group, lax.rem(me + step * stride, peers)),
            device_id_type=MESH,
        )
    pl.semaphore_wait(barrier, SPAN - 1)

    def gather(row, first, count, source, target, base):
        def one(k, carry):
            target[base + first + k] = source[tables_ref[row, first + k]]
            return carry

        lax.fori_loop(0, count, one, 0)

    def far_copy(s, c):
        start, count = chunks[c]
        target = far[s].at[pl.ds(start, count)]
        if c >= refinable:
            target = late[s].at[pl.ds(start - first_limit, count)]
        return pltpu.make_async_remote_copy(
            src_ref=out_far.at[pl.ds(start, count)], dst_ref=target,
            send_sem=l_send.at[c], recv_sem=f_recv.at[s, c],
            device_id=far_inner, device_id_type=MESH,
        )

    def forward_copy(s, c):
        start, count = chunks[c]
        return pltpu.make_async_remote_copy(
            src_ref=far[s].at[pl.ds(start, count)], dst_ref=far[s].at[pl.ds(start, count)],
            send_sem=f_send.at[s, c], recv_sem=f_recv.at[s, c],
            device_id=near_devices[1], device_id_type=MESH,
        )

    def side_copy(s, k, source, base):
        start, count = chunks[k]
        return pltpu.make_async_remote_copy(
            src_ref=source.at[pl.ds(base + start, count)], dst_ref=side[s].at[pl.ds(start, count)],
            send_sem=p_send.at[s, k], recv_sem=p_recv.at[s, k],
            device_id=near_devices[0], device_id_type=MESH,
        )

    def filtered(s, k):
        return side_copy(s, k, out_side, s * cap)

    def passed_on(s, k):
        return side_copy(s, k, far[s], 0)

    def near_copy():
        return pltpu.make_async_remote_copy(
            src_ref=out_near, dst_ref=near1, send_sem=n_send.at[0], recv_sem=n_recv.at[0],
            device_id=near_devices[0], device_id_type=MESH,
        )

    def plane_copy(c):
        start, count = plane_chunks[c]
        return pltpu.make_async_remote_copy(
            src_ref=out_plane.at[pl.ds(start, count)], dst_ref=near2.at[pl.ds(start, count)],
            send_sem=n_send.at[1 + c], recv_sem=n_recv.at[1 + c],
            device_id=near_devices[1], device_id_type=MESH,
        )

    def plane_pass():
        return pltpu.make_async_remote_copy(
            src_ref=near2.at[pl.ds(0, cap)], dst_ref=near3,
            send_sem=n_send.at[3], recv_sem=n_recv.at[3],
            device_id=near_devices[0], device_id_type=MESH,
        )

    def send_far(s, c):
        gather(2, chunks[c][0], chunks[c][1], blocks_ref, out_far, 0)
        far_copy(s, c).start()

    @pl.when(inner == 1)
    def _():
        for c in range(last + 1):
            send_far(0, c)

    @pl.when(inner == 0)
    def _():
        for c in range(refinable):
            send_far(1, c)

    gather(0, 0, cap, blocks_ref, out_near, 0)
    near_copy().start()
    for c in range(2):
        gather(1, plane_chunks[c][0], plane_chunks[c][1], blocks_ref, out_plane, 0)
        plane_copy(c).start()

    lane = lax.broadcasted_iota(jnp.int32, (cluster, LANES), 1)
    per = LANES // 2 // head_width
    chosen = [
        jnp.where(lane // head_width == c, 1.0, 0.0).astype(bf16) for c in range(2 * per)
    ]
    low = lax.broadcasted_iota(jnp.int32, (head_width, LANES), 1) < cluster
    scale = math.log2(math.e) / head_width**0.5
    turned = (((1,), (1,)), ((), ()))

    def unit(size):
        row = lax.broadcasted_iota(jnp.int32, (size, size), 0)
        column = lax.broadcasted_iota(jnp.int32, (size, size), 1)
        return jnp.where(row == column, 1.0, 0.0).astype(bf16)

    wv_turned[...] = lax.dot_general(
        unit(width), wv_ref[...], turned, preferred_element_type=f32
    ).astype(bf16)

    def project(i, carry):
        rows = blocks_ref[pl.ds(i * SPAN, SPAN)].reshape(SPAN * cluster, width)
        result = jnp.dot(rows, wq_ref[...], preferred_element_type=f32) * scale
        queries[pl.ds(i * SPAN, SPAN)] = result.astype(bf16).reshape(SPAN, cluster, width)
        return carry

    lax.fori_loop(0, block_count // SPAN, project, 0)

    def several(places, query_blocks, key_blocks):
        count = len(places)
        keys = jnp.dot(
            jnp.concatenate(key_blocks, axis=0), wk_ref[...], preferred_element_type=f32
        ).astype(bf16)
        values = [
            lax.dot_general(wv_turned[...], rows, turned, preferred_element_type=f32).astype(bf16)
            for rows in key_blocks
        ]
        scores = []
        for i in range(count):
            for g in range(HEADS // per):
                band = (g // 2) * LANES
                query = query_blocks[i][:, band : band + LANES]
                stacked = jnp.concatenate(
                    [query * chosen[(g % 2) * per + c] for c in range(per)], axis=0
                )
                scores.append(
                    lax.dot_general(
                        keys[i * cluster : (i + 1) * cluster, band : band + LANES],
                        stacked, turned, preferred_element_type=f32,
                    )
                )
        weights = []
        for i in range(count):
            for g in range(HEADS // per):
                score = scores[i * (HEADS // per) + g]
                columns = pl.ds(g * per * cluster, per * cluster)
                top = jnp.max(score, axis=0, keepdims=True)
                weight = jnp.exp2(score - top)
                parts[places[i], head_width : head_width + 1, columns] = top
                parts[places[i], head_width + 1 : head_width + 2, columns] = jnp.sum(
                    weight, axis=0, keepdims=True
                )
                weights.append(weight.astype(bf16))
        for i in range(count):
            for g in range(HEADS // per):
                rows = per * head_width
                result = jnp.dot(
                    values[i][g * rows : (g + 1) * rows], weights[i * (HEADS // per) + g],
                    preferred_element_type=f32,
                )
                for k in range(per // 2):
                    top = 2 * k * head_width
                    lanes = slice(k * LANES, (k + 1) * LANES)
                    first = (g * per // 2 + k) * LANES
                    parts[places[i], 0:head_width, pl.ds(first, LANES)] = jnp.where(
                        low,
                        result[top : top + head_width, lanes],
                        result[top + head_width : top + 2 * head_width, lanes],
                    )

    def own_blocks(first, count, batch):
        def one(i, carry):
            index = [first + i * batch + k for k in range(batch)]
            several(index, [queries[j] for j in index], [blocks_ref[j] for j in index])
            return carry

        lax.fori_loop(0, count // batch, one, 0)

    def listed(which, source):
        batch = 5 if cap % 5 == 0 else 1

        def one(i, carry):
            index = [which * cap + i * batch + k for k in range(batch)]
            several(
                [block_count + j for j in index],
                [queries[reader_ref[j]] for j in index],
                [source[key_ref[j]] for j in index],
            )
            return carry

        lax.fori_loop(0, cap // batch, one, 0)

    def on_inner(work):
        pl.when(inner == 1)(work)

    def on_outer(work):
        pl.when(inner == 0)(work)

    def relay(s, c):
        far_copy(s, c).wait_recv()
        forward_copy(s, c).start()

    def refine(s):
        arrived(s, relayed, refinable)
        gather(3 + s, 0, cap, far[s], out_side, s * cap)
        for k in range(2):
            filtered(s, k).start()

    def pass_on(s, k):
        far_copy(s, k).wait_recv()
        passed_on(s, k).start()

    def arrived(s, first, stop):
        for c in range(first, stop):
            far_copy(s, c).wait_recv()

    def late_arrived(s):
        arrived(s, refinable, last + 1)
        for k in range(union_limit - first_limit):
            far[s][first_limit + k] = late[s][k]

    def side_arrived(s):
        for k in range(2):
            filtered(s, k).wait_recv()

    eighth = block_count // 8
    own_blocks(0, 3 * eighth, 4)
    on_inner(lambda: relay(1, 0))
    own_blocks(3 * eighth, 3 * eighth, 4)
    on_inner(lambda: relay(1, 1))
    own_blocks(6 * eighth, 2 * eighth, 4)
    on_inner(lambda: relay(1, 2))
    listed(0, blocks_ref)
    on_inner(lambda: relay(1, 3))
    near_copy().wait_recv()
    listed(1, near1)

    @pl.when(inner == 1)
    def _():
        refine(1)
        relay(0, 0)
        plane_copy(0).wait_recv()
        plane_pass().start()
        relay(0, 1)
        side_arrived(1)
        listed(7, side1)
        relay(0, 2)
        plane_copy(1).wait_recv()
        relay(0, 3)
        listed(2, near2)
        refine(0)
        plane_pass().wait_recv()
        listed(3, near3)
        late_arrived(0)
        listed(4, far0)
        late_arrived(1)
        listed(5, far1)
        side_arrived(0)
        listed(6, side0)

    @pl.when(inner == 0)
    def _():
        plane_copy(0).wait_recv()
        plane_pass().start()
        pass_on(1, 0)
        pass_on(1, 1)
        plane_copy(1).wait_recv()
        listed(2, near2)
        plane_pass().wait_recv()
        listed(3, near3)
        arrived(1, 2, relayed)
        listed(5, far1)
        side_arrived(1)
        listed(7, side1)
        pass_on(0, 0)
        for c in range(refinable, last + 1):
            send_far(1, c)
        pass_on(0, 1)
        side_arrived(0)
        listed(6, side0)
        arrived(0, 2, relayed)
        listed(4, far0)

    def combine(i, carry):
        for k in range(SPAN):
            j = i * SPAN + k
            places = [j] + [slot_ref[j * pair_count + p] for p in range(pair_count)]
            tops = [parts[a, head_width : head_width + 1, :] for a in places]
            sums = [parts[a, head_width + 1 : head_width + 2, :] for a in places]
            top = functools.reduce(jnp.maximum, tops)
            factors = [jnp.exp2(t - top) for t in tops]
            total = sum(f * s for f, s in zip(factors, sums))
            inverse = 1.0 / total
            merged = sum(
                parts[a, 0:head_width, :] * (f * inverse) for a, f in zip(places, factors)
            ).astype(bf16)
            stacked = jnp.concatenate(
                [merged[:, c : c + LANES] for c in range(0, HEADS * cluster, LANES)], axis=0
            )
            upright = lax.dot_general(
                unit(LANES), stacked, turned, preferred_element_type=f32
            ).astype(bf16)
            rows = pl.ds(pl.multiple_of(j * cluster, cluster), cluster)
            out_ref[rows, 0:LANES] = upright[0:cluster]
            out_ref[rows, LANES : 2 * LANES] = upright[cluster : 2 * cluster]
        return carry

    lax.fori_loop(0, block_count // SPAN, combine, 0)

    @pl.when(inner == 1)
    def _():
        for s in range(2):
            for c in range(relayed):
                forward_copy(s, c).wait_send()
            for k in range(2):
                filtered(s, k).wait_send()

    @pl.when(inner == 0)
    def _():
        for s in range(2):
            for k in range(2):
                passed_on(s, k).wait_send()

    for c in range(last + 1):
        far_copy(0, c).wait_send()
    near_copy().wait_send()
    for c in range(2):
        plane_copy(c).wait_send()
    plane_pass().wait_send()


def finish_kernel(placed_ref, attended_ref, wo_ref, wm_ref, out_ref, wo_sorted):
    f32, bf16 = jnp.float32, jnp.bfloat16
    width = wo_ref.shape[0]
    head_width = width // HEADS

    @pl.when(pl.program_id(0) == 0)
    def _():
        for h in range(HEADS):
            start = (h % 2) * (width // 2) + (h // 2) * head_width
            wo_sorted[start : start + head_width, :] = wo_ref[
                h * head_width : (h + 1) * head_width, :
            ]

    projected = jnp.dot(attended_ref[...], wo_sorted[...], preferred_element_type=f32)
    middle = (placed_ref[...].astype(f32) + projected).astype(bf16).astype(f32)
    second = layer_norm(middle).astype(bf16)
    mixed = middle + jnp.tanh(jnp.dot(second, wm_ref[...], preferred_element_type=f32))
    out_ref[...] = mixed.astype(bf16)


def body(features, assignment, pairs, w_query, w_key, w_value, w_out, w_mix):
    rows_dev, width = features.shape
    block_count, pair_count = pairs.shape
    cluster = rows_dev // block_count
    capacity = (block_count * pair_count + SPAN - 1) // SPAN + 1
    stride = lax.axis_size("elec") // SPAN
    position = lax.axis_index("elec") // stride
    group_rows = SPAN * cluster
    groups = rows_dev // group_rows
    bf16 = jnp.bfloat16

    column, need = own_needs(pairs, block_count, stride)
    need_rows = SPAN * block_count // LANES
    batch = math.gcd(groups, 2)
    tile = pl.BlockSpec((batch * group_rows, width), lambda i: (i, 0))
    full = (2 * capacity, 2 * capacity, block_count, block_count)
    small = (capacity + 18, capacity + 18, capacity + 27, capacity + 34)
    limits = tuple(min(a, b) for a, b in zip(small, full))
    teams = lax.axis_size("groups") * stride
    placed, normed, needs, over = pl.pallas_call(
        functools.partial(place_kernel, stride, limits),
        grid=(groups // batch,),
        in_specs=[
            pl.BlockSpec((batch, 1, group_rows), lambda i: (i, 0, 0)),
            pl.BlockSpec((need_rows, LANES), lambda i: (0, 0)),
            tile,
        ],
        out_specs=[
            tile,
            tile,
            pl.BlockSpec((SPAN, need_rows, LANES), lambda i: (0, 0, 0)),
            pl.BlockSpec(memory_space=pltpu.SMEM),
        ],
        out_shape=[jax.ShapeDtypeStruct((rows_dev, width), bf16)] * 2
        + [
            jax.ShapeDtypeStruct((SPAN, need_rows, LANES), jnp.int32),
            jax.ShapeDtypeStruct((1, 1), jnp.float32),
        ],
        scratch_shapes=[
            pltpu.VMEM((SPAN, need_rows, LANES), jnp.int32),
            pltpu.VMEM((teams, 8, LANES), jnp.float32),
            pltpu.SemaphoreType.DMA((SPAN,)),
            pltpu.SemaphoreType.DMA((SPAN,)),
            pltpu.SemaphoreType.DMA((teams,)),
            pltpu.SemaphoreType.DMA((teams,)),
        ],
        compiler_params=pltpu.CompilerParams(collective_id=1, has_side_effects=True),
    )(
        assignment.reshape(groups, 1, group_rows), need.reshape(need_rows, LANES), features
    )

    tables, reader, key, slot = make_plan(
        needs.reshape(SPAN, SPAN, block_count), column, position, capacity, pair_count
    )
    block = (cluster, width)
    part = (head_step(width), HEADS * cluster)
    in_smem = pl.BlockSpec(memory_space=pltpu.SMEM)
    in_vmem = pl.BlockSpec(memory_space=pltpu.VMEM)

    def layer(which, sizes):
        near_limit, end_limit, first_limit, union_limit = sizes
        steps = 4 + len({end_limit, first_limit, union_limit}) - 1
        buffers = [
            capacity, near_limit, capacity, union_limit, union_limit,
            max(union_limit - first_limit, 1), max(union_limit - first_limit, 1),
            capacity, capacity,
            capacity, near_limit, union_limit, 2 * capacity, block_count,
        ]
        return pl.pallas_call(
            functools.partial(layer_kernel, capacity, sizes, stride, pair_count),
            in_specs=[in_smem] * 4 + [in_vmem] * 4,
            out_specs=in_vmem,
            out_shape=jax.ShapeDtypeStruct((rows_dev, width), bf16),
            scratch_shapes=[pltpu.VMEM((count,) + block, bf16) for count in buffers]
            + [
                pltpu.VMEM((width, width), bf16),
                pltpu.VMEM((block_count + SPAN * capacity,) + part, jnp.float32),
                pltpu.SemaphoreType.DMA((4,)),
                pltpu.SemaphoreType.DMA((4,)),
                pltpu.SemaphoreType.DMA((steps,)),
                pltpu.SemaphoreType.DMA((2, 4)),
                pltpu.SemaphoreType.DMA((2, steps)),
                pltpu.SemaphoreType.DMA((2, 2)),
                pltpu.SemaphoreType.DMA((2, 2)),
            ],
            compiler_params=pltpu.CompilerParams(
                collective_id=which, has_side_effects=True, vmem_limit_bytes=60 * 2**20
            ),
        )

    attended = lax.cond(
        over[0, 0] <= 0.0, layer(0, limits), layer(2, full),
        tables, reader, key, slot, normed.reshape(block_count, cluster, width),
        w_query, w_key, w_value,
    )
    finish_rows = math.gcd(groups, 4) * group_rows
    tile = pl.BlockSpec((finish_rows, width), lambda i: (i, 0))
    weight = pl.BlockSpec((width, width), lambda i: (0, 0))
    return pl.pallas_call(
        finish_kernel,
        grid=(rows_dev // finish_rows,),
        in_specs=[tile, tile, weight, weight],
        out_specs=tile,
        out_shape=jax.ShapeDtypeStruct((rows_dev, width), bf16),
        scratch_shapes=[pltpu.VMEM((width, width), bf16)],
        compiler_params=pltpu.CompilerParams(vmem_limit_bytes=60 * 2**20),
    )(placed, attended, w_out, w_mix)


def solution(mesh):
    placed = (
        P(("groups", "elec"), None),
        P(("groups", "elec")),
        P(("groups", "elec"), None),
        P(),
        P(),
        P(),
        P(),
        P(),
    )
    return jax.shard_map(
        body, mesh=mesh, in_specs=placed, out_specs=P(("groups", "elec"), None), check_vma=False
    )
```

```python
import functools
import math

import jax
import jax.numpy as jnp
from jax import lax
from jax.experimental import pallas as pl
from jax.experimental.pallas import tpu as pltpu
from jax.sharding import PartitionSpec as P

HEADS = 16
SPAN = 8
LANES = 128
MESH = pl.DeviceIdType.MESH


def layer_norm(rows):
    mean = jnp.mean(rows, axis=-1, keepdims=True)
    centred = rows - mean
    variance = jnp.mean(centred * centred, axis=-1, keepdims=True)
    return centred * lax.rsqrt(variance + 1e-05)


def own_needs(listed, block_count, stride):
    flat = listed.reshape(-1)
    column = (flat // block_count // stride) * block_count + flat % block_count
    columns = jnp.arange(SPAN * block_count, dtype=jnp.int32)
    hit = column[None, :] == columns[:, None]
    return column, jnp.max(jnp.where(hit, 1, 0), axis=1).astype(jnp.int32)


def before(flags):
    size = flags.shape[-1]
    lower = (jnp.arange(size)[:, None] < jnp.arange(size)[None, :]).astype(jnp.bfloat16)
    counts = jnp.dot(
        flags.reshape(-1, size).astype(jnp.bfloat16), lower, preferred_element_type=jnp.float32
    )
    return counts.reshape(flags.shape).astype(jnp.int32)


def invert(place, flags, values, size):
    hit = (place[..., None, :] == jnp.arange(size, dtype=jnp.int32)[:, None]) & (
        flags[..., None, :] > 0
    )
    return jnp.sum(jnp.where(hit, values[..., None, :], 0), axis=-1).astype(jnp.int32)


def make_plan(needs, column, position, capacity, pair_count):
    blocks = needs.shape[-1]
    owners = jnp.arange(SPAN, dtype=jnp.int32)
    static = list(range(SPAN))

    def arrange(*readers):
        flags, left = [], jnp.ones((SPAN, blocks), jnp.int32)
        for chosen in readers:
            flags.append(jnp.stack([needs[chosen(o), o] for o in static]) * left)
            left = left - flags[-1]
        flags = jnp.stack(flags + [left])
        counts = jnp.sum(flags, axis=-1, keepdims=True)
        start = jnp.cumsum(counts, axis=0) - counts
        return jnp.sum(flags * (before(flags) + start), axis=0)

    def end(o):
        return 2 * (3 * (1 - o // 4)) + o % 2

    def middle(o):
        return 2 * (2 - o // 4) + o % 2

    order = arrange(
        lambda o: end(o) ^ 1, end, lambda o: middle(o) ^ 1, middle
    )
    near_order = arrange(lambda o: o ^ 3, lambda o: o ^ 2)
    rank = before(needs)
    within = jnp.arange(blocks, dtype=jnp.int32)

    def at(array, index):
        return lax.dynamic_index_in_dim(array, index, 0, keepdims=False)

    mine = lax.dynamic_index_in_dim(needs, position, 1, keepdims=False)
    mine_rank = lax.dynamic_index_in_dim(rank, position, 1, keepdims=False)
    all_flags = jnp.ones((blocks,), jnp.int32)
    lists = jnp.stack(
        [
            invert(at(mine_rank, position ^ 1), at(mine, position ^ 1), within, LANES),
            invert(at(near_order, position), all_flags, within, LANES),
            invert(at(order, position), all_flags, within, LANES),
        ]
    )

    z, y = position // 2, position % 2
    half = z // 2
    inner = (z + half) % 2
    partner_needs = at(needs, position ^ 1)
    partner_rank = at(rank, position ^ 1)
    sources = [2 * (2 - half) + y, 2 * (3 * (1 - half)) + y]
    filters = jnp.stack(
        [
            invert(at(partner_rank, s), at(partner_needs, s), at(order, s), LANES)
            for s in sources
        ]
    )
    tables = jnp.concatenate([lists, filters], axis=0)

    my_rank = at(rank, position)
    oz = owners // 2
    outer_owner = 1 - (oz + oz // 2) % 2
    same_half = owners // 4 == position // 4
    same_line = owners % 2 == y
    source_group = jnp.where(
        same_half, owners ^ position, jnp.where(same_line, 4 + outer_owner, 6 + outer_owner)
    )
    by_rank = (owners == (position ^ 1)) | (~same_half & ~same_line & (inner > 0))
    location = jnp.where(
        (owners == position)[:, None],
        within[None, :],
        jnp.where(
            by_rank[:, None], my_rank, jnp.where(same_half[:, None], near_order, order)
        ),
    )
    hit = column[:, None] == jnp.arange(SPAN * blocks, dtype=jnp.int32)[None, :]
    groups = jnp.broadcast_to(source_group[:, None], location.shape)
    packed = (groups * blocks + location).reshape(-1)
    packed = jnp.sum(jnp.where(hit, packed[None, :], 0), axis=1)
    entries = column.shape[0]
    group, key = packed // blocks, packed % blocks
    steps = jnp.arange(entries, dtype=jnp.int32)
    earlier = (group[:, None] == group[None, :]) & (steps[None, :] < steps[:, None])
    slots = group * capacity + jnp.sum(jnp.where(earlier, 1, 0), axis=1)
    slot_hit = slots[None, :] == jnp.arange(SPAN * capacity, dtype=jnp.int32)[:, None]
    jobs = jnp.sum(
        jnp.where(slot_hit, ((steps // pair_count) * blocks + key)[None, :], 0), axis=1
    )
    return (
        tables,
        (jobs // blocks).astype(jnp.int32),
        (jobs % blocks).astype(jnp.int32),
        (slots + blocks).astype(jnp.int32),
    )


def head_step(width):
    return -(-(width // HEADS + 2) // 8) * 8


def excess(readers, limits):
    rows = lax.broadcasted_iota(jnp.int32, readers[0].shape, 0)
    lanes = lax.broadcasted_iota(jnp.int32, readers[0].shape, 1)
    left = lanes < LANES // 2
    lower = rows < SPAN // 4
    large = jnp.maximum
    end = jnp.where(lower, large(readers[6], readers[7]), large(readers[0], readers[1]))
    middle = [jnp.where(lower, readers[4 + k], readers[2 + k]) for k in range(2)]
    first = large(end, jnp.where(left, middle[1], middle[0]))
    union = large(end, large(*middle))
    near = large(readers[4], readers[5])
    for row, k in ((0, 2), (1, 0), (2, 6)):
        near = jnp.where(rows == row, large(readers[k], readers[k + 1]), near)
    over = None
    for flags, limit in zip((near, end, first, union), limits):
        for part in (left, ~left):
            count = jnp.sum(jnp.where(part, flags, 0).astype(jnp.float32), axis=1, keepdims=True)
            worst = jnp.max(count, axis=0, keepdims=True) - float(limit)
            over = worst if over is None else jnp.maximum(over, worst)
    return over


def place_kernel(
    stride, limits, assignment_ref, need_ref, features_ref, placed_ref, normed_ref, needs_ref,
    over_ref, landing, flags, s_send, s_recv, g_send, g_recv,
):
    groups, _, size = assignment_ref.shape
    me = lax.axis_index("elec")
    group = lax.axis_index("groups")
    peers = lax.axis_size("elec")
    position = me // stride
    step_index = pl.program_id(0)
    teams = flags.shape[0]
    team = group * stride + lax.rem(me, stride)

    def toward(step):
        return (group, lax.rem(me + step * stride, peers))

    def across(step):
        other = lax.rem(team + step, teams)
        return (other // stride, position * stride + lax.rem(other, stride))

    def ask(step):
        return pltpu.make_async_remote_copy(
            src_ref=need_ref, dst_ref=landing.at[step],
            send_sem=s_send.at[step], recv_sem=s_recv.at[step],
            device_id=toward(step), device_id_type=MESH,
        )

    def tell(step):
        return pltpu.make_async_remote_copy(
            src_ref=flags.at[0], dst_ref=flags.at[step],
            send_sem=g_send.at[step], recv_sem=g_recv.at[step],
            device_id=across(step), device_id_type=MESH,
        )

    @pl.when(step_index == 0)
    def _():
        barrier = pltpu.get_barrier_semaphore()
        for step in range(1, SPAN):
            pl.semaphore_signal(barrier, inc=1, device_id=toward(step), device_id_type=MESH)
        for step in range(1, teams):
            pl.semaphore_signal(barrier, inc=1, device_id=across(step), device_id_type=MESH)
        pl.semaphore_wait(barrier, SPAN - 1 + teams - 1)
        for step in range(1, SPAN):
            ask(step).start()
        landing[0] = need_ref[...]

    @pl.when(step_index == pl.num_programs(0) - 1)
    def _():
        for step in range(1, SPAN):
            ask(step).wait()
        readers = [landing[lax.rem(position - q + SPAN, SPAN)] for q in range(SPAN)]
        for q in range(SPAN):
            needs_ref[q] = readers[q]
        flags[0] = jnp.broadcast_to(excess(readers, limits), flags.shape[1:])
        for step in range(1, teams):
            tell(step).start()

    lane = lax.broadcasted_iota(jnp.int32, (size, LANES), 1).astype(jnp.float32)
    for i in range(groups):
        rows = pl.ds(i * size, size)
        base = me * (features_ref.shape[0] * pl.num_programs(0)) + (
            (step_index * groups + i) * size
        )
        local = (assignment_ref[i] - base).astype(jnp.float32)
        takes = jnp.broadcast_to(local, (LANES, size)).T
        one_hot = jnp.concatenate(
            [jnp.where(takes == lane + k, 1.0, 0.0) for k in range(0, size, LANES)], axis=1
        ).astype(jnp.bfloat16)
        placed = jnp.dot(one_hot, features_ref[rows, :], preferred_element_type=jnp.float32)
        placed_ref[rows, :] = placed.astype(jnp.bfloat16)
        normed_ref[rows, :] = layer_norm(placed).astype(jnp.bfloat16)

    @pl.when(step_index == pl.num_programs(0) - 1)
    def _():
        for step in range(1, teams):
            tell(step).wait()
        worst = flags[0]
        for step in range(1, teams):
            worst = jnp.maximum(worst, flags[step])
        over_ref[0, 0] = jnp.max(worst)


def layer_kernel(
    capacity, limits, stride, pair_count,
    tables_ref, reader_ref, key_ref, slot_ref, blocks_ref, wq_ref, wk_ref, wv_ref,
    out_ref,
    near1, near2, near3, far0, far1, rest0, rest1, side0, side1, out_near, out_plane, out_far, out_side,
    queries, wv_turned, parts,
    n_send, n_recv, l_send, f_send, f_recv, p_send, p_recv,
):
    f32, bf16 = jnp.float32, jnp.bfloat16
    me = lax.axis_index("elec")
    group = lax.axis_index("groups")
    peers = lax.axis_size("elec")
    position = me // stride
    rest = lax.rem(me, stride)
    block_count, cluster, width = blocks_ref.shape
    head_width = width // HEADS
    cap = capacity
    z, y = position // 2, lax.rem(position, 2)
    half = z // 2
    inner = lax.rem(z + half, 2)
    pair_z = z + 1 - 2 * lax.rem(z, 2)
    pair_y = 1 - y

    def device(zz, yy):
        return (group, (2 * zz + yy) * stride + rest)

    near_devices = [device(z, pair_y), device(pair_z, y), device(pair_z, pair_y)]
    far_inner = device(2 - half, y)
    far, late, side = [far0, far1], [rest0, rest1], [side0, side1]
    near_limit, end_limit, first_limit, union_limit = limits
    part_one = (cap + 1) // 2
    part_two = cap + (end_limit - cap + 1) // 2
    bounds = [0, part_one, cap, part_two, end_limit]
    relayed = len(bounds) - 1
    for bound in (first_limit, union_limit):
        if bound > bounds[-1]:
            bounds.append(bound)
    chunks = [(a, b - a) for a, b in zip(bounds, bounds[1:])]
    last = len(chunks) - 1
    refinable = bounds.index(first_limit)
    plane_chunks = [(0, cap), (cap, near_limit - cap)]

    barrier = pltpu.get_barrier_semaphore()
    for step in range(1, SPAN):
        pl.semaphore_signal(
            barrier, inc=1, device_id=(group, lax.rem(me + step * stride, peers)),
            device_id_type=MESH,
        )
    pl.semaphore_wait(barrier, SPAN - 1)

    def gather(row, first, count, source, target, base):
        def one(k, carry):
            target[base + first + k] = source[tables_ref[row, first + k]]
            return carry

        lax.fori_loop(0, count, one, 0)

    def far_copy(s, c):
        start, count = chunks[c]
        target = far[s].at[pl.ds(start, count)]
        if c >= refinable:
            target = late[s].at[pl.ds(start - first_limit, count)]
        return pltpu.make_async_remote_copy(
            src_ref=out_far.at[pl.ds(start, count)], dst_ref=target,
            send_sem=l_send.at[c], recv_sem=f_recv.at[s, c],
            device_id=far_inner, device_id_type=MESH,
        )

    def forward_copy(s, c):
        start, count = chunks[c]
        return pltpu.make_async_remote_copy(
            src_ref=far[s].at[pl.ds(start, count)], dst_ref=far[s].at[pl.ds(start, count)],
            send_sem=f_send.at[s, c], recv_sem=f_recv.at[s, c],
            device_id=near_devices[1], device_id_type=MESH,
        )

    def side_copy(s, k, source, base):
        start, count = chunks[k]
        return pltpu.make_async_remote_copy(
            src_ref=source.at[pl.ds(base + start, count)], dst_ref=side[s].at[pl.ds(start, count)],
            send_sem=p_send.at[s, k], recv_sem=p_recv.at[s, k],
            device_id=near_devices[0], device_id_type=MESH,
        )

    def filtered(s, k):
        return side_copy(s, k, out_side, s * cap)

    def passed_on(s, k):
        return side_copy(s, k, far[s], 0)

    def near_copy():
        return pltpu.make_async_remote_copy(
            src_ref=out_near, dst_ref=near1, send_sem=n_send.at[0], recv_sem=n_recv.at[0],
            device_id=near_devices[0], device_id_type=MESH,
        )

    def plane_copy(c):
        start, count = plane_chunks[c]
        return pltpu.make_async_remote_copy(
            src_ref=out_plane.at[pl.ds(start, count)], dst_ref=near2.at[pl.ds(start, count)],
            send_sem=n_send.at[1 + c], recv_sem=n_recv.at[1 + c],
            device_id=near_devices[1], device_id_type=MESH,
        )

    def plane_pass():
        return pltpu.make_async_remote_copy(
            src_ref=near2.at[pl.ds(0, cap)], dst_ref=near3,
            send_sem=n_send.at[3], recv_sem=n_recv.at[3],
            device_id=near_devices[0], device_id_type=MESH,
        )

    def send_far(s, c):
        gather(2, chunks[c][0], chunks[c][1], blocks_ref, out_far, 0)
        far_copy(s, c).start()

    @pl.when(inner == 1)
    def _():
        for c in range(last + 1):
            send_far(0, c)

    @pl.when(inner == 0)
    def _():
        for c in range(refinable):
            send_far(1, c)

    gather(0, 0, cap, blocks_ref, out_near, 0)
    near_copy().start()
    for c in range(2):
        gather(1, plane_chunks[c][0], plane_chunks[c][1], blocks_ref, out_plane, 0)
        plane_copy(c).start()

    lane = lax.broadcasted_iota(jnp.int32, (cluster, LANES), 1)
    per = LANES // 2 // head_width
    chosen = [
        jnp.where(lane // head_width == c, 1.0, 0.0).astype(bf16) for c in range(2 * per)
    ]
    low = lax.broadcasted_iota(jnp.int32, (head_width, LANES), 1) < cluster
    scale = math.log2(math.e) / head_width**0.5
    turned = (((1,), (1,)), ((), ()))

    def unit(size):
        row = lax.broadcasted_iota(jnp.int32, (size, size), 0)
        column = lax.broadcasted_iota(jnp.int32, (size, size), 1)
        return jnp.where(row == column, 1.0, 0.0).astype(bf16)

    wv_turned[...] = lax.dot_general(
        unit(width), wv_ref[...], turned, preferred_element_type=f32
    ).astype(bf16)

    def project(i, carry):
        rows = blocks_ref[pl.ds(i * SPAN, SPAN)].reshape(SPAN * cluster, width)
        result = jnp.dot(rows, wq_ref[...], preferred_element_type=f32) * scale
        queries[pl.ds(i * SPAN, SPAN)] = result.astype(bf16).reshape(SPAN, cluster, width)
        return carry

    lax.fori_loop(0, block_count // SPAN, project, 0)

    def several(places, query_blocks, key_blocks):
        count = len(places)
        keys = jnp.dot(
            jnp.concatenate(key_blocks, axis=0), wk_ref[...], preferred_element_type=f32
        ).astype(bf16)
        values = [
            lax.dot_general(wv_turned[...], rows, turned, preferred_element_type=f32).astype(bf16)
            for rows in key_blocks
        ]
        scores = []
        for i in range(count):
            for g in range(HEADS // per):
                band = (g // 2) * LANES
                query = query_blocks[i][:, band : band + LANES]
                stacked = jnp.concatenate(
                    [query * chosen[(g % 2) * per + c] for c in range(per)], axis=0
                )
                scores.append(
                    lax.dot_general(
                        keys[i * cluster : (i + 1) * cluster, band : band + LANES],
                        stacked, turned, preferred_element_type=f32,
                    )
                )
        weights = []
        for i in range(count):
            for g in range(HEADS // per):
                score = scores[i * (HEADS // per) + g]
                columns = pl.ds(g * per * cluster, per * cluster)
                top = jnp.max(score, axis=0, keepdims=True)
                weight = jnp.exp2(score - top)
                parts[places[i], head_width : head_width + 1, columns] = top
                parts[places[i], head_width + 1 : head_width + 2, columns] = jnp.sum(
                    weight, axis=0, keepdims=True
                )
                weights.append(weight.astype(bf16))
        for i in range(count):
            for g in range(HEADS // per):
                rows = per * head_width
                result = jnp.dot(
                    values[i][g * rows : (g + 1) * rows], weights[i * (HEADS // per) + g],
                    preferred_element_type=f32,
                )
                for k in range(per // 2):
                    top = 2 * k * head_width
                    lanes = slice(k * LANES, (k + 1) * LANES)
                    first = (g * per // 2 + k) * LANES
                    parts[places[i], 0:head_width, pl.ds(first, LANES)] = jnp.where(
                        low,
                        result[top : top + head_width, lanes],
                        result[top + head_width : top + 2 * head_width, lanes],
                    )

    def own_blocks(first, count, batch):
        def one(i, carry):
            index = [first + i * batch + k for k in range(batch)]
            several(index, [queries[j] for j in index], [blocks_ref[j] for j in index])
            return carry

        lax.fori_loop(0, count // batch, one, 0)

    def listed(which, source):
        batch = 5 if cap % 5 == 0 else 1

        def one(i, carry):
            index = [which * cap + i * batch + k for k in range(batch)]
            several(
                [block_count + j for j in index],
                [queries[reader_ref[j]] for j in index],
                [source[key_ref[j]] for j in index],
            )
            return carry

        lax.fori_loop(0, cap // batch, one, 0)

    def on_inner(work):
        pl.when(inner == 1)(work)

    def on_outer(work):
        pl.when(inner == 0)(work)

    def relay(s, c):
        far_copy(s, c).wait_recv()
        forward_copy(s, c).start()

    def refine(s):
        arrived(s, relayed, refinable)
        gather(3 + s, 0, cap, far[s], out_side, s * cap)
        for k in range(2):
            filtered(s, k).start()

    def pass_on(s, k):
        far_copy(s, k).wait_recv()
        passed_on(s, k).start()

    def arrived(s, first, stop):
        for c in range(first, stop):
            far_copy(s, c).wait_recv()

    def late_arrived(s):
        arrived(s, refinable, last + 1)
        for k in range(union_limit - first_limit):
            far[s][first_limit + k] = late[s][k]

    def side_arrived(s):
        for k in range(2):
            filtered(s, k).wait_recv()

    eighth = block_count // 8
    own_blocks(0, 3 * eighth, 4)
    on_inner(lambda: relay(1, 0))
    own_blocks(3 * eighth, 3 * eighth, 4)
    on_inner(lambda: relay(1, 1))
    own_blocks(6 * eighth, 2 * eighth, 4)
    on_inner(lambda: relay(1, 2))
    listed(0, blocks_ref)
    on_inner(lambda: relay(1, 3))
    near_copy().wait_recv()
    listed(1, near1)

    @pl.when(inner == 1)
    def _():
        refine(1)
        relay(0, 0)
        plane_copy(0).wait_recv()
        plane_pass().start()
        relay(0, 1)
        side_arrived(1)
        listed(7, side1)
        relay(0, 2)
        plane_copy(1).wait_recv()
        relay(0, 3)
        listed(2, near2)
        refine(0)
        plane_pass().wait_recv()
        listed(3, near3)
        late_arrived(0)
        listed(4, far0)
        late_arrived(1)
        listed(5, far1)
        side_arrived(0)
        listed(6, side0)

    @pl.when(inner == 0)
    def _():
        plane_copy(0).wait_recv()
        plane_pass().start()
        pass_on(1, 0)
        pass_on(1, 1)
        plane_copy(1).wait_recv()
        listed(2, near2)
        plane_pass().wait_recv()
        listed(3, near3)
        arrived(1, 2, relayed)
        listed(5, far1)
        side_arrived(1)
        listed(7, side1)
        pass_on(0, 0)
        for c in range(refinable, last + 1):
            send_far(1, c)
        pass_on(0, 1)
        side_arrived(0)
        listed(6, side0)
        arrived(0, 2, relayed)
        listed(4, far0)

    def combine(i, carry):
        for k in range(SPAN):
            j = i * SPAN + k
            places = [j] + [slot_ref[j * pair_count + p] for p in range(pair_count)]
            tops = [parts[a, head_width : head_width + 1, :] for a in places]
            sums = [parts[a, head_width + 1 : head_width + 2, :] for a in places]
            top = functools.reduce(jnp.maximum, tops)
            factors = [jnp.exp2(t - top) for t in tops]
            total = sum(f * s for f, s in zip(factors, sums))
            inverse = 1.0 / total
            merged = sum(
                parts[a, 0:head_width, :] * (f * inverse) for a, f in zip(places, factors)
            ).astype(bf16)
            stacked = jnp.concatenate(
                [merged[:, c : c + LANES] for c in range(0, HEADS * cluster, LANES)], axis=0
            )
            upright = lax.dot_general(
                unit(LANES), stacked, turned, preferred_element_type=f32
            ).astype(bf16)
            rows = pl.ds(pl.multiple_of(j * cluster, cluster), cluster)
            out_ref[rows, 0:LANES] = upright[0:cluster]
            out_ref[rows, LANES : 2 * LANES] = upright[cluster : 2 * cluster]
        return carry

    lax.fori_loop(0, block_count // SPAN, combine, 0)

    @pl.when(inner == 1)
    def _():
        for s in range(2):
            for c in range(relayed):
                forward_copy(s, c).wait_send()
            for k in range(2):
                filtered(s, k).wait_send()

    @pl.when(inner == 0)
    def _():
        for s in range(2):
            for k in range(2):
                passed_on(s, k).wait_send()

    for c in range(last + 1):
        far_copy(0, c).wait_send()
    near_copy().wait_send()
    for c in range(2):
        plane_copy(c).wait_send()
    plane_pass().wait_send()


def finish_kernel(placed_ref, attended_ref, wo_ref, wm_ref, out_ref, wo_sorted):
    f32, bf16 = jnp.float32, jnp.bfloat16
    width = wo_ref.shape[0]
    head_width = width // HEADS

    @pl.when(pl.program_id(0) == 0)
    def _():
        for h in range(HEADS):
            start = (h % 2) * (width // 2) + (h // 2) * head_width
            wo_sorted[start : start + head_width, :] = wo_ref[
                h * head_width : (h + 1) * head_width, :
            ]

    projected = jnp.dot(attended_ref[...], wo_sorted[...], preferred_element_type=f32)
    middle = (placed_ref[...].astype(f32) + projected).astype(bf16).astype(f32)
    second = layer_norm(middle).astype(bf16)
    mixed = middle + jnp.tanh(jnp.dot(second, wm_ref[...], preferred_element_type=f32))
    out_ref[...] = mixed.astype(bf16)


def body(features, assignment, pairs, w_query, w_key, w_value, w_out, w_mix):
    rows_dev, width = features.shape
    block_count, pair_count = pairs.shape
    cluster = rows_dev // block_count
    capacity = (block_count * pair_count + SPAN - 1) // SPAN + 1
    stride = lax.axis_size("elec") // SPAN
    position = lax.axis_index("elec") // stride
    group_rows = SPAN * cluster
    groups = rows_dev // group_rows
    bf16 = jnp.bfloat16

    column, need = own_needs(pairs, block_count, stride)
    need_rows = SPAN * block_count // LANES
    batch = math.gcd(groups, 2)
    tile = pl.BlockSpec((batch * group_rows, width), lambda i: (i, 0))
    full = (2 * capacity, 2 * capacity, block_count, block_count)
    small = (capacity + 17, capacity + 17, capacity + 27, capacity + 33)
    limits = tuple(min(a, b) for a, b in zip(small, full))
    teams = lax.axis_size("groups") * stride
    placed, normed, needs, over = pl.pallas_call(
        functools.partial(place_kernel, stride, limits),
        grid=(groups // batch,),
        in_specs=[
            pl.BlockSpec((batch, 1, group_rows), lambda i: (i, 0, 0)),
            pl.BlockSpec((need_rows, LANES), lambda i: (0, 0)),
            tile,
        ],
        out_specs=[
            tile,
            tile,
            pl.BlockSpec((SPAN, need_rows, LANES), lambda i: (0, 0, 0)),
            pl.BlockSpec(memory_space=pltpu.SMEM),
        ],
        out_shape=[jax.ShapeDtypeStruct((rows_dev, width), bf16)] * 2
        + [
            jax.ShapeDtypeStruct((SPAN, need_rows, LANES), jnp.int32),
            jax.ShapeDtypeStruct((1, 1), jnp.float32),
        ],
        scratch_shapes=[
            pltpu.VMEM((SPAN, need_rows, LANES), jnp.int32),
            pltpu.VMEM((teams, 8, LANES), jnp.float32),
            pltpu.SemaphoreType.DMA((SPAN,)),
            pltpu.SemaphoreType.DMA((SPAN,)),
            pltpu.SemaphoreType.DMA((teams,)),
            pltpu.SemaphoreType.DMA((teams,)),
        ],
        compiler_params=pltpu.CompilerParams(collective_id=1, has_side_effects=True),
    )(
        assignment.reshape(groups, 1, group_rows), need.reshape(need_rows, LANES), features
    )

    tables, reader, key, slot = make_plan(
        needs.reshape(SPAN, SPAN, block_count), column, position, capacity, pair_count
    )
    block = (cluster, width)
    part = (head_step(width), HEADS * cluster)
    in_smem = pl.BlockSpec(memory_space=pltpu.SMEM)
    in_vmem = pl.BlockSpec(memory_space=pltpu.VMEM)

    def layer(which, sizes):
        near_limit, end_limit, first_limit, union_limit = sizes
        steps = 4 + len({end_limit, first_limit, union_limit}) - 1
        buffers = [
            capacity, near_limit, capacity, union_limit, union_limit,
            max(union_limit - first_limit, 1), max(union_limit - first_limit, 1),
            capacity, capacity,
            capacity, near_limit, union_limit, 2 * capacity, block_count,
        ]
        return pl.pallas_call(
            functools.partial(layer_kernel, capacity, sizes, stride, pair_count),
            in_specs=[in_smem] * 4 + [in_vmem] * 4,
            out_specs=in_vmem,
            out_shape=jax.ShapeDtypeStruct((rows_dev, width), bf16),
            scratch_shapes=[pltpu.VMEM((count,) + block, bf16) for count in buffers]
            + [
                pltpu.VMEM((width, width), bf16),
                pltpu.VMEM((block_count + SPAN * capacity,) + part, jnp.float32),
                pltpu.SemaphoreType.DMA((4,)),
                pltpu.SemaphoreType.DMA((4,)),
                pltpu.SemaphoreType.DMA((steps,)),
                pltpu.SemaphoreType.DMA((2, 4)),
                pltpu.SemaphoreType.DMA((2, steps)),
                pltpu.SemaphoreType.DMA((2, 2)),
                pltpu.SemaphoreType.DMA((2, 2)),
            ],
            compiler_params=pltpu.CompilerParams(
                collective_id=which, has_side_effects=True, vmem_limit_bytes=60 * 2**20
            ),
        )

    attended = lax.cond(
        over[0, 0] <= 0.0, layer(0, limits), layer(2, full),
        tables, reader, key, slot, normed.reshape(block_count, cluster, width),
        w_query, w_key, w_value,
    )
    finish_rows = math.gcd(groups, 4) * group_rows
    tile = pl.BlockSpec((finish_rows, width), lambda i: (i, 0))
    weight = pl.BlockSpec((width, width), lambda i: (0, 0))
    return pl.pallas_call(
        finish_kernel,
        grid=(rows_dev // finish_rows,),
        in_specs=[tile, tile, weight, weight],
        out_specs=tile,
        out_shape=jax.ShapeDtypeStruct((rows_dev, width), bf16),
        scratch_shapes=[pltpu.VMEM((width, width), bf16)],
        compiler_params=pltpu.CompilerParams(vmem_limit_bytes=60 * 2**20),
    )(placed, attended, w_out, w_mix)


def solution(mesh):
    placed = (
        P(("groups", "elec"), None),
        P(("groups", "elec")),
        P(("groups", "elec"), None),
        P(),
        P(),
        P(),
        P(),
        P(),
    )
    return jax.shard_map(
        body, mesh=mesh, in_specs=placed, out_specs=P(("groups", "elec"), None), check_vma=False
    )
```

```python
import functools
import math

import jax
import jax.numpy as jnp
from jax import lax
from jax.experimental import pallas as pl
from jax.experimental.pallas import tpu as pltpu
from jax.sharding import PartitionSpec as P

HEADS = 16
SPAN = 8
LANES = 128
MESH = pl.DeviceIdType.MESH


def layer_norm(rows):
    mean = jnp.mean(rows, axis=-1, keepdims=True)
    centred = rows - mean
    variance = jnp.mean(centred * centred, axis=-1, keepdims=True)
    return centred * lax.rsqrt(variance + 1e-05)


def own_needs(listed, block_count, stride):
    flat = listed.reshape(-1)
    column = (flat // block_count // stride) * block_count + flat % block_count
    columns = jnp.arange(SPAN * block_count, dtype=jnp.int32)
    hit = column[None, :] == columns[:, None]
    return column, jnp.max(jnp.where(hit, 1, 0), axis=1).astype(jnp.int32)


def before(flags):
    size = flags.shape[-1]
    lower = (jnp.arange(size)[:, None] < jnp.arange(size)[None, :]).astype(jnp.bfloat16)
    counts = jnp.dot(
        flags.reshape(-1, size).astype(jnp.bfloat16), lower, preferred_element_type=jnp.float32
    )
    return counts.reshape(flags.shape).astype(jnp.int32)


def invert(place, flags, values, size):
    hit = (place[..., None, :] == jnp.arange(size, dtype=jnp.int32)[:, None]) & (
        flags[..., None, :] > 0
    )
    return jnp.sum(jnp.where(hit, values[..., None, :], 0), axis=-1).astype(jnp.int32)


def make_plan(needs, column, position, capacity, pair_count):
    blocks = needs.shape[-1]
    owners = jnp.arange(SPAN, dtype=jnp.int32)
    static = list(range(SPAN))

    def arrange(*readers):
        flags, left = [], jnp.ones((SPAN, blocks), jnp.int32)
        for chosen in readers:
            flags.append(jnp.stack([needs[chosen(o), o] for o in static]) * left)
            left = left - flags[-1]
        flags = jnp.stack(flags + [left])
        counts = jnp.sum(flags, axis=-1, keepdims=True)
        start = jnp.cumsum(counts, axis=0) - counts
        return jnp.sum(flags * (before(flags) + start), axis=0)

    def end(o):
        return 2 * (3 * (1 - o // 4)) + o % 2

    def middle(o):
        return 2 * (2 - o // 4) + o % 2

    order = arrange(
        lambda o: end(o) ^ 1, end, lambda o: middle(o) ^ 1, middle
    )
    near_order = arrange(lambda o: o ^ 3, lambda o: o ^ 2)
    rank = before(needs)
    within = jnp.arange(blocks, dtype=jnp.int32)

    def at(array, index):
        return lax.dynamic_index_in_dim(array, index, 0, keepdims=False)

    mine = lax.dynamic_index_in_dim(needs, position, 1, keepdims=False)
    mine_rank = lax.dynamic_index_in_dim(rank, position, 1, keepdims=False)
    all_flags = jnp.ones((blocks,), jnp.int32)
    lists = jnp.stack(
        [
            invert(at(mine_rank, position ^ 1), at(mine, position ^ 1), within, LANES),
            invert(at(near_order, position), all_flags, within, LANES),
            invert(at(order, position), all_flags, within, LANES),
        ]
    )

    z, y = position // 2, position % 2
    half = z // 2
    inner = (z + half) % 2
    partner_needs = at(needs, position ^ 1)
    partner_rank = at(rank, position ^ 1)
    sources = [2 * (2 - half) + y, 2 * (3 * (1 - half)) + y]
    filters = jnp.stack(
        [
            invert(at(partner_rank, s), at(partner_needs, s), at(order, s), LANES)
            for s in sources
        ]
    )
    tables = jnp.concatenate([lists, filters], axis=0)

    my_rank = at(rank, position)
    oz = owners // 2
    outer_owner = 1 - (oz + oz // 2) % 2
    same_half = owners // 4 == position // 4
    same_line = owners % 2 == y
    source_group = jnp.where(
        same_half, owners ^ position, jnp.where(same_line, 4 + outer_owner, 6 + outer_owner)
    )
    by_rank = (owners == (position ^ 1)) | (~same_half & ~same_line & (inner > 0))
    location = jnp.where(
        (owners == position)[:, None],
        within[None, :],
        jnp.where(
            by_rank[:, None], my_rank, jnp.where(same_half[:, None], near_order, order)
        ),
    )
    hit = column[:, None] == jnp.arange(SPAN * blocks, dtype=jnp.int32)[None, :]
    groups = jnp.broadcast_to(source_group[:, None], location.shape)
    packed = (groups * blocks + location).reshape(-1)
    packed = jnp.sum(jnp.where(hit, packed[None, :], 0), axis=1)
    entries = column.shape[0]
    group, key = packed // blocks, packed % blocks
    steps = jnp.arange(entries, dtype=jnp.int32)
    earlier = (group[:, None] == group[None, :]) & (steps[None, :] < steps[:, None])
    slots = group * capacity + jnp.sum(jnp.where(earlier, 1, 0), axis=1)
    slot_hit = slots[None, :] == jnp.arange(SPAN * capacity, dtype=jnp.int32)[:, None]
    jobs = jnp.sum(
        jnp.where(slot_hit, ((steps // pair_count) * blocks + key)[None, :], 0), axis=1
    )
    return (
        tables,
        (jobs // blocks).astype(jnp.int32),
        (jobs % blocks).astype(jnp.int32),
        (slots + blocks).astype(jnp.int32),
    )


def head_step(width):
    return -(-(width // HEADS + 2) // 8) * 8


def excess(readers, limits):
    rows = lax.broadcasted_iota(jnp.int32, readers[0].shape, 0)
    lanes = lax.broadcasted_iota(jnp.int32, readers[0].shape, 1)
    left = lanes < LANES // 2
    lower = rows < SPAN // 4
    large = jnp.maximum
    end = jnp.where(lower, large(readers[6], readers[7]), large(readers[0], readers[1]))
    middle = [jnp.where(lower, readers[4 + k], readers[2 + k]) for k in range(2)]
    first = large(end, jnp.where(left, middle[1], middle[0]))
    union = large(end, large(*middle))
    near = large(readers[4], readers[5])
    for row, k in ((0, 2), (1, 0), (2, 6)):
        near = jnp.where(rows == row, large(readers[k], readers[k + 1]), near)
    over = None
    for flags, limit in zip((near, end, first, union), limits):
        for part in (left, ~left):
            count = jnp.sum(jnp.where(part, flags, 0).astype(jnp.float32), axis=1, keepdims=True)
            worst = jnp.max(count, axis=0, keepdims=True) - float(limit)
            over = worst if over is None else jnp.maximum(over, worst)
    return over


def place_kernel(
    stride, limits, assignment_ref, need_ref, features_ref, placed_ref, normed_ref, needs_ref,
    over_ref, landing, flags, s_send, s_recv, g_send, g_recv,
):
    groups, _, size = assignment_ref.shape
    me = lax.axis_index("elec")
    group = lax.axis_index("groups")
    peers = lax.axis_size("elec")
    position = me // stride
    step_index = pl.program_id(0)
    teams = flags.shape[0]
    team = group * stride + lax.rem(me, stride)

    def toward(step):
        return (group, lax.rem(me + step * stride, peers))

    def across(step):
        other = lax.rem(team + step, teams)
        return (other // stride, position * stride + lax.rem(other, stride))

    def ask(step):
        return pltpu.make_async_remote_copy(
            src_ref=need_ref, dst_ref=landing.at[step],
            send_sem=s_send.at[step], recv_sem=s_recv.at[step],
            device_id=toward(step), device_id_type=MESH,
        )

    def tell(step):
        return pltpu.make_async_remote_copy(
            src_ref=flags.at[0], dst_ref=flags.at[step],
            send_sem=g_send.at[step], recv_sem=g_recv.at[step],
            device_id=across(step), device_id_type=MESH,
        )

    @pl.when(step_index == 0)
    def _():
        barrier = pltpu.get_barrier_semaphore()
        for step in range(1, SPAN):
            pl.semaphore_signal(barrier, inc=1, device_id=toward(step), device_id_type=MESH)
        for step in range(1, teams):
            pl.semaphore_signal(barrier, inc=1, device_id=across(step), device_id_type=MESH)
        pl.semaphore_wait(barrier, SPAN - 1 + teams - 1)
        for step in range(1, SPAN):
            ask(step).start()
        landing[0] = need_ref[...]

    @pl.when(step_index == pl.num_programs(0) - 1)
    def _():
        for step in range(1, SPAN):
            ask(step).wait()
        readers = [landing[lax.rem(position - q + SPAN, SPAN)] for q in range(SPAN)]
        for q in range(SPAN):
            needs_ref[q] = readers[q]
        flags[0] = jnp.broadcast_to(excess(readers, limits), flags.shape[1:])
        for step in range(1, teams):
            tell(step).start()

    lane = lax.broadcasted_iota(jnp.int32, (size, LANES), 1).astype(jnp.float32)
    for i in range(groups):
        rows = pl.ds(i * size, size)
        base = me * (features_ref.shape[0] * pl.num_programs(0)) + (
            (step_index * groups + i) * size
        )
        local = (assignment_ref[i] - base).astype(jnp.float32)
        takes = jnp.broadcast_to(local, (LANES, size)).T
        one_hot = jnp.concatenate(
            [jnp.where(takes == lane + k, 1.0, 0.0) for k in range(0, size, LANES)], axis=1
        ).astype(jnp.bfloat16)
        placed = jnp.dot(one_hot, features_ref[rows, :], preferred_element_type=jnp.float32)
        placed_ref[rows, :] = placed.astype(jnp.bfloat16)
        normed_ref[rows, :] = layer_norm(placed).astype(jnp.bfloat16)

    @pl.when(step_index == pl.num_programs(0) - 1)
    def _():
        for step in range(1, teams):
            tell(step).wait()
        worst = flags[0]
        for step in range(1, teams):
            worst = jnp.maximum(worst, flags[step])
        over_ref[0, 0] = jnp.max(worst)


def layer_kernel(
    capacity, limits, stride, pair_count,
    tables_ref, reader_ref, key_ref, slot_ref, blocks_ref, wq_ref, wk_ref, wv_ref,
    out_ref,
    near1, near2, near3, far0, far1, rest0, rest1, side0, side1, out_near, out_plane, out_far, out_side,
    queries, wv_turned, parts,
    n_send, n_recv, l_send, f_send, f_recv, p_send, p_recv,
):
    f32, bf16 = jnp.float32, jnp.bfloat16
    me = lax.axis_index("elec")
    group = lax.axis_index("groups")
    peers = lax.axis_size("elec")
    position = me // stride
    rest = lax.rem(me, stride)
    block_count, cluster, width = blocks_ref.shape
    head_width = width // HEADS
    cap = capacity
    z, y = position // 2, lax.rem(position, 2)
    half = z // 2
    inner = lax.rem(z + half, 2)
    pair_z = z + 1 - 2 * lax.rem(z, 2)
    pair_y = 1 - y

    def device(zz, yy):
        return (group, (2 * zz + yy) * stride + rest)

    near_devices = [device(z, pair_y), device(pair_z, y), device(pair_z, pair_y)]
    far_inner = device(2 - half, y)
    far, late, side = [far0, far1], [rest0, rest1], [side0, side1]
    near_limit, end_limit, first_limit, union_limit = limits
    part_one = (cap + 1) // 2
    part_two = cap + 2 * (end_limit - cap) // 3
    bounds = [0, part_one, cap, part_two, end_limit]
    relayed = len(bounds) - 1
    for bound in (first_limit, union_limit):
        if bound > bounds[-1]:
            bounds.append(bound)
    chunks = [(a, b - a) for a, b in zip(bounds, bounds[1:])]
    last = len(chunks) - 1
    refinable = bounds.index(first_limit)
    plane_chunks = [(0, cap), (cap, near_limit - cap)]

    barrier = pltpu.get_barrier_semaphore()
    for step in range(1, SPAN):
        pl.semaphore_signal(
            barrier, inc=1, device_id=(group, lax.rem(me + step * stride, peers)),
            device_id_type=MESH,
        )
    pl.semaphore_wait(barrier, SPAN - 1)

    def gather(row, first, count, source, target, base):
        def one(k, carry):
            target[base + first + k] = source[tables_ref[row, first + k]]
            return carry

        lax.fori_loop(0, count, one, 0)

    def far_copy(s, c):
        start, count = chunks[c]
        target = far[s].at[pl.ds(start, count)]
        if c >= refinable:
            target = late[s].at[pl.ds(start - first_limit, count)]
        return pltpu.make_async_remote_copy(
            src_ref=out_far.at[pl.ds(start, count)], dst_ref=target,
            send_sem=l_send.at[c], recv_sem=f_recv.at[s, c],
            device_id=far_inner, device_id_type=MESH,
        )

    def forward_copy(s, c):
        start, count = chunks[c]
        return pltpu.make_async_remote_copy(
            src_ref=far[s].at[pl.ds(start, count)], dst_ref=far[s].at[pl.ds(start, count)],
            send_sem=f_send.at[s, c], recv_sem=f_recv.at[s, c],
            device_id=near_devices[1], device_id_type=MESH,
        )

    def side_copy(s, k, source, base):
        start, count = chunks[k]
        return pltpu.make_async_remote_copy(
            src_ref=source.at[pl.ds(base + start, count)], dst_ref=side[s].at[pl.ds(start, count)],
            send_sem=p_send.at[s, k], recv_sem=p_recv.at[s, k],
            device_id=near_devices[0], device_id_type=MESH,
        )

    def filtered(s, k):
        return side_copy(s, k, out_side, s * cap)

    def passed_on(s, k):
        return side_copy(s, k, far[s], 0)

    def near_copy():
        return pltpu.make_async_remote_copy(
            src_ref=out_near, dst_ref=near1, send_sem=n_send.at[0], recv_sem=n_recv.at[0],
            device_id=near_devices[0], device_id_type=MESH,
        )

    def plane_copy(c):
        start, count = plane_chunks[c]
        return pltpu.make_async_remote_copy(
            src_ref=out_plane.at[pl.ds(start, count)], dst_ref=near2.at[pl.ds(start, count)],
            send_sem=n_send.at[1 + c], recv_sem=n_recv.at[1 + c],
            device_id=near_devices[1], device_id_type=MESH,
        )

    def plane_pass():
        return pltpu.make_async_remote_copy(
            src_ref=near2.at[pl.ds(0, cap)], dst_ref=near3,
            send_sem=n_send.at[3], recv_sem=n_recv.at[3],
            device_id=near_devices[0], device_id_type=MESH,
        )

    def send_far(s, c):
        gather(2, chunks[c][0], chunks[c][1], blocks_ref, out_far, 0)
        far_copy(s, c).start()

    @pl.when(inner == 1)
    def _():
        for c in range(last + 1):
            send_far(0, c)

    @pl.when(inner == 0)
    def _():
        for c in range(refinable):
            send_far(1, c)

    gather(0, 0, cap, blocks_ref, out_near, 0)
    near_copy().start()
    for c in range(2):
        gather(1, plane_chunks[c][0], plane_chunks[c][1], blocks_ref, out_plane, 0)
        plane_copy(c).start()

    lane = lax.broadcasted_iota(jnp.int32, (cluster, LANES), 1)
    per = LANES // 2 // head_width
    chosen = [
        jnp.where(lane // head_width == c, 1.0, 0.0).astype(bf16) for c in range(2 * per)
    ]
    low = lax.broadcasted_iota(jnp.int32, (head_width, LANES), 1) < cluster
    scale = math.log2(math.e) / head_width**0.5
    turned = (((1,), (1,)), ((), ()))

    def unit(size):
        row = lax.broadcasted_iota(jnp.int32, (size, size), 0)
        column = lax.broadcasted_iota(jnp.int32, (size, size), 1)
        return jnp.where(row == column, 1.0, 0.0).astype(bf16)

    wv_turned[...] = lax.dot_general(
        unit(width), wv_ref[...], turned, preferred_element_type=f32
    ).astype(bf16)

    def project(i, carry):
        rows = blocks_ref[pl.ds(i * SPAN, SPAN)].reshape(SPAN * cluster, width)
        result = jnp.dot(rows, wq_ref[...], preferred_element_type=f32) * scale
        queries[pl.ds(i * SPAN, SPAN)] = result.astype(bf16).reshape(SPAN, cluster, width)
        return carry

    lax.fori_loop(0, block_count // SPAN, project, 0)

    def several(places, query_blocks, key_blocks):
        count = len(places)
        keys = jnp.dot(
            jnp.concatenate(key_blocks, axis=0), wk_ref[...], preferred_element_type=f32
        ).astype(bf16)
        values = [
            lax.dot_general(wv_turned[...], rows, turned, preferred_element_type=f32).astype(bf16)
            for rows in key_blocks
        ]
        scores = []
        for i in range(count):
            for g in range(HEADS // per):
                band = (g // 2) * LANES
                query = query_blocks[i][:, band : band + LANES]
                stacked = jnp.concatenate(
                    [query * chosen[(g % 2) * per + c] for c in range(per)], axis=0
                )
                scores.append(
                    lax.dot_general(
                        keys[i * cluster : (i + 1) * cluster, band : band + LANES],
                        stacked, turned, preferred_element_type=f32,
                    )
                )
        weights = []
        for i in range(count):
            for g in range(HEADS // per):
                score = scores[i * (HEADS // per) + g]
                columns = pl.ds(g * per * cluster, per * cluster)
                top = jnp.max(score, axis=0, keepdims=True)
                weight = jnp.exp2(score - top)
                parts[places[i], head_width : head_width + 1, columns] = top
                parts[places[i], head_width + 1 : head_width + 2, columns] = jnp.sum(
                    weight, axis=0, keepdims=True
                )
                weights.append(weight.astype(bf16))
        for i in range(count):
            for g in range(HEADS // per):
                rows = per * head_width
                result = jnp.dot(
                    values[i][g * rows : (g + 1) * rows], weights[i * (HEADS // per) + g],
                    preferred_element_type=f32,
                )
                for k in range(per // 2):
                    top = 2 * k * head_width
                    lanes = slice(k * LANES, (k + 1) * LANES)
                    first = (g * per // 2 + k) * LANES
                    parts[places[i], 0:head_width, pl.ds(first, LANES)] = jnp.where(
                        low,
                        result[top : top + head_width, lanes],
                        result[top + head_width : top + 2 * head_width, lanes],
                    )

    def own_blocks(first, count, batch):
        def one(i, carry):
            index = [first + i * batch + k for k in range(batch)]
            several(index, [queries[j] for j in index], [blocks_ref[j] for j in index])
            return carry

        lax.fori_loop(0, count // batch, one, 0)

    def listed(which, source):
        batch = 5 if cap % 5 == 0 else 1

        def one(i, carry):
            index = [which * cap + i * batch + k for k in range(batch)]
            several(
                [block_count + j for j in index],
                [queries[reader_ref[j]] for j in index],
                [source[key_ref[j]] for j in index],
            )
            return carry

        lax.fori_loop(0, cap // batch, one, 0)

    def on_inner(work):
        pl.when(inner == 1)(work)

    def on_outer(work):
        pl.when(inner == 0)(work)

    def relay(s, c):
        far_copy(s, c).wait_recv()
        forward_copy(s, c).start()

    def refine(s):
        arrived(s, relayed, refinable)
        gather(3 + s, 0, cap, far[s], out_side, s * cap)
        for k in range(2):
            filtered(s, k).start()

    def pass_on(s, k):
        far_copy(s, k).wait_recv()
        passed_on(s, k).start()

    def arrived(s, first, stop):
        for c in range(first, stop):
            far_copy(s, c).wait_recv()

    def late_arrived(s):
        arrived(s, refinable, last + 1)
        for k in range(union_limit - first_limit):
            far[s][first_limit + k] = late[s][k]

    def side_arrived(s):
        for k in range(2):
            filtered(s, k).wait_recv()

    eighth = block_count // 8
    own_blocks(0, 3 * eighth, 4)
    on_inner(lambda: relay(1, 0))
    own_blocks(3 * eighth, 3 * eighth, 4)
    on_inner(lambda: relay(1, 1))
    own_blocks(6 * eighth, 2 * eighth, 4)
    on_inner(lambda: relay(1, 2))
    listed(0, blocks_ref)
    on_inner(lambda: relay(1, 3))
    near_copy().wait_recv()
    listed(1, near1)

    @pl.when(inner == 1)
    def _():
        refine(1)
        relay(0, 0)
        plane_copy(0).wait_recv()
        plane_pass().start()
        relay(0, 1)
        side_arrived(1)
        listed(7, side1)
        relay(0, 2)
        plane_copy(1).wait_recv()
        relay(0, 3)
        listed(2, near2)
        refine(0)
        plane_pass().wait_recv()
        listed(3, near3)
        late_arrived(0)
        listed(4, far0)
        late_arrived(1)
        listed(5, far1)
        side_arrived(0)
        listed(6, side0)

    @pl.when(inner == 0)
    def _():
        plane_copy(0).wait_recv()
        plane_pass().start()
        pass_on(1, 0)
        pass_on(1, 1)
        plane_copy(1).wait_recv()
        listed(2, near2)
        plane_pass().wait_recv()
        listed(3, near3)
        arrived(1, 2, relayed)
        listed(5, far1)
        side_arrived(1)
        listed(7, side1)
        pass_on(0, 0)
        for c in range(refinable, last + 1):
            send_far(1, c)
        pass_on(0, 1)
        side_arrived(0)
        listed(6, side0)
        arrived(0, 2, relayed)
        listed(4, far0)

    def combine(i, carry):
        for k in range(SPAN):
            j = i * SPAN + k
            places = [j] + [slot_ref[j * pair_count + p] for p in range(pair_count)]
            tops = [parts[a, head_width : head_width + 1, :] for a in places]
            sums = [parts[a, head_width + 1 : head_width + 2, :] for a in places]
            top = functools.reduce(jnp.maximum, tops)
            factors = [jnp.exp2(t - top) for t in tops]
            total = sum(f * s for f, s in zip(factors, sums))
            inverse = 1.0 / total
            merged = sum(
                parts[a, 0:head_width, :] * (f * inverse) for a, f in zip(places, factors)
            ).astype(bf16)
            stacked = jnp.concatenate(
                [merged[:, c : c + LANES] for c in range(0, HEADS * cluster, LANES)], axis=0
            )
            upright = lax.dot_general(
                unit(LANES), stacked, turned, preferred_element_type=f32
            ).astype(bf16)
            rows = pl.ds(pl.multiple_of(j * cluster, cluster), cluster)
            out_ref[rows, 0:LANES] = upright[0:cluster]
            out_ref[rows, LANES : 2 * LANES] = upright[cluster : 2 * cluster]
        return carry

    lax.fori_loop(0, block_count // SPAN, combine, 0)

    @pl.when(inner == 1)
    def _():
        for s in range(2):
            for c in range(relayed):
                forward_copy(s, c).wait_send()
            for k in range(2):
                filtered(s, k).wait_send()

    @pl.when(inner == 0)
    def _():
        for s in range(2):
            for k in range(2):
                passed_on(s, k).wait_send()

    for c in range(last + 1):
        far_copy(0, c).wait_send()
    near_copy().wait_send()
    for c in range(2):
        plane_copy(c).wait_send()
    plane_pass().wait_send()


def finish_kernel(placed_ref, attended_ref, wo_ref, wm_ref, out_ref, wo_sorted):
    f32, bf16 = jnp.float32, jnp.bfloat16
    width = wo_ref.shape[0]
    head_width = width // HEADS

    @pl.when(pl.program_id(0) == 0)
    def _():
        for h in range(HEADS):
            start = (h % 2) * (width // 2) + (h // 2) * head_width
            wo_sorted[start : start + head_width, :] = wo_ref[
                h * head_width : (h + 1) * head_width, :
            ]

    projected = jnp.dot(attended_ref[...], wo_sorted[...], preferred_element_type=f32)
    middle = (placed_ref[...].astype(f32) + projected).astype(bf16).astype(f32)
    second = layer_norm(middle).astype(bf16)
    mixed = middle + jnp.tanh(jnp.dot(second, wm_ref[...], preferred_element_type=f32))
    out_ref[...] = mixed.astype(bf16)


def body(features, assignment, pairs, w_query, w_key, w_value, w_out, w_mix):
    rows_dev, width = features.shape
    block_count, pair_count = pairs.shape
    cluster = rows_dev // block_count
    capacity = (block_count * pair_count + SPAN - 1) // SPAN + 1
    stride = lax.axis_size("elec") // SPAN
    position = lax.axis_index("elec") // stride
    group_rows = SPAN * cluster
    groups = rows_dev // group_rows
    bf16 = jnp.bfloat16

    column, need = own_needs(pairs, block_count, stride)
    need_rows = SPAN * block_count // LANES
    batch = math.gcd(groups, 2)
    tile = pl.BlockSpec((batch * group_rows, width), lambda i: (i, 0))
    full = (2 * capacity, 2 * capacity, block_count, block_count)
    small = (capacity + 17, capacity + 17, capacity + 27, capacity + 33)
    limits = tuple(min(a, b) for a, b in zip(small, full))
    teams = lax.axis_size("groups") * stride
    placed, normed, needs, over = pl.pallas_call(
        functools.partial(place_kernel, stride, limits),
        grid=(groups // batch,),
        in_specs=[
            pl.BlockSpec((batch, 1, group_rows), lambda i: (i, 0, 0)),
            pl.BlockSpec((need_rows, LANES), lambda i: (0, 0)),
            tile,
        ],
        out_specs=[
            tile,
            tile,
            pl.BlockSpec((SPAN, need_rows, LANES), lambda i: (0, 0, 0)),
            pl.BlockSpec(memory_space=pltpu.SMEM),
        ],
        out_shape=[jax.ShapeDtypeStruct((rows_dev, width), bf16)] * 2
        + [
            jax.ShapeDtypeStruct((SPAN, need_rows, LANES), jnp.int32),
            jax.ShapeDtypeStruct((1, 1), jnp.float32),
        ],
        scratch_shapes=[
            pltpu.VMEM((SPAN, need_rows, LANES), jnp.int32),
            pltpu.VMEM((teams, 8, LANES), jnp.float32),
            pltpu.SemaphoreType.DMA((SPAN,)),
            pltpu.SemaphoreType.DMA((SPAN,)),
            pltpu.SemaphoreType.DMA((teams,)),
            pltpu.SemaphoreType.DMA((teams,)),
        ],
        compiler_params=pltpu.CompilerParams(collective_id=1, has_side_effects=True),
    )(
        assignment.reshape(groups, 1, group_rows), need.reshape(need_rows, LANES), features
    )

    tables, reader, key, slot = make_plan(
        needs.reshape(SPAN, SPAN, block_count), column, position, capacity, pair_count
    )
    block = (cluster, width)
    part = (head_step(width), HEADS * cluster)
    in_smem = pl.BlockSpec(memory_space=pltpu.SMEM)
    in_vmem = pl.BlockSpec(memory_space=pltpu.VMEM)

    def layer(which, sizes):
        near_limit, end_limit, first_limit, union_limit = sizes
        steps = 4 + len({end_limit, first_limit, union_limit}) - 1
        buffers = [
            capacity, near_limit, capacity, union_limit, union_limit,
            max(union_limit - first_limit, 1), max(union_limit - first_limit, 1),
            capacity, capacity,
            capacity, near_limit, union_limit, 2 * capacity, block_count,
        ]
        return pl.pallas_call(
            functools.partial(layer_kernel, capacity, sizes, stride, pair_count),
            in_specs=[in_smem] * 4 + [in_vmem] * 4,
            out_specs=in_vmem,
            out_shape=jax.ShapeDtypeStruct((rows_dev, width), bf16),
            scratch_shapes=[pltpu.VMEM((count,) + block, bf16) for count in buffers]
            + [
                pltpu.VMEM((width, width), bf16),
                pltpu.VMEM((block_count + SPAN * capacity,) + part, jnp.float32),
                pltpu.SemaphoreType.DMA((4,)),
                pltpu.SemaphoreType.DMA((4,)),
                pltpu.SemaphoreType.DMA((steps,)),
                pltpu.SemaphoreType.DMA((2, 4)),
                pltpu.SemaphoreType.DMA((2, steps)),
                pltpu.SemaphoreType.DMA((2, 2)),
                pltpu.SemaphoreType.DMA((2, 2)),
            ],
            compiler_params=pltpu.CompilerParams(
                collective_id=which, has_side_effects=True, vmem_limit_bytes=60 * 2**20
            ),
        )

    attended = lax.cond(
        over[0, 0] <= 0.0, layer(0, limits), layer(2, full),
        tables, reader, key, slot, normed.reshape(block_count, cluster, width),
        w_query, w_key, w_value,
    )
    finish_rows = math.gcd(groups, 4) * group_rows
    tile = pl.BlockSpec((finish_rows, width), lambda i: (i, 0))
    weight = pl.BlockSpec((width, width), lambda i: (0, 0))
    return pl.pallas_call(
        finish_kernel,
        grid=(rows_dev // finish_rows,),
        in_specs=[tile, tile, weight, weight],
        out_specs=tile,
        out_shape=jax.ShapeDtypeStruct((rows_dev, width), bf16),
        scratch_shapes=[pltpu.VMEM((width, width), bf16)],
        compiler_params=pltpu.CompilerParams(vmem_limit_bytes=60 * 2**20),
    )(placed, attended, w_out, w_mix)


def solution(mesh):
    placed = (
        P(("groups", "elec"), None),
        P(("groups", "elec")),
        P(("groups", "elec"), None),
        P(),
        P(),
        P(),
        P(),
        P(),
    )
    return jax.shard_map(
        body, mesh=mesh, in_specs=placed, out_specs=P(("groups", "elec"), None), check_vma=False
    )
```
